32 devices in a mesh: fsdp: 2 (over x), ctx: 4 (over y, core), tp: 4 (over z).
Axes of the slice: x: 2, y: 2, z: 4, core: 2. Of those that a mesh axis runs over, the one named last changes fastest.
Arguments:
- latents: float32 [4, 256, 16], P('fsdp', 'ctx'), may hold values from -6 to 6
- noise: float32 [4, 256, 16], P('fsdp', 'ctx'), may hold values from -6 to 6
- var_target: float32 [4, 256, 16], P('fsdp', 'ctx'), may hold values from -6 to 6
- timesteps: int32 [4], P('fsdp'), may hold values from 0 to 999
- labels: int32 [4], P('fsdp'), may hold values from 0 to 1000
- attend_weight: float32 [4, 1024, 3, 1024], P(None, 'fsdp', None, 'tp'), may hold values from -0.1875 to 0.1875
- attend_mean: float32 [4, 1024, 3, 1024], P(None, 'fsdp', None, 'tp'), may hold values from -0.00044727084 to 0.00044727084
- attend_square: float32 [4, 1024, 3, 1024], P(None, 'fsdp', None, 'tp'), may hold values from 1.2503201e-08 to 5.0012805e-08
- hidden_weight: float32 [4, 1024, 4, 1024], P(None, 'fsdp', None, 'tp'), may hold values from -0.1875 to 0.1875
- hidden_mean: float32 [4, 1024, 4, 1024], P(None, 'fsdp', None, 'tp'), may hold values from -0.00044727084 to 0.00044727084
- hidden_square: float32 [4, 1024, 4, 1024], P(None, 'fsdp', None, 'tp'), may hold values from 1.2503201e-08 to 5.0012805e-08
- output_weight: float32 [4, 1024, 5, 1024], P(None, 'fsdp', None, 'tp'), may hold values from -0.1875 to 0.1875
- output_mean: float32 [4, 1024, 5, 1024], P(None, 'fsdp', None, 'tp'), may hold values from -0.00044727084 to 0.00044727084
- output_square: float32 [4, 1024, 5, 1024], P(None, 'fsdp', None, 'tp'), may hold values from 1.2503201e-08 to 5.0012805e-08
- patch_weight: float32 [1024, 16], P('fsdp'), may hold values from -1.5 to 1.5
- patch_mean: float32 [1024, 16], P('fsdp'), may hold values from -0.00044727084 to 0.00044727084
- patch_square: float32 [1024, 16], P('fsdp'), may hold values from 1.2503201e-08 to 5.0012805e-08
- freq_weight: float32 [1024, 256], P('fsdp'), may hold values from -0.375 to 0.375
- freq_mean: float32 [1024, 256], P('fsdp'), may hold values from -0.00044727084 to 0.00044727084
- freq_square: float32 [1024, 256], P('fsdp'), may hold values from 1.2503201e-08 to 5.0012805e-08
- time_weight: float32 [1024, 1024], P('fsdp'), may hold values from -0.1875 to 0.1875
- time_mean: float32 [1024, 1024], P('fsdp'), may hold values from -0.00044727084 to 0.00044727084
- time_square: float32 [1024, 1024], P('fsdp'), may hold values from 1.2503201e-08 to 5.0012805e-08
- label_table: float32 [1024, 1001], P('fsdp'), may hold values from -1.5 to 1.5
- label_mean: float32 [1024, 1001], P('fsdp'), may hold values from -0.00044727084 to 0.00044727084
- label_square: float32 [1024, 1001], P('fsdp'), may hold values from 1.2503201e-08 to 5.0012805e-08
- cond_weight: float32 [1024, 26624], P('fsdp', 'tp'), may hold values from -0.1875 to 0.1875
- cond_mean: float32 [1024, 26624], P('fsdp', 'tp'), may hold values from -0.00044727084 to 0.00044727084
- cond_square: float32 [1024, 26624], P('fsdp', 'tp'), may hold values from 1.2503201e-08 to 5.0012805e-08
- head_weight: float32 [1024, 32], P('fsdp'), may hold values from -0.1875 to 0.1875
- head_mean: float32 [1024, 32], P('fsdp'), may hold values from -0.00044727084 to 0.00044727084
- head_square: float32 [1024, 32], P('fsdp'), may hold values from 1.2503201e-08 to 5.0012805e-08
Outputs:
- loss: float32 [], replicated
- grad_norm: float32 [], replicated
- attend_next: float32 [4, 1024, 3, 1024], P(None, 'fsdp', None, 'tp')
- attend_mean_next: float32 [4, 1024, 3, 1024], P(None, 'fsdp', None, 'tp')
- attend_square_next: float32 [4, 1024, 3, 1024], P(None, 'fsdp', None, 'tp')
- hidden_next: float32 [4, 1024, 4, 1024], P(None, 'fsdp', None, 'tp')
- hidden_mean_next: float32 [4, 1024, 4, 1024], P(None, 'fsdp', None, 'tp')
- hidden_square_next: float32 [4, 1024, 4, 1024], P(None, 'fsdp', None, 'tp')
- output_next: float32 [4, 1024, 5, 1024], P(None, 'fsdp', None, 'tp')
- output_mean_next: float32 [4, 1024, 5, 1024], P(None, 'fsdp', None, 'tp')
- output_square_next: float32 [4, 1024, 5, 1024], P(None, 'fsdp', None, 'tp')
- patch_next: float32 [1024, 16], P('fsdp')
- patch_mean_next: float32 [1024, 16], P('fsdp')
- patch_square_next: float32 [1024, 16], P('fsdp')
- freq_next: float32 [1024, 256], P('fsdp')
- freq_mean_next: float32 [1024, 256], P('fsdp')
- freq_square_next: float32 [1024, 256], P('fsdp')
- time_next: float32 [1024, 1024], P('fsdp')
- time_mean_next: float32 [1024, 1024], P('fsdp')
- time_square_next: float32 [1024, 1024], P('fsdp')
- label_next: float32 [1024, 1001], P('fsdp')
- label_mean_next: float32 [1024, 1001], P('fsdp')
- label_square_next: float32 [1024, 1001], P('fsdp')
- cond_next: float32 [1024, 26624], P('fsdp', 'tp')
- cond_mean_next: float32 [1024, 26624], P('fsdp', 'tp')
- cond_square_next: float32 [1024, 26624], P('fsdp', 'tp')
- head_next: float32 [1024, 32], P('fsdp')
- head_mean_next: float32 [1024, 32], P('fsdp')
- head_square_next: float32 [1024, 32], P('fsdp')
The draws below stay inside these ranges and needn't reach their ends.
All inputs are finite; a program needn't handle non-finite values.
Results may differ from the reference program's by a relative error of at most 0.0065.
The reference program's roundings to bfloat16 on the way count: a program that leaves them out, or rounds other values in their place, can miss the bound.
Values may be sent and summed in bfloat16 or wider, within the bound.
A program may use at most 576 MiB of HBM per device.

```python
import math
import jax
import jax.numpy as jnp
from jax import lax

D = 1024
HEADS = 16
HEAD_DIM = 64
FF = 4096
CLASSES = 1001
FREQ = 256
PATCH_IN = 16
PATCH_OUT = 32
LAYERS = 4
GRID = 16
STEP = 5
IMG_DEV = 2
SEQ = 256
MODS = 26
IMAGES = 4
PARAMS = 79979520


def plant(array, own_key, least, top_value):
    index_at = [jax.random.randint(jax.random.fold_in(own_key, axis), (), 0, length) for axis, length in enumerate(array.shape)]
    main_axis = array.shape.index(max(array.shape))
    next_to = index_at[:main_axis] + [(index_at[main_axis] + 1) % array.shape[main_axis]] + index_at[main_axis + 1:]
    return array.at[tuple(index_at)].set(least).at[tuple(next_to)].set(top_value)


def block_levels(stream_key, shape, cuts, low, largest):
    loudness, own = 1.0, jax.random.fold_in(stream_key, 6)
    for axis_at, blocks in cuts:
        steps = jnp.exp(jax.random.uniform(jax.random.fold_in(own, axis_at), (blocks,), jnp.float32, low / len(cuts), largest / len(cuts)))
        loudness = loudness * jnp.repeat(steps, shape[axis_at] // blocks).reshape([-1 if axis == axis_at else 1 for axis in range(len(shape))])
    return loudness


def bell_draw(own_key, dims, scale, bound, split=(), kind=jnp.bfloat16):
    level = block_levels(own_key, dims, split, -0.22, 0.18) if split else 1.0
    entries = jax.random.normal(own_key, dims, jnp.float32) * scale * level
    return jnp.minimum(jnp.maximum(entries, -bound), bound).astype(kind)


def setup_inputs(seed: int = 0) -> dict:
    splits = jax.random.split(jax.random.key(seed), 33)
    return {
        "latents": bell_draw(splits[0], (IMAGES, SEQ, PATCH_IN), 1.0, 6.0, ((0, 2), (1, 4)), jnp.float32),
        "noise": bell_draw(splits[1], (IMAGES, SEQ, PATCH_IN), 1.0, 6.0, ((0, 2), (1, 4)), jnp.float32),
        "var_target": bell_draw(splits[2], (IMAGES, SEQ, PATCH_IN), 1.0, 6.0, ((0, 2), (1, 4)), jnp.float32),
        "timesteps": plant(jax.random.randint(splits[3], (IMAGES,), 0, 1000), jax.random.fold_in(splits[3], 1), 0, 999).astype(jnp.int32),
        "labels": plant(jax.random.randint(splits[4], (IMAGES,), 0, CLASSES), jax.random.fold_in(splits[4], 1), 0, CLASSES - 1).astype(jnp.int32),
        "attend_weight": bell_draw(splits[5], (LAYERS, D, 3, D), D ** -0.5, 0.1875, ((1, 2), (3, 4)), jnp.float32),
        "attend_mean": bell_draw(splits[6], (LAYERS, D, 3, D), (PARAMS ** -0.5), 0.00044727084, ((1, 2), (3, 4)), jnp.float32),
        "attend_square": jnp.clip(jnp.exp(math.log(5.001280456440327e-08) - 1.3862944 * jax.random.uniform(splits[7], (LAYERS, D, 3, D), jnp.float32) ** block_levels(splits[7], (LAYERS, D, 3, D), ((1, 2), (3, 4)), -0.2, 0.2)), 1.2503201141100817e-08, 5.001280456440327e-08),
        "hidden_weight": bell_draw(splits[8], (LAYERS, D, 4, D), D ** -0.5, 0.1875, ((1, 2), (3, 4)), jnp.float32),
        "hidden_mean": bell_draw(splits[9], (LAYERS, D, 4, D), (PARAMS ** -0.5), 0.00044727084, ((1, 2), (3, 4)), jnp.float32),
        "hidden_square": jnp.clip(jnp.exp(math.log(5.001280456440327e-08) - 1.3862944 * jax.random.uniform(splits[10], (LAYERS, D, 4, D), jnp.float32) ** block_levels(splits[10], (LAYERS, D, 4, D), ((1, 2), (3, 4)), -0.2, 0.2)), 1.2503201141100817e-08, 5.001280456440327e-08),
        "output_weight": bell_draw(splits[11], (LAYERS, D, 5, D), D ** -0.5, 0.1875, ((1, 2), (3, 4)), jnp.float32),
        "output_mean": bell_draw(splits[12], (LAYERS, D, 5, D), (PARAMS ** -0.5), 0.00044727084, ((1, 2), (3, 4)), jnp.float32),
        "output_square": jnp.clip(jnp.exp(math.log(5.001280456440327e-08) - 1.3862944 * jax.random.uniform(splits[13], (LAYERS, D, 5, D), jnp.float32) ** block_levels(splits[13], (LAYERS, D, 5, D), ((1, 2), (3, 4)), -0.2, 0.2)), 1.2503201141100817e-08, 5.001280456440327e-08),
        "patch_weight": bell_draw(splits[14], (D, PATCH_IN), PATCH_IN ** -0.5, 1.5, ((0, 2),), jnp.float32),
        "patch_mean": bell_draw(splits[15], (D, PATCH_IN), (PARAMS ** -0.5), 0.00044727084, ((0, 2),), jnp.float32),
        "patch_square": jnp.clip(jnp.exp(math.log(5.001280456440327e-08) - 1.3862944 * jax.random.uniform(splits[16], (D, PATCH_IN), jnp.float32) ** block_levels(splits[16], (D, PATCH_IN), ((0, 2),), -0.2, 0.2)), 1.2503201141100817e-08, 5.001280456440327e-08),
        "freq_weight": bell_draw(splits[17], (D, FREQ), FREQ ** -0.5, 0.375, ((0, 2),), jnp.float32),
        "freq_mean": bell_draw(splits[18], (D, FREQ), (PARAMS ** -0.5), 0.00044727084, ((0, 2),), jnp.float32),
        "freq_square": jnp.clip(jnp.exp(math.log(5.001280456440327e-08) - 1.3862944 * jax.random.uniform(splits[19], (D, FREQ), jnp.float32) ** block_levels(splits[19], (D, FREQ), ((0, 2),), -0.2, 0.2)), 1.2503201141100817e-08, 5.001280456440327e-08),
        "time_weight": bell_draw(splits[20], (D, D), D ** -0.5, 0.1875, ((0, 2),), jnp.float32),
        "time_mean": bell_draw(splits[21], (D, D), (PARAMS ** -0.5), 0.00044727084, ((0, 2),), jnp.float32),
        "time_square": jnp.clip(jnp.exp(math.log(5.001280456440327e-08) - 1.3862944 * jax.random.uniform(splits[22], (D, D), jnp.float32) ** block_levels(splits[22], (D, D), ((0, 2),), -0.2, 0.2)), 1.2503201141100817e-08, 5.001280456440327e-08),
        "label_table": bell_draw(splits[23], (D, CLASSES), 0.25, 1.5, ((0, 2),), jnp.float32),
        "label_mean": bell_draw(splits[24], (D, CLASSES), (PARAMS ** -0.5), 0.00044727084, ((0, 2),), jnp.float32),
        "label_square": jnp.clip(jnp.exp(math.log(5.001280456440327e-08) - 1.3862944 * jax.random.uniform(splits[25], (D, CLASSES), jnp.float32) ** block_levels(splits[25], (D, CLASSES), ((0, 2),), -0.2, 0.2)), 1.2503201141100817e-08, 5.001280456440327e-08),
        "cond_weight": bell_draw(splits[26], (D, MODS * D), D ** -0.5, 0.1875, ((0, 2), (1, 4)), jnp.float32),
        "cond_mean": bell_draw(splits[27], (D, MODS * D), (PARAMS ** -0.5), 0.00044727084, ((0, 2), (1, 4)), jnp.float32),
        "cond_square": jnp.clip(jnp.exp(math.log(5.001280456440327e-08) - 1.3862944 * jax.random.uniform(splits[28], (D, MODS * D), jnp.float32) ** block_levels(splits[28], (D, MODS * D), ((0, 2), (1, 4)), -0.2, 0.2)), 1.2503201141100817e-08, 5.001280456440327e-08),
        "head_weight": bell_draw(splits[29], (D, PATCH_OUT), D ** -0.5, 0.1875, ((0, 2),), jnp.float32),
        "head_mean": bell_draw(splits[30], (D, PATCH_OUT), (PARAMS ** -0.5), 0.00044727084, ((0, 2),), jnp.float32),
        "head_square": jnp.clip(jnp.exp(math.log(5.001280456440327e-08) - 1.3862944 * jax.random.uniform(splits[31], (D, PATCH_OUT), jnp.float32) ** block_levels(splits[31], (D, PATCH_OUT), ((0, 2),), -0.2, 0.2)), 1.2503201141100817e-08, 5.001280456440327e-08),
    }


@jax.custom_vjp
def low(v):
    return lax.optimization_barrier(v.astype(jnp.bfloat16)).astype(jnp.float32)

@jax.custom_vjp
def low_back(v):
    return v

def low_keep(v):
    return (low(v), None)

def low_pass(kept, grad):
    return (grad,)

def back_keep(v):
    return (v, None)

def back_low(kept, grad):
    return (low(grad),)
low.defvjp(low_keep, low_pass)
low_back.defvjp(back_keep, back_low)
HIGH = lax.Precision.HIGHEST
RATE = 0.05
DECAY = 0.1
BETA = 0.5
EPSILON = 1e-08
CLIP = 1.0

def modln(h, shift, scale):
    mean = lax.optimization_barrier(jnp.mean(h, -1, keepdims=True))
    cent = h - mean
    var = lax.optimization_barrier(jnp.mean(cent * cent, -1, keepdims=True))
    return cent * lax.rsqrt(var + 1e-06) * (1.0 + scale) + shift

def gelu_tanh(v):
    return jax.nn.gelu(v, approximate=True)

def noise_level(steps):
    phase = (steps.astype(jnp.float32) / 1000.0 + 0.008) / 1.008 * (0.5 * math.pi)
    return jnp.cos(phase) ** 2

def time_freqs(steps):
    half = FREQ // 2
    rates = jnp.exp(-math.log(10000.0) * jnp.arange(half, dtype=jnp.float32) / half)
    angles = steps.astype(jnp.float32)[:, None] * rates[None, :]
    return jnp.concatenate([jnp.cos(angles), jnp.sin(angles)], -1)

def positions(first, count, width):
    index = first + jnp.arange(count, dtype=jnp.int32)
    row = (index // GRID).astype(jnp.float32)
    column = (index % GRID).astype(jnp.float32)
    quarter = width // 4
    rates = jnp.power(10000.0, -jnp.arange(quarter, dtype=jnp.float32) / quarter)
    across = column[:, None] * rates[None, :]
    down = row[:, None] * rates[None, :]
    return jnp.concatenate([jnp.sin(across), jnp.cos(across), jnp.sin(down), jnp.cos(down)], -1)

def block(h, mods, attend, hidden, output):
    count = h.shape[0]
    scale = 1.0 / math.sqrt(HEAD_DIM)
    u_in = low(modln(h, mods[:, 0, None], mods[:, 1, None]))
    qkv = low_back(low(jnp.einsum('gsd,dke->gske', u_in, attend, precision=HIGH)))
    query = qkv[:, :, 0].reshape(count, SEQ, HEADS, HEAD_DIM)
    keys = qkv[:, :, 1].reshape(count, SEQ, HEADS, HEAD_DIM)
    values = qkv[:, :, 2].reshape(count, SEQ, HEADS, HEAD_DIM)
    scores = low_back(jnp.einsum('gqhe,gkhe->ghqk', query, keys, precision=HIGH) * scale)
    probs = low(jax.nn.softmax(scores, -1))
    attended = low_back(low(jnp.einsum('ghqk,gkhe->gqhe', probs, values, precision=HIGH))).reshape(count, SEQ, D)
    branch_a = low_back(jnp.einsum('gsc,dc->gsd', attended, output[:, 0], precision=HIGH))
    h_mid = h + mods[:, 2, None] * branch_a
    w_in = low(modln(h_mid, mods[:, 3, None], mods[:, 4, None]))
    pre = low_back(jnp.einsum('gsd,dk->gsk', w_in, hidden.reshape(D, FF), precision=HIGH))
    act = low(gelu_tanh(pre))
    branch_m = low_back(jnp.einsum('gsk,dk->gsd', act, output[:, 1:].reshape(D, FF), precision=HIGH))
    return h_mid + mods[:, 5, None] * branch_m

def group_loss(weights, batch):
    attend, hidden, output, patch, freq, time, table, cond, head = weights
    latents, noise, var_target, steps, labels = batch
    count = latents.shape[0]
    level = noise_level(steps)[:, None, None]
    noisy = low(jnp.sqrt(level) * latents + jnp.sqrt(1.0 - level) * noise)
    h = jnp.einsum('gsp,dp->gsd', noisy, patch, precision=HIGH) + positions(0, SEQ, D)[None]
    act = jnp.dot(low(time_freqs(steps)), freq.T, precision=HIGH)
    temb = jnp.dot(low(jax.nn.silu(act)), time.T, precision=HIGH)
    onehot = (labels[:, None] == jnp.arange(CLASSES, dtype=jnp.int32)[None]).astype(jnp.float32)
    cvec = temb + jnp.dot(onehot, table.T, precision=HIGH)
    mods = jnp.dot(low(jax.nn.silu(cvec)), cond, precision=HIGH).reshape(count, MODS, D)
    for layer in range(LAYERS):
        h = block(h, mods[:, 6 * layer:6 * layer + 6], attend[layer], hidden[layer], output[layer])
    final_in = low(modln(h, mods[:, 6 * LAYERS, None], mods[:, 6 * LAYERS + 1, None]))
    pred = low_back(jnp.einsum('gsd,dp->gsp', final_in, head, precision=HIGH))
    target = jnp.concatenate([noise, var_target], -1)
    return jnp.sum((pred - target) ** 2)

def adamw(weight, mean, square, grad):
    mean_next = BETA * mean + (1.0 - BETA) * grad
    square_next = BETA * square + (1.0 - BETA) * grad * grad
    fixed_mean = mean_next / (1.0 - BETA ** STEP)
    fixed_square = square_next / (1.0 - BETA ** STEP)
    weight_next = weight - RATE * (fixed_mean / (jnp.sqrt(fixed_square) + EPSILON) + DECAY * weight)
    return [weight_next, mean_next, square_next]

def reference(latents, noise, var_target, timesteps, labels, attend_weight, attend_mean, attend_square, hidden_weight, hidden_mean, hidden_square, output_weight, output_mean, output_square, patch_weight, patch_mean, patch_square, freq_weight, freq_mean, freq_square, time_weight, time_mean, time_square, label_table, label_mean, label_square, cond_weight, cond_mean, cond_square, head_weight, head_mean, head_square):
    trios = [(attend_weight, attend_mean, attend_square), (hidden_weight, hidden_mean, hidden_square), (output_weight, output_mean, output_square), (patch_weight, patch_mean, patch_square), (freq_weight, freq_mean, freq_square), (time_weight, time_mean, time_square), (label_table, label_mean, label_square), (cond_weight, cond_mean, cond_square), (head_weight, head_mean, head_square)]
    weights = tuple((trio[0] for trio in trios))
    groups = IMAGES // IMG_DEV
    batch = (latents.reshape(groups, IMG_DEV, SEQ, PATCH_IN), noise.reshape(groups, IMG_DEV, SEQ, PATCH_IN), var_target.reshape(groups, IMG_DEV, SEQ, PATCH_IN), timesteps.reshape(groups, IMG_DEV), labels.reshape(groups, IMG_DEV))

    def total(params):
        lowered = tuple((low(w) for w in params))
        step_loss = jax.checkpoint(group_loss)

        def scan_step(carry, part):
            return (carry + step_loss(lowered, part), None)
        summed, _ = lax.scan(scan_step, jnp.zeros((), jnp.float32), batch)
        return summed
    loss, back = jax.vjp(total, weights)
    grads = back(jnp.ones((), loss.dtype))[0]
    squares = sum((jnp.sum(g * g) for g in grads))
    grad_norm = jnp.sqrt(squares)
    clip = jnp.minimum(1.0, CLIP / (grad_norm + 1e-06))
    updated = []
    for trio, grad in zip(trios, grads):
        updated.extend(adamw(trio[0], trio[1], trio[2], grad * clip))
    return (loss, grad_norm, *updated)
```

```python
import math

import jax
import jax.numpy as jnp
from jax import lax
from jax.sharding import PartitionSpec as P

HEAD_DIM = 64
FREQ = 256
GRID = 16
STEP = 5


HIGH = lax.Precision.HIGHEST
RATE = 0.05
DECAY = 0.1
BETA = 0.5
EPSILON = 1e-08
CLIP = 1.0
LOW = jnp.bfloat16


def modln(h, shift, scale):
    mean = jnp.mean(h, -1, keepdims=True)
    cent = h - mean
    var = jnp.mean(cent * cent, -1, keepdims=True)
    return cent * lax.rsqrt(var + 1e-06) * (1.0 + scale) + shift


def gelu_tanh(v):
    return jax.nn.gelu(v, approximate=True)


def noise_level(steps):
    phase = (steps.astype(jnp.float32) / 1000.0 + 0.008) / 1.008 * (0.5 * math.pi)
    return jnp.cos(phase) ** 2


def time_freqs(steps):
    half = FREQ // 2
    rates = jnp.exp(-math.log(10000.0) * jnp.arange(half, dtype=jnp.float32) / half)
    angles = steps.astype(jnp.float32)[:, None] * rates[None, :]
    return jnp.concatenate([jnp.cos(angles), jnp.sin(angles)], -1)


def positions(first, count, width):
    index = first + jnp.arange(count, dtype=jnp.int32)
    row = (index // GRID).astype(jnp.float32)
    column = (index % GRID).astype(jnp.float32)
    quarter = width // 4
    rates = jnp.power(10000.0, -jnp.arange(quarter, dtype=jnp.float32) / quarter)
    across = column[:, None] * rates[None, :]
    down = row[:, None] * rates[None, :]
    return jnp.concatenate([jnp.sin(across), jnp.cos(across), jnp.sin(down), jnp.cos(down)], -1)


def adamw(weight, mean, square, grad):
    mean_next = BETA * mean + (1.0 - BETA) * grad
    square_next = BETA * square + (1.0 - BETA) * grad * grad
    fixed_mean = mean_next / (1.0 - BETA**STEP)
    fixed_square = square_next / (1.0 - BETA**STEP)
    weight_next = weight - RATE * (fixed_mean / (jnp.sqrt(fixed_square) + EPSILON) + DECAY * weight)
    return [weight_next, mean_next, square_next]


def rank_sum(left, right):
    total = left[0][:, None] * right[0][None, :]
    for k in range(1, left.shape[0]):
        total = total + left[k][:, None] * right[k][None, :]
    return total


def rank_square(left, right):
    one = jnp.einsum("nd,md->nm", left, left, precision=HIGH)
    two = jnp.einsum("nd,md->nm", right, right, precision=HIGH)
    return jnp.sum(one * two)


def tp_total(part):
    return lax.psum(part.astype(LOW), "tp").astype(jnp.float32)


def gather_layer(attend, hidden, output):
    return (
        lax.all_gather(attend.astype(LOW), "fsdp", axis=0, tiled=True),
        lax.all_gather(hidden.astype(LOW), "fsdp", axis=0, tiled=True),
        lax.all_gather(output.astype(LOW), "fsdp", axis=0, tiled=True),
    )


def reduce_layer(grads):
    shards = [
        lax.psum_scatter(g.astype(LOW), "fsdp", scatter_dimension=0, tiled=True) for g in grads
    ]
    return [lax.psum(s, "ctx").astype(jnp.float32) for s in shards]


def layer_forward(h, mods, weights):
    attend, hidden, output = weights
    count, rows, width = h.shape
    local = attend.shape[2]
    heads = local // HEAD_DIM
    scale = 1.0 / math.sqrt(HEAD_DIM)
    u_in = modln(h, mods[:, 0, None], mods[:, 1, None]).astype(LOW)
    qkv = jnp.einsum("gsd,dke->gske", u_in, attend, preferred_element_type=jnp.float32).astype(LOW)
    both = lax.all_gather(qkv[:, :, 1:], "ctx", axis=1, tiled=True)
    query = qkv[:, :, 0].reshape(count, rows, heads, HEAD_DIM)
    keys = both[:, :, 0].reshape(count, -1, heads, HEAD_DIM)
    values = both[:, :, 1].reshape(count, -1, heads, HEAD_DIM)
    scores = jnp.einsum("gqhe,gkhe->ghqk", query, keys, preferred_element_type=jnp.float32) * scale
    top = jnp.max(scores, -1, keepdims=True)
    expo = jnp.exp(scores - top)
    probs = expo / jnp.sum(expo, -1, keepdims=True)
    probs_low = probs.astype(LOW)
    attended = (
        jnp.einsum("ghqk,gkhe->gqhe", probs_low, values, preferred_element_type=jnp.float32)
        .astype(LOW)
        .reshape(count, rows, local)
    )
    branch_a = tp_total(
        jnp.einsum("gsc,dc->gsd", attended, output[:, 0], preferred_element_type=jnp.float32)
    )
    h_mid = h + mods[:, 2, None] * branch_a
    w_in = modln(h_mid, mods[:, 3, None], mods[:, 4, None]).astype(LOW)
    pre = jnp.einsum("gsd,dkc->gskc", w_in, hidden, preferred_element_type=jnp.float32).reshape(
        count, rows, 4 * local
    )
    act = gelu_tanh(pre).astype(LOW)
    out_mlp = output[:, 1:].reshape(width, 4 * local)
    branch_m = tp_total(jnp.einsum("gsk,dk->gsd", act, out_mlp, preferred_element_type=jnp.float32))
    h_out = h_mid + mods[:, 5, None] * branch_m
    kept = (h, u_in, query, keys, values, probs, probs_low, attended, branch_a, h_mid, w_in, pre)
    return h_out, kept + (act, out_mlp, branch_m)


def layer_backward(kept, mods, weights, grad_out):
    attend, hidden, output = weights
    (h, u_in, query, keys, values, probs, probs_low, attended, branch_a, h_mid, w_in, pre) = kept[:12]
    act, out_mlp, branch_m = kept[12:]
    count, rows, width = h.shape
    local = attend.shape[2]
    scale = 1.0 / math.sqrt(HEAD_DIM)
    d_gate_m = jnp.sum(grad_out * branch_m, 1)
    d_branch = (mods[:, 5, None] * grad_out).astype(LOW)
    d_act = jnp.einsum("gsd,dk->gsk", d_branch, out_mlp, preferred_element_type=jnp.float32)
    d_out_mlp = jnp.einsum("gsd,gsk->dk", d_branch, act, preferred_element_type=jnp.float32)
    _, gelu_back = jax.vjp(gelu_tanh, pre)
    d_pre = gelu_back(d_act)[0].astype(LOW).reshape(count, rows, 4, local)
    d_hidden = jnp.einsum("gsd,gskc->dkc", w_in, d_pre, preferred_element_type=jnp.float32)
    d_w = tp_total(jnp.einsum("gskc,dkc->gsd", d_pre, hidden, preferred_element_type=jnp.float32))
    _, norm_back = jax.vjp(modln, h_mid, mods[:, 3, None], mods[:, 4, None])
    d_mid, d_shift_m, d_scale_m = norm_back(d_w)
    d_mid = d_mid + grad_out
    d_gate_a = jnp.sum(d_mid * branch_a, 1)
    d_branch_a = (mods[:, 2, None] * d_mid).astype(LOW)
    d_att = jnp.einsum(
        "gsd,dc->gsc", d_branch_a, output[:, 0], preferred_element_type=jnp.float32
    ).astype(LOW)
    d_out_att = jnp.einsum("gsd,gsc->dc", d_branch_a, attended, preferred_element_type=jnp.float32)
    d_att = d_att.reshape(count, rows, -1, HEAD_DIM)
    d_probs = jnp.einsum("gqhe,gkhe->ghqk", d_att, values, preferred_element_type=jnp.float32)
    d_values = jnp.einsum("ghqk,gqhe->gkhe", probs_low, d_att, preferred_element_type=jnp.float32)
    d_scores = (probs * (d_probs - jnp.sum(d_probs * probs, -1, keepdims=True))).astype(LOW)
    d_query = (
        jnp.einsum("ghqk,gkhe->gqhe", d_scores, keys, preferred_element_type=jnp.float32) * scale
    ).astype(LOW)
    d_keys = (
        jnp.einsum("ghqk,gqhe->gkhe", d_scores, query, preferred_element_type=jnp.float32) * scale
    )
    d_both = lax.psum_scatter(
        jnp.stack(
            [d_keys.reshape(count, -1, local), d_values.reshape(count, -1, local)], 2
        ).astype(LOW),
        "ctx",
        scatter_dimension=1,
        tiled=True,
    )
    d_qkv = jnp.concatenate([d_query.reshape(count, rows, 1, local), d_both], 2)
    d_attend = jnp.einsum("gsd,gske->dke", u_in, d_qkv, preferred_element_type=jnp.float32)
    d_u = tp_total(jnp.einsum("gske,dke->gsd", d_qkv, attend, preferred_element_type=jnp.float32))
    _, norm_back = jax.vjp(modln, h, mods[:, 0, None], mods[:, 1, None])
    d_h, d_shift_a, d_scale_a = norm_back(d_u)
    d_mods = jnp.stack(
        [d_shift_a[:, 0], d_scale_a[:, 0], d_gate_a, d_shift_m[:, 0], d_scale_m[:, 0], d_gate_m], 1
    )
    d_output = jnp.concatenate([d_out_att[:, None], d_out_mlp.reshape(width, 4, local)], 1)
    return (d_h + d_mid, d_mods, (d_attend, d_hidden, d_output))


def per_device(
    latents,
    noise,
    var_target,
    timesteps,
    labels,
    attend_weight,
    attend_mean,
    attend_square,
    hidden_weight,
    hidden_mean,
    hidden_square,
    output_weight,
    output_mean,
    output_square,
    patch_weight,
    patch_mean,
    patch_square,
    freq_weight,
    freq_mean,
    freq_square,
    time_weight,
    time_mean,
    time_square,
    label_table,
    label_mean,
    label_square,
    cond_weight,
    cond_mean,
    cond_square,
    head_weight,
    head_mean,
    head_square,
):
    count, rows, patch_in = latents.shape
    layers, shard = attend_weight.shape[:2]
    columns = cond_weight.shape[1]

    steps_all = lax.all_gather(timesteps, "fsdp", axis=0, tiled=True)
    labels_all = lax.all_gather(labels, "fsdp", axis=0, tiled=True)
    freqs = time_freqs(steps_all).astype(LOW)
    act = jnp.dot(freqs, freq_weight.astype(LOW).T, preferred_element_type=jnp.float32)
    swish = lax.all_gather(jax.nn.silu(act).astype(LOW), "fsdp", axis=1, tiled=True)
    time_low = time_weight.astype(LOW)
    temb = jnp.dot(swish, time_low.T, preferred_element_type=jnp.float32)
    onehot = (labels_all[:, None] == jnp.arange(label_table.shape[1], dtype=jnp.int32)[None]).astype(
        LOW
    )
    cvec = temb + jnp.dot(onehot, label_table.astype(LOW).T, preferred_element_type=jnp.float32)
    cond_in = jax.nn.silu(cvec).astype(LOW)
    cond_low = cond_weight.astype(LOW)
    mods = lax.psum_scatter(
        jnp.dot(cond_in, cond_low, preferred_element_type=jnp.float32),
        "fsdp",
        scatter_dimension=0,
        tiled=True,
    )
    patch_head = lax.all_gather(
        jnp.concatenate([patch_weight, head_weight], 1).astype(LOW), "fsdp", axis=0, tiled=True
    )
    patch_full, head_full = patch_head[:, :patch_in], patch_head[:, patch_in:]
    width = patch_full.shape[0]
    mods = lax.all_gather(mods, "tp", axis=1, tiled=True).reshape(count, -1, width)

    level = noise_level(timesteps)[:, None, None]
    noisy = (jnp.sqrt(level) * latents + jnp.sqrt(1.0 - level) * noise).astype(LOW)
    first = lax.axis_index("ctx") * rows
    h = (
        jnp.einsum("gsp,dp->gsd", noisy, patch_full, preferred_element_type=jnp.float32)
        + positions(first, rows, width)[None]
    )
    kept = []
    weights = []
    for layer in range(layers):
        weights.append(
            gather_layer(attend_weight[layer], hidden_weight[layer], output_weight[layer])
        )
        h, saved = layer_forward(h, mods[:, 6 * layer : 6 * layer + 6], weights[layer])
        kept.append(saved)
    final_in = modln(h, mods[:, 6 * layers, None], mods[:, 6 * layers + 1, None]).astype(LOW)
    pred = jnp.einsum("gsd,dp->gsp", final_in, head_full, preferred_element_type=jnp.float32)
    diff = pred - jnp.concatenate([noise, var_target], -1)
    loss = lax.psum(jnp.sum(diff * diff), ("fsdp", "ctx"))
    d_pred = (2.0 * diff).astype(LOW)
    d_head = jnp.einsum("gsd,gsp->dp", final_in, d_pred, preferred_element_type=jnp.float32)
    d_final = jnp.einsum("gsp,dp->gsd", d_pred, head_full, preferred_element_type=jnp.float32)
    _, norm_back = jax.vjp(modln, h, mods[:, 6 * layers, None], mods[:, 6 * layers + 1, None])
    d_h, d_shift_f, d_scale_f = norm_back(d_final)
    mod_grads = [None] * layers
    layer_shards = [None] * layers
    for layer in reversed(range(layers)):
        d_h, mod_grads[layer], grads = layer_backward(
            kept[layer], mods[:, 6 * layer : 6 * layer + 6], weights[layer], d_h
        )
        layer_shards[layer] = reduce_layer(grads)

    d_mods = jnp.concatenate(mod_grads + [d_shift_f, d_scale_f], 1).reshape(count, -1)
    d_cols = lax.dynamic_slice_in_dim(d_mods, lax.axis_index("tp") * columns, columns, 1)
    d_cols = lax.all_gather(lax.psum(d_cols, "ctx"), "fsdp", axis=0, tiled=True)
    d_silu = lax.psum(
        jnp.dot(d_cols, cond_low.astype(jnp.float32).T, precision=HIGH), "tp"
    )
    _, silu_back = jax.vjp(jax.nn.silu, cvec)
    d_cvec = silu_back(d_silu)[0]
    d_swish = lax.psum_scatter(
        jnp.dot(d_cvec, time_low.astype(jnp.float32), precision=HIGH),
        "fsdp",
        scatter_dimension=1,
        tiled=True,
    )
    _, act_back = jax.vjp(jax.nn.silu, act)
    d_act = act_back(d_swish)[0]
    d_patch = jnp.einsum("gsd,gsp->dp", d_h, noisy.astype(jnp.float32), precision=HIGH)
    d_small = lax.psum(
        lax.psum_scatter(
            jnp.concatenate([d_patch, d_head], 1), "fsdp", scatter_dimension=0, tiled=True
        ),
        "ctx",
    )
    lefts = {"freq": d_act, "time": d_cvec, "label": d_cvec, "cond": cond_in.astype(jnp.float32)}
    rights = {
        "freq": freqs.astype(jnp.float32),
        "time": swish.astype(jnp.float32),
        "label": onehot.astype(jnp.float32),
        "cond": d_cols,
    }

    split_sq = sum(jnp.sum(g * g) for parts in layer_shards for g in parts) + rank_square(
        lefts["cond"], rights["cond"]
    )
    copied_sq = jnp.sum(d_small * d_small) + sum(
        rank_square(lefts[k], rights[k]) for k in ("freq", "time", "label")
    )
    total_sq = lax.psum(split_sq + copied_sq / lax.axis_size("tp"), ("fsdp", "tp"))
    grad_norm = jnp.sqrt(total_sq)
    clip = jnp.minimum(1.0, CLIP / (grad_norm + 1e-06))
    grads_all = (
        jnp.stack([s[0] for s in layer_shards]),
        jnp.stack([s[1] for s in layer_shards]),
        jnp.stack([s[2] for s in layer_shards]),
        d_small[:, :patch_in],
        rank_sum(lefts["freq"], rights["freq"]),
        rank_sum(lefts["time"], rights["time"]),
        rank_sum(lefts["label"], rights["label"]),
        rank_sum(lefts["cond"], rights["cond"]),
        d_small[:, patch_in:],
    )
    olds = (
        (attend_weight, attend_mean, attend_square),
        (hidden_weight, hidden_mean, hidden_square),
        (output_weight, output_mean, output_square),
        (patch_weight, patch_mean, patch_square),
        (freq_weight, freq_mean, freq_square),
        (time_weight, time_mean, time_square),
        (label_table, label_mean, label_square),
        (cond_weight, cond_mean, cond_square),
        (head_weight, head_mean, head_square),
    )
    updated = []
    for trio, grad in zip(olds, grads_all):
        updated.extend(adamw(trio[0], trio[1], trio[2], grad * clip))
    return (loss, grad_norm, *updated)


def solution(mesh):
    image = P("fsdp", "ctx", None)
    layer = P(None, "fsdp", None, "tp")
    rows = P("fsdp", None)
    cond = P("fsdp", "tp")
    weights = (layer,) * 9 + (rows,) * 12 + (cond,) * 3 + (rows,) * 3
    return jax.shard_map(
        per_device,
        mesh=mesh,
        in_specs=(image, image, image, P("fsdp"), P("fsdp")) + weights,
        out_specs=(P(), P()) + weights,
        check_vma=False,
    )
```

```python
import functools
import math

import jax
import jax.numpy as jnp
from jax import lax
from jax.experimental import pallas as pl
from jax.experimental.pallas import tpu as pltpu
from jax.sharding import PartitionSpec as P

HEAD_DIM = 64
FREQ = 256
GRID = 16
STEP = 5


HIGH = lax.Precision.HIGHEST
RATE = 0.05
DECAY = 0.1
BETA = 0.5
EPSILON = 1e-08
CLIP = 1.0
LOW = jnp.bfloat16


def modln(h, shift, scale):
    mean = jnp.mean(h, -1, keepdims=True)
    cent = h - mean
    var = jnp.mean(cent * cent, -1, keepdims=True)
    return cent * lax.rsqrt(var + 1e-06) * (1.0 + scale) + shift


def gelu_tanh(v):
    return jax.nn.gelu(v, approximate=True)


def noise_level(steps):
    phase = (steps.astype(jnp.float32) / 1000.0 + 0.008) / 1.008 * (0.5 * math.pi)
    return jnp.cos(phase) ** 2


def time_freqs(steps):
    half = FREQ // 2
    rates = jnp.exp(-math.log(10000.0) * jnp.arange(half, dtype=jnp.float32) / half)
    angles = steps.astype(jnp.float32)[:, None] * rates[None, :]
    return jnp.concatenate([jnp.cos(angles), jnp.sin(angles)], -1)


def positions(first, count, width):
    index = first + jnp.arange(count, dtype=jnp.int32)
    row = (index // GRID).astype(jnp.float32)
    column = (index % GRID).astype(jnp.float32)
    quarter = width // 4
    rates = jnp.power(10000.0, -jnp.arange(quarter, dtype=jnp.float32) / quarter)
    across = column[:, None] * rates[None, :]
    down = row[:, None] * rates[None, :]
    return jnp.concatenate([jnp.sin(across), jnp.cos(across), jnp.sin(down), jnp.cos(down)], -1)


def adamw(weight, mean, square, grad):
    mean_next = BETA * mean + (1.0 - BETA) * grad
    square_next = BETA * square + (1.0 - BETA) * grad * grad
    fixed_mean = mean_next / (1.0 - BETA**STEP)
    fixed_square = square_next / (1.0 - BETA**STEP)
    weight_next = weight - RATE * (fixed_mean / (jnp.sqrt(fixed_square) + EPSILON) + DECAY * weight)
    return [weight_next, mean_next, square_next]


def rank_sum(left, right):
    total = left[0][:, None] * right[0][None, :]
    for k in range(1, left.shape[0]):
        total = total + left[k][:, None] * right[k][None, :]
    return total


def rank_square(left, right):
    one = jnp.einsum("nd,md->nm", left, left, precision=HIGH)
    two = jnp.einsum("nd,md->nm", right, right, precision=HIGH)
    return jnp.sum(one * two)


def tp_total(part):
    return lax.psum(part.astype(LOW), "tp").astype(jnp.float32)


def gather_layer(attend, hidden, output):
    return (
        lax.all_gather(attend.astype(LOW), "fsdp", axis=0, tiled=True),
        lax.all_gather(hidden.astype(LOW), "fsdp", axis=0, tiled=True),
        lax.all_gather(output.astype(LOW), "fsdp", axis=0, tiled=True),
    )


def reduce_layer(grads):
    shards = [
        lax.psum_scatter(g.astype(LOW), "fsdp", scatter_dimension=0, tiled=True) for g in grads
    ]
    return [lax.psum(s, "ctx").astype(jnp.float32) for s in shards]


MESH = pl.DeviceIdType.MESH


def dot(left, right):
    return jnp.dot(left, right, preferred_element_type=jnp.float32)


def dot_nt(left, right):
    return lax.dot_general(left, right, (((1,), (1,)), ((), ())), preferred_element_type=jnp.float32)


def dot_tn(left, right):
    return lax.dot_general(left, right, (((0,), (0,)), ((), ())), preferred_element_type=jnp.float32)


def remote(src, dst, sems, where, **device):
    send, recv = (sems.at[(0, *where)], sems.at[(1, *where)])
    return pltpu.make_async_remote_copy(
        src_ref=src, dst_ref=dst, send_sem=send, recv_sem=recv, device_id=device, device_id_type=MESH
    )


def meet(sizes):
    barrier = pltpu.get_barrier_semaphore()
    count = 0
    for axis, size in sizes.items():
        for step in range(1, size):
            peer = lax.rem(lax.axis_index(axis) + step, size)
            pl.semaphore_signal(barrier, inc=1, device_id={axis: peer}, device_id_type=MESH)
            count += 1
    pl.semaphore_wait(barrier, count)


def norm_parts(h):
    mean = jnp.mean(h, -1, keepdims=True)
    cent = h - mean
    var = jnp.mean(cent * cent, -1, keepdims=True)
    inv = lax.rsqrt(var + 1e-06)
    return cent * inv, inv


def norm_back(grad, normed, inv, scale):
    grad_shift = jnp.sum(grad, 1)
    grad_scale = jnp.sum(grad * normed, 1)
    inner = grad * (1.0 + scale)
    mean = jnp.mean(inner, -1, keepdims=True)
    along = jnp.mean(inner * normed, -1, keepdims=True)
    return inv * (inner - mean - normed * along), grad_shift, grad_scale


def tp_send(part, size, send, first, sems):
    me = lax.axis_index("tp")
    send[...] = part.astype(LOW).reshape(send.shape)
    for step in range(1, size):
        peer = lax.rem(me + step, size)
        remote(send.at[peer], first.at[step - 1], sems, (0, step - 1), tp=peer).start()


def tp_finish(size, send, first, full, sems):
    me = lax.axis_index("tp")
    total = send[me].astype(jnp.float32)
    for step in range(1, size):
        peer = lax.rem(me + step, size)
        remote(send.at[peer], first.at[step - 1], sems, (0, step - 1), tp=peer).wait()
        total = total + first[step - 1].astype(jnp.float32)
    full[me] = total.astype(LOW)
    for step in range(1, size):
        peer = lax.rem(me + step, size)
        remote(full.at[me], full.at[me], sems, (1, step - 1), tp=peer).start()
    for step in range(1, size):
        peer = lax.rem(me + step, size)
        source = lax.rem(me + size - step, size)
        remote(full.at[me], full.at[me], sems, (1, step - 1), tp=peer).wait_send()
        remote(full.at[source], full.at[source], sems, (1, step - 1), tp=peer).wait_recv()


def spread(block, heads):
    lane = lax.broadcasted_iota(jnp.int32, block.shape, 1) // HEAD_DIM
    zero = jnp.zeros_like(block)
    return jnp.concatenate([jnp.where(lane == k, block, zero) for k in range(heads)], 0)


def pick(stacked, heads):
    rows = stacked.shape[0] // heads
    lane = lax.broadcasted_iota(jnp.int32, (rows, stacked.shape[1]), 1) // HEAD_DIM
    total = jnp.zeros((rows, stacked.shape[1]), stacked.dtype)
    for k in range(heads):
        total = jnp.where(lane == k, stacked[k * rows : (k + 1) * rows], total)
    return total


ROOT_2_PI = math.sqrt(2.0 / math.pi)


def gelu_parts(v):
    inside = jnp.tanh(ROOT_2_PI * (v + 0.044715 * (v * v * v)))
    value = v * (0.5 * (1.0 + inside))
    slope = 0.5 * (1.0 + inside) + 0.5 * v * (1.0 - inside * inside) * ROOT_2_PI * (
        1.0 + 3 * 0.044715 * v * v
    )
    return value, slope


def forward_kernel(
    sizes, h0_ref, mods_ref, low_ref, h_out, full_ref,
    keep_h, keep_mid, keep_a, keep_m, keep_q, keep_kv, keep_p, keep_att, keep_pre,
    weights, kv, h_ref, send_a, first_a, full_a, send_m, first_m, full_m,
    x_sems, pair_sems, own_sems, kv_sems, a_sems, m_sems,
):
    nf, nc, nt = sizes["fsdp"], sizes["ctx"], sizes["tp"]
    layer, layers = pl.program_id(0), pl.num_programs(0)
    total_layers = low_ref.shape[0]
    f, c = lax.axis_index("fsdp"), lax.axis_index("ctx")
    core = lax.rem(c, 2)
    sibling = c + 1 - 2 * core
    count, rows, width = h_ref.shape
    local = weights.shape[-1]
    heads = local // HEAD_DIM
    scale = 1.0 / math.sqrt(HEAD_DIM)

    def x_copy(k, step):
        peer = lax.rem(f + step, nf)
        return remote(
            low_ref.at[k, :, core], weights.at[k, :, f, core], x_sems, (k, step - 1), fsdp=peer
        )

    def x_arrived(k, step):
        source = lax.rem(f + nf - step, nf)
        block = weights.at[k, :, source, core]
        remote(block, block, x_sems, (k, step - 1), fsdp=source).wait_recv()

    def pair_copy(k, step, half):
        source = lax.rem(f + nf - step, nf)
        block = weights.at[k, :, source, half]
        return remote(block, block, pair_sems, (k, step - 1), ctx=sibling)

    def own_copy(k):
        return pltpu.make_async_copy(low_ref.at[k], weights.at[k, :, f], own_sems.at[0, k])

    def store_copy(k):
        return pltpu.make_async_copy(weights.at[k], full_ref.at[k], own_sems.at[1, k])

    def pass_on(k):
        for step in range(1, nf):
            x_arrived(k, step)
            pair_copy(k, step, core).start()

    @pl.when(layer == 0)
    def _():
        meet(sizes)
        for k in range(total_layers):
            for step in range(1, nf):
                x_copy(k, step).start()
            own_copy(k).start()
        h_ref[...] = h0_ref[...]
        pass_on(0)

    def mod(k):
        return mods_ref[6 * layer + k]

    own_copy(layer).wait()
    for step in range(1, nf):
        pair_copy(layer, step, 1 - core).wait_recv()
    store_copy(layer).start()

    def matrix(k):
        return weights[layer, k].reshape(width, local)

    h = h_ref[...]
    keep_h[0] = h
    normed, _ = norm_parts(h)
    u_in = (normed * (1.0 + mod(1)) + mod(0)).astype(LOW).reshape(count * rows, width)
    key = dot(u_in, matrix(1)).astype(LOW)
    kv[layer, c, :, :, :local] = key.reshape(count, rows, local)
    value = dot(u_in, matrix(2)).astype(LOW)
    kv[layer, c, :, :, local:] = value.reshape(count, rows, local)
    for step in range(1, nc):
        peer = lax.rem(c + step, nc)
        block = kv.at[layer, c]
        remote(block, block, kv_sems, (layer, step - 1), ctx=peer).start()
    query = dot(u_in, matrix(0)).astype(LOW)
    keep_q[0] = query.reshape(count, rows, local)
    for step in range(1, nc):
        peer = lax.rem(c + step, nc)
        source = lax.rem(c + nc - step, nc)
        remote(kv.at[layer, c], kv.at[layer, c], kv_sems, (layer, step - 1), ctx=peer).wait_send()
        block = kv.at[layer, source]
        remote(block, block, kv_sems, (layer, step - 1), ctx=peer).wait_recv()
    keep_kv[0] = kv[layer]
    for g in range(count):
        keys = kv[layer, :, g, :, :local].reshape(nc * rows, local)
        values = kv[layer, :, g, :, local:].reshape(nc * rows, local)
        stacked = spread(query[g * rows : (g + 1) * rows], heads)
        scores = dot_nt(stacked, keys) * scale
        expo = jnp.exp(scores - jnp.max(scores, -1, keepdims=True))
        probs = expo / jnp.sum(expo, -1, keepdims=True)
        keep_p[0, g] = probs
        keep_att[0, g * rows : (g + 1) * rows] = pick(dot(probs.astype(LOW), values), heads).astype(LOW)
    tp_send(dot_nt(keep_att[0], matrix(7)), nt, send_a, first_a, a_sems)
    tp_finish(nt, send_a, first_a, full_a, a_sems)
    branch = full_a[...].reshape(count, rows, width)
    keep_a[0] = branch
    h_mid = h_ref[...] + mod(2) * branch.astype(jnp.float32)
    keep_mid[0] = h_mid
    normed, _ = norm_parts(h_mid)
    w_in = (normed * (1.0 + mod(4)) + mod(3)).astype(LOW).reshape(count * rows, width)
    part = jnp.zeros((count * rows, width), jnp.float32)
    for k in range(4):
        pre = dot(w_in, matrix(3 + k))
        keep_pre[0, k] = pre
        part = part + dot_nt(gelu_parts(pre)[0].astype(LOW), matrix(8 + k))
    tp_send(part, nt, send_m, first_m, m_sems)

    @pl.when(layer + 1 < layers)
    def _():
        pass_on(layer + 1)

    tp_finish(nt, send_m, first_m, full_m, m_sems)
    branch = full_m[...].reshape(count, rows, width)
    keep_m[0] = branch
    h_ref[...] = keep_mid[0] + mod(5) * branch.astype(jnp.float32)

    @pl.when(layer == layers - 1)
    def _():
        h_out[...] = h_ref[...]
        for k in range(total_layers):
            store_copy(k).wait()
            for step in range(1, nf):
                x_copy(k, step).wait_send()
                pair_copy(k, step, core).wait_send()


def forward(mesh, h0, mods, low):
    sizes = dict(mesh.shape)
    nf, nc, nt = sizes["fsdp"], sizes["ctx"], sizes["tp"]
    count, rows, width = h0.shape
    layers, blocks, _, half, local = low.shape
    heads = local // HEAD_DIM
    tokens = count * rows
    f32 = jnp.float32

    def kept(shape, dtype):
        spec = pl.BlockSpec((1, *shape), lambda i: (i,) + (0,) * len(shape))
        return jax.ShapeDtypeStruct((layers, *shape), dtype), spec

    saves = [
        kept((count, rows, width), f32),
        kept((count, rows, width), f32),
        kept((count, rows, width), LOW),
        kept((count, rows, width), LOW),
        kept((count, rows, local), LOW),
        kept((nc, count, rows, 2 * local), LOW),
        kept((count, heads * rows, nc * rows), f32),
        kept((tokens, local), LOW),
        kept((4, tokens, local), f32),
    ]
    anywhere = pl.BlockSpec(memory_space=pl.ANY)
    vmem = pl.BlockSpec(memory_space=pltpu.VMEM)
    part = pltpu.VMEM((nt, tokens // nt, width), LOW)
    first = pltpu.VMEM((nt - 1, tokens // nt, width), LOW)
    dma = pltpu.SemaphoreType.DMA
    return pl.pallas_call(
        functools.partial(forward_kernel, sizes),
        grid=(layers,),
        out_shape=[
            jax.ShapeDtypeStruct(h0.shape, f32),
            jax.ShapeDtypeStruct((layers, blocks, nf, 2, half, local), LOW),
            *(shape for shape, _ in saves),
        ],
        in_specs=[vmem, vmem, anywhere],
        out_specs=[vmem, anywhere, *(spec for _, spec in saves)],
        scratch_shapes=[
            pltpu.VMEM((layers, blocks, nf, 2, half, local), LOW),
            pltpu.VMEM((layers, nc, count, rows, 2 * local), LOW),
            pltpu.VMEM((count, rows, width), f32),
            part, first, part, part, first, part,
            dma((2, layers, max(nf - 1, 1))),
            dma((2, layers, max(nf - 1, 1))),
            dma((2, layers)),
            dma((2, layers, nc - 1)),
            dma((2, 2, nt - 1)),
            dma((2, 2, nt - 1)),
        ],
        compiler_params=pltpu.CompilerParams(
            collective_id=1, has_side_effects=True, vmem_limit_bytes=56 * 2**20
        ),
        cost_estimate=pl.CostEstimate(
            flops=2 * tokens * width * blocks * local * layers,
            bytes_accessed=layers * blocks * width * local * 4,
            transcendentals=0,
        ),
        name="forward_layers",
    )(h0, mods, low)


def layer_backward(kept, mods, weights, grad_out):
    attend, hidden, output = weights
    (h, u_in, query, keys, values, probs, probs_low, attended, branch_a, h_mid, w_in, pre) = kept[:12]
    act, out_mlp, branch_m = kept[12:]
    count, rows, width = h.shape
    local = attend.shape[2]
    scale = 1.0 / math.sqrt(HEAD_DIM)
    d_gate_m = jnp.sum(grad_out * branch_m, 1)
    d_branch = (mods[:, 5, None] * grad_out).astype(LOW)
    d_act = jnp.einsum("gsd,dk->gsk", d_branch, out_mlp, preferred_element_type=jnp.float32)
    d_out_mlp = jnp.einsum("gsd,gsk->dk", d_branch, act, preferred_element_type=jnp.float32)
    _, gelu_back = jax.vjp(gelu_tanh, pre)
    d_pre = gelu_back(d_act)[0].astype(LOW).reshape(count, rows, 4, local)
    d_hidden = jnp.einsum("gsd,gskc->dkc", w_in, d_pre, preferred_element_type=jnp.float32)
    d_w = tp_total(jnp.einsum("gskc,dkc->gsd", d_pre, hidden, preferred_element_type=jnp.float32))
    _, norm_back = jax.vjp(modln, h_mid, mods[:, 3, None], mods[:, 4, None])
    d_mid, d_shift_m, d_scale_m = norm_back(d_w)
    d_mid = d_mid + grad_out
    d_gate_a = jnp.sum(d_mid * branch_a, 1)
    d_branch_a = (mods[:, 2, None] * d_mid).astype(LOW)
    d_att = jnp.einsum(
        "gsd,dc->gsc", d_branch_a, output[:, 0], preferred_element_type=jnp.float32
    ).astype(LOW)
    d_out_att = jnp.einsum("gsd,gsc->dc", d_branch_a, attended, preferred_element_type=jnp.float32)
    d_att = d_att.reshape(count, rows, -1, HEAD_DIM)
    d_probs = jnp.einsum("gqhe,gkhe->ghqk", d_att, values, preferred_element_type=jnp.float32)
    d_values = jnp.einsum("ghqk,gqhe->gkhe", probs_low, d_att, preferred_element_type=jnp.float32)
    d_scores = (probs * (d_probs - jnp.sum(d_probs * probs, -1, keepdims=True))).astype(LOW)
    d_query = (
        jnp.einsum("ghqk,gkhe->gqhe", d_scores, keys, preferred_element_type=jnp.float32) * scale
    ).astype(LOW)
    d_keys = (
        jnp.einsum("ghqk,gqhe->gkhe", d_scores, query, preferred_element_type=jnp.float32) * scale
    )
    d_both = lax.psum_scatter(
        jnp.stack(
            [d_keys.reshape(count, -1, local), d_values.reshape(count, -1, local)], 2
        ).astype(LOW),
        "ctx",
        scatter_dimension=1,
        tiled=True,
    )
    d_qkv = jnp.concatenate([d_query.reshape(count, rows, 1, local), d_both], 2)
    d_attend = jnp.einsum("gsd,gske->dke", u_in, d_qkv, preferred_element_type=jnp.float32)
    d_u = tp_total(jnp.einsum("gske,dke->gsd", d_qkv, attend, preferred_element_type=jnp.float32))
    _, norm_back = jax.vjp(modln, h, mods[:, 0, None], mods[:, 1, None])
    d_h, d_shift_a, d_scale_a = norm_back(d_u)
    d_mods = jnp.stack(
        [d_shift_a[:, 0], d_scale_a[:, 0], d_gate_a, d_shift_m[:, 0], d_scale_m[:, 0], d_gate_m], 1
    )
    d_output = jnp.concatenate([d_out_att[:, None], d_out_mlp.reshape(width, 4, local)], 1)
    return (d_h + d_mid, d_mods, (d_attend, d_hidden, d_output))


def per_device(
    mesh,
    latents,
    noise,
    var_target,
    timesteps,
    labels,
    attend_weight,
    attend_mean,
    attend_square,
    hidden_weight,
    hidden_mean,
    hidden_square,
    output_weight,
    output_mean,
    output_square,
    patch_weight,
    patch_mean,
    patch_square,
    freq_weight,
    freq_mean,
    freq_square,
    time_weight,
    time_mean,
    time_square,
    label_table,
    label_mean,
    label_square,
    cond_weight,
    cond_mean,
    cond_square,
    head_weight,
    head_mean,
    head_square,
):
    count, rows, patch_in = latents.shape
    layers, shard = attend_weight.shape[:2]
    columns = cond_weight.shape[1]

    steps_all = lax.all_gather(timesteps, "fsdp", axis=0, tiled=True)
    labels_all = lax.all_gather(labels, "fsdp", axis=0, tiled=True)
    freqs = time_freqs(steps_all).astype(LOW)
    act = jnp.dot(freqs, freq_weight.astype(LOW).T, preferred_element_type=jnp.float32)
    swish = lax.all_gather(jax.nn.silu(act).astype(LOW), "fsdp", axis=1, tiled=True)
    time_low = time_weight.astype(LOW)
    temb = jnp.dot(swish, time_low.T, preferred_element_type=jnp.float32)
    onehot = (labels_all[:, None] == jnp.arange(label_table.shape[1], dtype=jnp.int32)[None]).astype(
        LOW
    )
    cvec = temb + jnp.dot(onehot, label_table.astype(LOW).T, preferred_element_type=jnp.float32)
    cond_in = jax.nn.silu(cvec).astype(LOW)
    cond_low = cond_weight.astype(LOW)
    mods = lax.psum_scatter(
        jnp.dot(cond_in, cond_low, preferred_element_type=jnp.float32),
        "fsdp",
        scatter_dimension=0,
        tiled=True,
    )
    patch_head = lax.all_gather(
        jnp.concatenate([patch_weight, head_weight], 1).astype(LOW), "fsdp", axis=0, tiled=True
    )
    patch_full, head_full = patch_head[:, :patch_in], patch_head[:, patch_in:]
    width = patch_full.shape[0]
    mods = lax.all_gather(mods, "tp", axis=1, tiled=True).reshape(count, -1, width)

    level = noise_level(timesteps)[:, None, None]
    noisy = (jnp.sqrt(level) * latents + jnp.sqrt(1.0 - level) * noise).astype(LOW)
    first = lax.axis_index("ctx") * rows
    h = (
        jnp.einsum("gsp,dp->gsd", noisy, patch_full, preferred_element_type=jnp.float32)
        + positions(first, rows, width)[None]
    )
    low = jnp.concatenate(
        [jnp.swapaxes(w, 1, 2).astype(LOW) for w in (attend_weight, hidden_weight, output_weight)], 1
    ).reshape(layers, -1, 2, shard // 2, attend_weight.shape[3])
    spread_mods = jnp.swapaxes(mods, 0, 1)[:, :, None]
    h, full, *saved = forward(mesh, h, spread_mods, low)
    full = full.reshape(layers, low.shape[1], width, -1)
    final_in = modln(h, mods[:, 6 * layers, None], mods[:, 6 * layers + 1, None]).astype(LOW)
    pred = jnp.einsum("gsd,dp->gsp", final_in, head_full, preferred_element_type=jnp.float32)
    diff = pred - jnp.concatenate([noise, var_target], -1)
    loss = lax.psum(jnp.sum(diff * diff), ("fsdp", "ctx"))
    d_pred = (2.0 * diff).astype(LOW)
    d_head = jnp.einsum("gsd,gsp->dp", final_in, d_pred, preferred_element_type=jnp.float32)
    d_final = jnp.einsum("gsp,dp->gsd", d_pred, head_full, preferred_element_type=jnp.float32)
    _, norm_back = jax.vjp(modln, h, mods[:, 6 * layers, None], mods[:, 6 * layers + 1, None])
    d_h, d_shift_f, d_scale_f = norm_back(d_final)
    mod_grads = [None] * layers
    layer_shards = [None] * layers
    for layer in reversed(range(layers)):
        weights = tuple(
            jnp.swapaxes(full[layer, lo:hi], 0, 1) for lo, hi in ((0, 3), (3, 7), (7, 12))
        )
        keep_h, keep_mid, keep_a, keep_m, keep_q, keep_kv, keep_p, keep_att, keep_pre = (
            k[layer] for k in saved
        )
        m = mods[:, 6 * layer : 6 * layer + 6]
        heads = keep_q.shape[-1] // HEAD_DIM
        both = jnp.swapaxes(keep_kv, 0, 1).reshape(count, -1, 2, heads, HEAD_DIM)
        probs = keep_p.reshape(count, heads, rows, -1)
        pre = jnp.swapaxes(keep_pre, 0, 1).reshape(count, rows, -1)
        kept = (
            keep_h,
            modln(keep_h, m[:, 0, None], m[:, 1, None]).astype(LOW),
            keep_q.reshape(count, rows, heads, HEAD_DIM),
            both[:, :, 0],
            both[:, :, 1],
            probs,
            probs.astype(LOW),
            keep_att.reshape(count, rows, -1),
            keep_a.astype(jnp.float32),
            keep_mid,
            modln(keep_mid, m[:, 3, None], m[:, 4, None]).astype(LOW),
            pre,
            gelu_tanh(pre).astype(LOW),
            weights[2][:, 1:].reshape(width, -1),
            keep_m.astype(jnp.float32),
        )
        d_h, mod_grads[layer], grads = layer_backward(kept, m, weights, d_h)
        layer_shards[layer] = reduce_layer(grads)

    d_mods = jnp.concatenate(mod_grads + [d_shift_f, d_scale_f], 1).reshape(count, -1)
    d_cols = lax.dynamic_slice_in_dim(d_mods, lax.axis_index("tp") * columns, columns, 1)
    d_cols = lax.all_gather(lax.psum(d_cols, "ctx"), "fsdp", axis=0, tiled=True)
    d_silu = lax.psum(
        jnp.dot(d_cols, cond_low.astype(jnp.float32).T, precision=HIGH), "tp"
    )
    _, silu_back = jax.vjp(jax.nn.silu, cvec)
    d_cvec = silu_back(d_silu)[0]
    d_swish = lax.psum_scatter(
        jnp.dot(d_cvec, time_low.astype(jnp.float32), precision=HIGH),
        "fsdp",
        scatter_dimension=1,
        tiled=True,
    )
    _, act_back = jax.vjp(jax.nn.silu, act)
    d_act = act_back(d_swish)[0]
    d_patch = jnp.einsum("gsd,gsp->dp", d_h, noisy.astype(jnp.float32), precision=HIGH)
    d_small = lax.psum(
        lax.psum_scatter(
            jnp.concatenate([d_patch, d_head], 1), "fsdp", scatter_dimension=0, tiled=True
        ),
        "ctx",
    )
    lefts = {"freq": d_act, "time": d_cvec, "label": d_cvec, "cond": cond_in.astype(jnp.float32)}
    rights = {
        "freq": freqs.astype(jnp.float32),
        "time": swish.astype(jnp.float32),
        "label": onehot.astype(jnp.float32),
        "cond": d_cols,
    }

    split_sq = sum(jnp.sum(g * g) for parts in layer_shards for g in parts) + rank_square(
        lefts["cond"], rights["cond"]
    )
    copied_sq = jnp.sum(d_small * d_small) + sum(
        rank_square(lefts[k], rights[k]) for k in ("freq", "time", "label")
    )
    total_sq = lax.psum(split_sq + copied_sq / lax.axis_size("tp"), ("fsdp", "tp"))
    grad_norm = jnp.sqrt(total_sq)
    clip = jnp.minimum(1.0, CLIP / (grad_norm + 1e-06))
    grads_all = (
        jnp.stack([s[0] for s in layer_shards]),
        jnp.stack([s[1] for s in layer_shards]),
        jnp.stack([s[2] for s in layer_shards]),
        d_small[:, :patch_in],
        rank_sum(lefts["freq"], rights["freq"]),
        rank_sum(lefts["time"], rights["time"]),
        rank_sum(lefts["label"], rights["label"]),
        rank_sum(lefts["cond"], rights["cond"]),
        d_small[:, patch_in:],
    )
    olds = (
        (attend_weight, attend_mean, attend_square),
        (hidden_weight, hidden_mean, hidden_square),
        (output_weight, output_mean, output_square),
        (patch_weight, patch_mean, patch_square),
        (freq_weight, freq_mean, freq_square),
        (time_weight, time_mean, time_square),
        (label_table, label_mean, label_square),
        (cond_weight, cond_mean, cond_square),
        (head_weight, head_mean, head_square),
    )
    updated = []
    for trio, grad in zip(olds, grads_all):
        updated.extend(adamw(trio[0], trio[1], trio[2], grad * clip))
    return (loss, grad_norm, *updated)


def solution(mesh):
    image = P("fsdp", "ctx", None)
    layer = P(None, "fsdp", None, "tp")
    rows = P("fsdp", None)
    cond = P("fsdp", "tp")
    weights = (layer,) * 9 + (rows,) * 12 + (cond,) * 3 + (rows,) * 3
    return jax.shard_map(
        functools.partial(per_device, mesh),
        mesh=mesh,
        in_specs=(image, image, image, P("fsdp"), P("fsdp")) + weights,
        out_specs=(P(), P()) + weights,
        check_vma=False,
    )
```

```python
import functools
import math

import jax
import jax.numpy as jnp
from jax import lax
from jax.experimental import pallas as pl
from jax.experimental.pallas import tpu as pltpu
from jax.sharding import PartitionSpec as P

HEAD_DIM = 64
FREQ = 256
GRID = 16
STEP = 5


HIGH = lax.Precision.HIGHEST
RATE = 0.05
DECAY = 0.1
BETA = 0.5
EPSILON = 1e-08
CLIP = 1.0
LOW = jnp.bfloat16


def modln(h, shift, scale):
    mean = jnp.mean(h, -1, keepdims=True)
    cent = h - mean
    var = jnp.mean(cent * cent, -1, keepdims=True)
    return cent * lax.rsqrt(var + 1e-06) * (1.0 + scale) + shift


def gelu_tanh(v):
    return jax.nn.gelu(v, approximate=True)


def noise_level(steps):
    phase = (steps.astype(jnp.float32) / 1000.0 + 0.008) / 1.008 * (0.5 * math.pi)
    return jnp.cos(phase) ** 2


def time_freqs(steps):
    half = FREQ // 2
    rates = jnp.exp(-math.log(10000.0) * jnp.arange(half, dtype=jnp.float32) / half)
    angles = steps.astype(jnp.float32)[:, None] * rates[None, :]
    return jnp.concatenate([jnp.cos(angles), jnp.sin(angles)], -1)


def positions(first, count, width):
    index = first + jnp.arange(count, dtype=jnp.int32)
    row = (index // GRID).astype(jnp.float32)
    column = (index % GRID).astype(jnp.float32)
    quarter = width // 4
    rates = jnp.power(10000.0, -jnp.arange(quarter, dtype=jnp.float32) / quarter)
    across = column[:, None] * rates[None, :]
    down = row[:, None] * rates[None, :]
    return jnp.concatenate([jnp.sin(across), jnp.cos(across), jnp.sin(down), jnp.cos(down)], -1)


def adamw(weight, mean, square, grad):
    mean_next = BETA * mean + (1.0 - BETA) * grad
    square_next = BETA * square + (1.0 - BETA) * grad * grad
    fixed_mean = mean_next / (1.0 - BETA**STEP)
    fixed_square = square_next / (1.0 - BETA**STEP)
    weight_next = weight - RATE * (fixed_mean / (jnp.sqrt(fixed_square) + EPSILON) + DECAY * weight)
    return [weight_next, mean_next, square_next]


def rank_sum(left, right):
    total = left[0][:, None] * right[0][None, :]
    for k in range(1, left.shape[0]):
        total = total + left[k][:, None] * right[k][None, :]
    return total


def rank_square(left, right):
    one = jnp.einsum("nd,md->nm", left, left, precision=HIGH)
    two = jnp.einsum("nd,md->nm", right, right, precision=HIGH)
    return jnp.sum(one * two)


MESH = pl.DeviceIdType.MESH


def dot(left, right):
    return jnp.dot(left, right, preferred_element_type=jnp.float32)


def dot_nt(left, right):
    return lax.dot_general(left, right, (((1,), (1,)), ((), ())), preferred_element_type=jnp.float32)


def dot_tn(left, right):
    return lax.dot_general(left, right, (((0,), (0,)), ((), ())), preferred_element_type=jnp.float32)


def remote(src, dst, sems, where, **device):
    send, recv = (sems.at[(0, *where)], sems.at[(1, *where)])
    return pltpu.make_async_remote_copy(
        src_ref=src, dst_ref=dst, send_sem=send, recv_sem=recv, device_id=device, device_id_type=MESH
    )


def meet(sizes):
    barrier = pltpu.get_barrier_semaphore()
    count = 0
    for axis, size in sizes.items():
        for step in range(1, size):
            peer = lax.rem(lax.axis_index(axis) + step, size)
            pl.semaphore_signal(barrier, inc=1, device_id={axis: peer}, device_id_type=MESH)
            count += 1
    pl.semaphore_wait(barrier, count)


def norm_parts(h):
    mean = jnp.mean(h, -1, keepdims=True)
    cent = h - mean
    var = jnp.mean(cent * cent, -1, keepdims=True)
    inv = lax.rsqrt(var + 1e-06)
    return cent * inv, inv


def norm_back(grad, normed, inv, scale):
    grad_shift = jnp.sum(grad, 1)
    grad_scale = jnp.sum(grad * normed, 1)
    inner = grad * (1.0 + scale)
    mean = jnp.mean(inner, -1, keepdims=True)
    along = jnp.mean(inner * normed, -1, keepdims=True)
    return inv * (inner - mean - normed * along), grad_shift, grad_scale


def tp_send(part, size, send, first, sems):
    me = lax.axis_index("tp")
    send[...] = part.astype(LOW).reshape(send.shape)
    for step in range(1, size):
        peer = lax.rem(me + step, size)
        remote(send.at[peer], first.at[step - 1], sems, (0, step - 1), tp=peer).start()


def tp_finish(size, send, first, full, sems):
    me = lax.axis_index("tp")
    total = send[me].astype(jnp.float32)
    for step in range(1, size):
        peer = lax.rem(me + step, size)
        remote(send.at[peer], first.at[step - 1], sems, (0, step - 1), tp=peer).wait()
        total = total + first[step - 1].astype(jnp.float32)
    full[me] = total.astype(LOW)
    for step in range(1, size):
        peer = lax.rem(me + step, size)
        remote(full.at[me], full.at[me], sems, (1, step - 1), tp=peer).start()
    for step in range(1, size):
        peer = lax.rem(me + step, size)
        source = lax.rem(me + size - step, size)
        remote(full.at[me], full.at[me], sems, (1, step - 1), tp=peer).wait_send()
        remote(full.at[source], full.at[source], sems, (1, step - 1), tp=peer).wait_recv()


def spread(block, heads):
    lane = lax.broadcasted_iota(jnp.int32, block.shape, 1) // HEAD_DIM
    zero = jnp.zeros_like(block)
    return jnp.concatenate([jnp.where(lane == k, block, zero) for k in range(heads)], 0)


def pick(stacked, heads):
    rows = stacked.shape[0] // heads
    lane = lax.broadcasted_iota(jnp.int32, (rows, stacked.shape[1]), 1) // HEAD_DIM
    total = jnp.zeros((rows, stacked.shape[1]), stacked.dtype)
    for k in range(heads):
        total = jnp.where(lane == k, stacked[k * rows : (k + 1) * rows], total)
    return total


ROOT_2_PI = math.sqrt(2.0 / math.pi)


def gelu_parts(v):
    inside = jnp.tanh(ROOT_2_PI * (v + 0.044715 * (v * v * v)))
    value = v * (0.5 * (1.0 + inside))
    slope = 0.5 * (1.0 + inside) + 0.5 * v * (1.0 - inside * inside) * ROOT_2_PI * (
        1.0 + 3 * 0.044715 * v * v
    )
    return value, slope


def forward_kernel(
    sizes, h0_ref, mods_ref, low_ref, h_out, full_ref,
    keep_h, keep_mid, keep_a, keep_m, keep_q, keep_kv, keep_p, keep_att, keep_pre,
    weights, kv, h_ref, send_a, first_a, full_a, send_m, first_m, full_m,
    x_sems, pair_sems, own_sems, kv_sems, a_sems, m_sems,
):
    nf, nc, nt = sizes["fsdp"], sizes["ctx"], sizes["tp"]
    layer, layers = pl.program_id(0), pl.num_programs(0)
    total_layers = low_ref.shape[0]
    f, c = lax.axis_index("fsdp"), lax.axis_index("ctx")
    core = lax.rem(c, 2)
    sibling = c + 1 - 2 * core
    count, rows, width = h_ref.shape
    local = weights.shape[-1]
    heads = local // HEAD_DIM
    scale = 1.0 / math.sqrt(HEAD_DIM)

    def x_copy(k, step):
        peer = lax.rem(f + step, nf)
        return remote(
            low_ref.at[k, :, core], weights.at[k, :, f, core], x_sems, (k, step - 1), fsdp=peer
        )

    def x_arrived(k, step):
        source = lax.rem(f + nf - step, nf)
        block = weights.at[k, :, source, core]
        remote(block, block, x_sems, (k, step - 1), fsdp=source).wait_recv()

    def pair_copy(k, step, half):
        source = lax.rem(f + nf - step, nf)
        block = weights.at[k, :, source, half]
        return remote(block, block, pair_sems, (k, step - 1), ctx=sibling)

    def own_copy(k):
        return pltpu.make_async_copy(low_ref.at[k], weights.at[k, :, f], own_sems.at[0, k])

    def store_copy(k):
        return pltpu.make_async_copy(weights.at[k], full_ref.at[k], own_sems.at[1, k])

    def pass_on(k):
        for step in range(1, nf):
            x_arrived(k, step)
            pair_copy(k, step, core).start()

    @pl.when(layer == 0)
    def _():
        meet(sizes)
        for k in range(total_layers):
            for step in range(1, nf):
                x_copy(k, step).start()
            own_copy(k).start()
        h_ref[...] = h0_ref[...]
        pass_on(0)

    def mod(k):
        return mods_ref[6 * layer + k]

    own_copy(layer).wait()
    for step in range(1, nf):
        pair_copy(layer, step, 1 - core).wait_recv()
    store_copy(layer).start()

    def matrix(k):
        return weights[layer, k].reshape(width, local)

    h = h_ref[...]
    keep_h[0] = h
    normed, _ = norm_parts(h)
    u_in = (normed * (1.0 + mod(1)) + mod(0)).astype(LOW).reshape(count * rows, width)
    key = dot(u_in, matrix(1)).astype(LOW)
    kv[layer, c, :, :, :local] = key.reshape(count, rows, local)
    value = dot(u_in, matrix(2)).astype(LOW)
    kv[layer, c, :, :, local:] = value.reshape(count, rows, local)
    for step in range(1, nc):
        peer = lax.rem(c + step, nc)
        block = kv.at[layer, c]
        remote(block, block, kv_sems, (layer, step - 1), ctx=peer).start()
    query = dot(u_in, matrix(0)).astype(LOW)
    keep_q[0] = query.reshape(count, rows, local)
    for step in range(1, nc):
        peer = lax.rem(c + step, nc)
        source = lax.rem(c + nc - step, nc)
        remote(kv.at[layer, c], kv.at[layer, c], kv_sems, (layer, step - 1), ctx=peer).wait_send()
        block = kv.at[layer, source]
        remote(block, block, kv_sems, (layer, step - 1), ctx=peer).wait_recv()
    keep_kv[0] = kv[layer]
    for g in range(count):
        keys = kv[layer, :, g, :, :local].reshape(nc * rows, local)
        values = kv[layer, :, g, :, local:].reshape(nc * rows, local)
        stacked = spread(query[g * rows : (g + 1) * rows], heads)
        scores = dot_nt(stacked, keys) * scale
        expo = jnp.exp(scores - jnp.max(scores, -1, keepdims=True))
        probs = expo / jnp.sum(expo, -1, keepdims=True)
        keep_p[0, g] = probs
        keep_att[0, g * rows : (g + 1) * rows] = pick(dot(probs.astype(LOW), values), heads).astype(LOW)
    tp_send(dot_nt(keep_att[0], matrix(7)), nt, send_a, first_a, a_sems)
    tp_finish(nt, send_a, first_a, full_a, a_sems)
    branch = full_a[...].reshape(count, rows, width)
    keep_a[0] = branch
    h_mid = h_ref[...] + mod(2) * branch.astype(jnp.float32)
    keep_mid[0] = h_mid
    normed, _ = norm_parts(h_mid)
    w_in = (normed * (1.0 + mod(4)) + mod(3)).astype(LOW).reshape(count * rows, width)
    part = jnp.zeros((count * rows, width), jnp.float32)
    for k in range(4):
        pre = dot(w_in, matrix(3 + k))
        keep_pre[0, k] = pre
        part = part + dot_nt(gelu_parts(pre)[0].astype(LOW), matrix(8 + k))
    tp_send(part, nt, send_m, first_m, m_sems)

    @pl.when(layer + 1 < layers)
    def _():
        pass_on(layer + 1)

    tp_finish(nt, send_m, first_m, full_m, m_sems)
    branch = full_m[...].reshape(count, rows, width)
    keep_m[0] = branch
    h_ref[...] = keep_mid[0] + mod(5) * branch.astype(jnp.float32)

    @pl.when(layer == layers - 1)
    def _():
        h_out[...] = h_ref[...]
        for k in range(total_layers):
            store_copy(k).wait()
            for step in range(1, nf):
                x_copy(k, step).wait_send()
                pair_copy(k, step, core).wait_send()


def forward(mesh, h0, mods, low):
    sizes = dict(mesh.shape)
    nf, nc, nt = sizes["fsdp"], sizes["ctx"], sizes["tp"]
    count, rows, width = h0.shape
    layers, blocks, _, half, local = low.shape
    heads = local // HEAD_DIM
    tokens = count * rows
    f32 = jnp.float32

    def kept(shape, dtype):
        spec = pl.BlockSpec((1, *shape), lambda i: (i,) + (0,) * len(shape))
        return jax.ShapeDtypeStruct((layers, *shape), dtype), spec

    saves = [
        kept((count, rows, width), f32),
        kept((count, rows, width), f32),
        kept((count, rows, width), LOW),
        kept((count, rows, width), LOW),
        kept((count, rows, local), LOW),
        kept((nc, count, rows, 2 * local), LOW),
        kept((count, heads * rows, nc * rows), f32),
        kept((tokens, local), LOW),
        kept((4, tokens, local), f32),
    ]
    anywhere = pl.BlockSpec(memory_space=pl.ANY)
    vmem = pl.BlockSpec(memory_space=pltpu.VMEM)
    part = pltpu.VMEM((nt, tokens // nt, width), LOW)
    first = pltpu.VMEM((nt - 1, tokens // nt, width), LOW)
    dma = pltpu.SemaphoreType.DMA
    return pl.pallas_call(
        functools.partial(forward_kernel, sizes),
        grid=(layers,),
        out_shape=[
            jax.ShapeDtypeStruct(h0.shape, f32),
            jax.ShapeDtypeStruct((layers, blocks, nf, 2, half, local), LOW),
            *(shape for shape, _ in saves),
        ],
        in_specs=[vmem, vmem, anywhere],
        out_specs=[vmem, anywhere, *(spec for _, spec in saves)],
        scratch_shapes=[
            pltpu.VMEM((layers, blocks, nf, 2, half, local), LOW),
            pltpu.VMEM((layers, nc, count, rows, 2 * local), LOW),
            pltpu.VMEM((count, rows, width), f32),
            part, first, part, part, first, part,
            dma((2, layers, max(nf - 1, 1))),
            dma((2, layers, max(nf - 1, 1))),
            dma((2, layers)),
            dma((2, layers, nc - 1)),
            dma((2, 2, nt - 1)),
            dma((2, 2, nt - 1)),
        ],
        compiler_params=pltpu.CompilerParams(
            collective_id=1, has_side_effects=True, vmem_limit_bytes=56 * 2**20
        ),
        cost_estimate=pl.CostEstimate(
            flops=2 * tokens * width * blocks * local * layers,
            bytes_accessed=layers * blocks * width * local * 4,
            transcendentals=0,
        ),
        name="forward_layers",
    )(h0, mods, low)


CHUNKS = 4


def backward_kernel(
    sizes, dh0_ref, mods_ref, w_ref, keep_h, keep_mid, keep_a, keep_m, keep_q, keep_kv, keep_p, keep_att, keep_pre,
    dh_out, dmods_ref, grads_ref, square_ref,
    dh_ref, dmid_ref, act_ref, dpre_ref, dba_ref, dqkv_ref,
    send_w, first_w, full_w, send_u, first_u, full_u, kv_send, kv_got,
    grads, pair_got, x_send, x_got, y_send, y_got, done,
    w_sems, u_sems, kv_sems, pair_sems, x_sems, y_sems, end_sems, own_sems,
):
    nf, nc, nt = sizes["fsdp"], sizes["ctx"], sizes["tp"]
    chips = nc // 2
    layers, blocks, _, half, local = grads_ref.shape
    each = blocks // CHUNKS
    step = pl.program_id(0)
    new = lax.rem(step, 2)
    old = 1 - new
    f, c = lax.axis_index("fsdp"), lax.axis_index("ctx")
    core = lax.rem(c, 2)
    sibling = c + 1 - 2 * core
    count, rows, width = dh_ref.shape
    tokens = count * rows
    heads = local // HEAD_DIM
    scale = 1.0 / math.sqrt(HEAD_DIM)
    piece = min(64, half)
    f32 = jnp.float32

    def chunk(q):
        return pl.ds(q * each, each)

    def pieces(body):
        def one(j, carry):
            b, r = j // (half // piece), lax.rem(j, half // piece)
            body(b, pl.ds(pl.multiple_of(r * piece, piece), piece))
            return carry

        return lambda q: lax.fori_loop(q * each * (half // piece), (q + 1) * each * (half // piece), one, 0)

    def each_chunk(body):
        def one(q, carry):
            body(q)
            return carry

        lax.fori_loop(0, CHUNKS, one, 0)

    def pair_copy(q):
        return remote(
            grads.at[old, chunk(q), :, 1 - core], pair_got.at[old, chunk(q)], pair_sems, (old, q), ctx=sibling
        )

    def x_copy(q, ahead):
        peer = lax.rem(f + ahead, nf)
        return remote(
            x_send.at[ahead - 1, chunk(q)], x_got.at[old, ahead - 1, chunk(q)], x_sems, (old, q, ahead - 1), fsdp=peer
        )

    def y_copy(q, ahead, parity):
        peer = lax.rem(c // 2 + ahead, chips) * 2 + core
        return remote(
            y_send.at[chunk(q)], y_got.at[parity, ahead - 1, chunk(q)], y_sems, (parity, q, ahead - 1), ctx=peer
        )

    def end_copy(q, layer, parity, to):
        return remote(
            done.at[chunk(q)], grads_ref.at[layer, chunk(q), to], end_sems, (parity, q), ctx=sibling
        )

    def own_copy(q, layer):
        return pltpu.make_async_copy(done.at[chunk(q)], grads_ref.at[layer, chunk(q), core], own_sems.at[q])

    def start_pair():
        each_chunk(lambda q: pair_copy(q).start())

    def start_x():
        def one(q):
            pair_copy(q).wait()
            for ahead in range(1, nf):
                peer = lax.rem(f + ahead, nf)

                def add(b, r):
                    total = grads[old, b, peer, core, r].astype(f32) + pair_got[old, b, peer, r].astype(f32)
                    x_send[ahead - 1, b, r] = total.astype(LOW)

                pieces(add)(q)
                x_copy(q, ahead).start()

        each_chunk(one)

    def start_y():
        def one(q):
            for ahead in range(1, nf):
                x_copy(q, ahead).wait()

            def add(b, r):
                total = grads[old, b, f, core, r].astype(f32) + pair_got[old, b, f, r].astype(f32)
                for ahead in range(1, nf):
                    total = total + x_got[old, ahead - 1, b, r].astype(f32)
                y_send[b, r] = total.astype(LOW)

            pieces(add)(q)
            for ahead in range(1, chips):
                y_copy(q, ahead, old).start()

        each_chunk(one)

    def wait_end(layer, parity):
        def one(q):
            own_copy(q, layer).wait()
            end_copy(q, layer, parity, core).wait_send()
            end_copy(q, layer, parity, 1 - core).wait_recv()

        each_chunk(one)

    def start_end():
        layer = layers + 1 - step

        @pl.when(step >= 3)
        def _():
            wait_end(layer + 1, old)

        def one(q):
            for ahead in range(1, chips):
                y_copy(q, ahead, new).wait()

            def add(b, r):
                total = y_send[b, r].astype(f32)
                for ahead in range(1, chips):
                    total = total + y_got[new, ahead - 1, b, r].astype(f32)
                low = total.astype(LOW)
                done[b, r] = low
                total = low.astype(f32)
                square_ref[...] += jnp.sum((total * total).reshape(piece // 8, 8, local), 0)

            pieces(add)(q)
            own_copy(q, layer).start()
            end_copy(q, layer, new, core).start()

        each_chunk(one)

    def matrix(k):
        return w_ref[0, k].reshape(width, local)

    def mod(k):
        return mods_ref[6 * (layers - 1 - step) + k]

    def keep_grad(k, value):
        grads[new, k] = value.astype(LOW).reshape(nf, 2, half, local)

    @pl.when(step == 0)
    def _():
        meet(sizes)
        dh_ref[...] = dh0_ref[...]
        square_ref[...] = jnp.zeros_like(square_ref)

    @pl.when((step >= 1) & (step <= layers))
    def _():
        start_pair()

    @pl.when(step < layers)
    def _():
        grad = dh_ref[...]
        dmods_ref[0, 5] = jnp.sum(grad * keep_m[0].astype(f32), 1)
        branch = (mod(5) * grad).astype(LOW).reshape(tokens, width)
        part = jnp.zeros((tokens, width), f32)
        for k in range(4):
            value, slope = gelu_parts(keep_pre[0, k])
            act_ref[k] = value.astype(LOW)
            d_pre = (dot(branch, matrix(8 + k)) * slope).astype(LOW)
            dpre_ref[k] = d_pre
            part = part + dot_nt(d_pre, matrix(3 + k))
        tp_send(part, nt, send_w, first_w, w_sems)
        for k in range(4):
            keep_grad(8 + k, dot_tn(branch, act_ref[k]))
        normed, _ = norm_parts(keep_mid[0])
        w_in = (normed * (1.0 + mod(4)) + mod(3)).astype(LOW).reshape(tokens, width)
        for k in range(4):
            keep_grad(3 + k, dot_tn(w_in, dpre_ref[k]))

    @pl.when((step >= 1) & (step <= layers))
    def _():
        start_x()

    @pl.when(step < layers)
    def _():
        tp_finish(nt, send_w, first_w, full_w, w_sems)
        normed, inv = norm_parts(keep_mid[0])
        d_mid, d_shift, d_scale = norm_back(
            full_w[...].reshape(count, rows, width).astype(f32), normed, inv, mod(4)
        )
        d_mid = d_mid + dh_ref[...]
        dmid_ref[...] = d_mid
        dmods_ref[0, 3] = d_shift
        dmods_ref[0, 4] = d_scale
        dmods_ref[0, 2] = jnp.sum(d_mid * keep_a[0].astype(f32), 1)
        branch = (mod(2) * d_mid).astype(LOW).reshape(tokens, width)
        dba_ref[...] = branch
        d_att = dot(branch, matrix(7)).astype(LOW)
        for g in range(count):
            keys = keep_kv[0, :, g, :, :local].reshape(nc * rows, local)
            values = keep_kv[0, :, g, :, local:].reshape(nc * rows, local)
            grad = spread(d_att[g * rows : (g + 1) * rows], heads)
            query = spread(keep_q[0, g], heads)
            probs = keep_p[0, g]
            d_probs = dot_nt(grad, values)
            d_scores = (probs * (d_probs - jnp.sum(d_probs * probs, -1, keepdims=True))).astype(LOW)
            d_values = dot_tn(probs.astype(LOW), grad)
            d_keys = dot_tn(d_scores, query) * scale
            kv_send[:, g, :, :local] = d_keys.astype(LOW).reshape(nc, rows, local)
            kv_send[:, g, :, local:] = d_values.astype(LOW).reshape(nc, rows, local)
            d_query = pick(dot(d_scores, keys), heads) * scale
            dqkv_ref[0, g * rows : (g + 1) * rows] = d_query.astype(LOW)
        for ahead in range(1, nc):
            peer = lax.rem(c + ahead, nc)
            remote(kv_send.at[peer], kv_got.at[new, ahead - 1], kv_sems, (new, ahead - 1), ctx=peer).start()
        keep_grad(7, dot_tn(dba_ref[...], keep_att[0]))
        both = kv_send[c].astype(f32)
        for ahead in range(1, nc):
            peer = lax.rem(c + ahead, nc)
            remote(kv_send.at[peer], kv_got.at[new, ahead - 1], kv_sems, (new, ahead - 1), ctx=peer).wait()
            both = both + kv_got[new, ahead - 1].astype(f32)
        both = both.reshape(tokens, 2 * local).astype(LOW)
        dqkv_ref[1] = both[:, :local]
        dqkv_ref[2] = both[:, local:]
        part = dot_nt(dqkv_ref[0], matrix(0))
        part = part + dot_nt(dqkv_ref[1], matrix(1))
        part = part + dot_nt(dqkv_ref[2], matrix(2))
        tp_send(part, nt, send_u, first_u, u_sems)
        normed, _ = norm_parts(keep_h[0])
        u_in = (normed * (1.0 + mod(1)) + mod(0)).astype(LOW).reshape(tokens, width)
        for k in range(3):
            keep_grad(k, dot_tn(u_in, dqkv_ref[k]))

    @pl.when(step >= 2)
    def _():
        start_end()

    @pl.when(step < layers)
    def _():
        tp_finish(nt, send_u, first_u, full_u, u_sems)
        normed, inv = norm_parts(keep_h[0])
        d_h, d_shift, d_scale = norm_back(
            full_u[...].reshape(count, rows, width).astype(f32), normed, inv, mod(1)
        )
        dmods_ref[0, 0] = d_shift
        dmods_ref[0, 1] = d_scale
        dh_ref[...] = d_h + dmid_ref[...]

    @pl.when(step == layers - 1)
    def _():
        dh_out[...] = dh_ref[...]

    @pl.when((step >= 1) & (step <= layers))
    def _():
        start_y()

    @pl.when(step == layers + 1)
    def _():
        wait_end(0, new)


def backward(mesh, dh0, mods, full, saved):
    sizes = dict(mesh.shape)
    nf, nc, nt = sizes["fsdp"], sizes["ctx"], sizes["tp"]
    chips = nc // 2
    count, rows, width = dh0.shape
    layers, blocks, _, _, half, local = full.shape
    tokens = count * rows
    f32 = jnp.float32

    def per_layer(array):
        shape = array.shape[1:]
        return pl.BlockSpec(
            (1, *shape), lambda i: (jnp.maximum(layers - 1 - i, 0),) + (0,) * len(shape)
        )

    anywhere = pl.BlockSpec(memory_space=pl.ANY)
    vmem = pl.BlockSpec(memory_space=pltpu.VMEM)
    part = pltpu.VMEM((nt, tokens // nt, width), LOW)
    first = pltpu.VMEM((nt - 1, tokens // nt, width), LOW)
    dma = pltpu.SemaphoreType.DMA
    dmods = jax.ShapeDtypeStruct((layers, 6, count, width), f32)
    return pl.pallas_call(
        functools.partial(backward_kernel, sizes),
        grid=(layers + 2,),
        out_shape=[
            jax.ShapeDtypeStruct(dh0.shape, f32),
            dmods,
            jax.ShapeDtypeStruct((layers, blocks, 2, half, local), LOW),
            jax.ShapeDtypeStruct((8, local), f32),
        ],
        in_specs=[vmem, vmem, per_layer(full), *(per_layer(s) for s in saved)],
        out_specs=[vmem, per_layer(dmods), anywhere, vmem],
        scratch_shapes=[
            pltpu.VMEM((count, rows, width), f32),
            pltpu.VMEM((count, rows, width), f32),
            pltpu.VMEM((4, tokens, local), LOW),
            pltpu.VMEM((4, tokens, local), LOW),
            pltpu.VMEM((tokens, width), LOW),
            pltpu.VMEM((3, tokens, local), LOW),
            part, first, part, part, first, part,
            pltpu.VMEM((nc, count, rows, 2 * local), LOW),
            pltpu.VMEM((2, nc - 1, count, rows, 2 * local), LOW),
            pltpu.VMEM((2, blocks, nf, 2, half, local), LOW),
            pltpu.VMEM((2, blocks, nf, half, local), LOW),
            pltpu.VMEM((max(nf - 1, 1), blocks, half, local), LOW),
            pltpu.VMEM((2, max(nf - 1, 1), blocks, half, local), LOW),
            pltpu.VMEM((blocks, half, local), LOW),
            pltpu.VMEM((2, max(chips - 1, 1), blocks, half, local), LOW),
            pltpu.VMEM((blocks, half, local), LOW),
            dma((2, 2, nt - 1)),
            dma((2, 2, nt - 1)),
            dma((2, 2, nc - 1)),
            dma((2, 2, CHUNKS)),
            dma((2, 2, CHUNKS, max(nf - 1, 1))),
            dma((2, 2, CHUNKS, max(chips - 1, 1))),
            dma((2, 2, CHUNKS)),
            dma((CHUNKS,)),
        ],
        compiler_params=pltpu.CompilerParams(
            collective_id=2, has_side_effects=True, vmem_limit_bytes=60 * 2**20
        ),
        cost_estimate=pl.CostEstimate(
            flops=4 * tokens * width * blocks * local * layers,
            bytes_accessed=layers * blocks * width * local * 4,
            transcendentals=0,
        ),
        name="backward_layers",
    )(dh0, mods, full, *saved)


def per_device(
    mesh,
    latents,
    noise,
    var_target,
    timesteps,
    labels,
    attend_weight,
    attend_mean,
    attend_square,
    hidden_weight,
    hidden_mean,
    hidden_square,
    output_weight,
    output_mean,
    output_square,
    patch_weight,
    patch_mean,
    patch_square,
    freq_weight,
    freq_mean,
    freq_square,
    time_weight,
    time_mean,
    time_square,
    label_table,
    label_mean,
    label_square,
    cond_weight,
    cond_mean,
    cond_square,
    head_weight,
    head_mean,
    head_square,
):
    count, rows, patch_in = latents.shape
    layers, shard = attend_weight.shape[:2]
    columns = cond_weight.shape[1]

    steps_all = lax.all_gather(timesteps, "fsdp", axis=0, tiled=True)
    labels_all = lax.all_gather(labels, "fsdp", axis=0, tiled=True)
    freqs = time_freqs(steps_all).astype(LOW)
    act = jnp.dot(freqs, freq_weight.astype(LOW).T, preferred_element_type=jnp.float32)
    swish = lax.all_gather(jax.nn.silu(act).astype(LOW), "fsdp", axis=1, tiled=True)
    time_low = time_weight.astype(LOW)
    temb = jnp.dot(swish, time_low.T, preferred_element_type=jnp.float32)
    onehot = (labels_all[:, None] == jnp.arange(label_table.shape[1], dtype=jnp.int32)[None]).astype(
        LOW
    )
    cvec = temb + jnp.dot(onehot, label_table.astype(LOW).T, preferred_element_type=jnp.float32)
    cond_in = jax.nn.silu(cvec).astype(LOW)
    cond_low = cond_weight.astype(LOW)
    mods = lax.psum_scatter(
        jnp.dot(cond_in, cond_low, preferred_element_type=jnp.float32),
        "fsdp",
        scatter_dimension=0,
        tiled=True,
    )
    patch_head = lax.all_gather(
        jnp.concatenate([patch_weight, head_weight], 1).astype(LOW), "fsdp", axis=0, tiled=True
    )
    patch_full, head_full = patch_head[:, :patch_in], patch_head[:, patch_in:]
    width = patch_full.shape[0]
    mods = lax.all_gather(mods, "tp", axis=1, tiled=True).reshape(count, -1, width)

    level = noise_level(timesteps)[:, None, None]
    noisy = (jnp.sqrt(level) * latents + jnp.sqrt(1.0 - level) * noise).astype(LOW)
    first = lax.axis_index("ctx") * rows
    h = (
        jnp.einsum("gsp,dp->gsd", noisy, patch_full, preferred_element_type=jnp.float32)
        + positions(first, rows, width)[None]
    )
    low = jnp.concatenate(
        [jnp.swapaxes(w, 1, 2).astype(LOW) for w in (attend_weight, hidden_weight, output_weight)], 1
    ).reshape(layers, -1, 2, shard // 2, attend_weight.shape[3])
    spread_mods = jnp.swapaxes(mods, 0, 1)[:, :, None]
    h, full, *saved = forward(mesh, h, spread_mods, low)
    final_in = modln(h, mods[:, 6 * layers, None], mods[:, 6 * layers + 1, None]).astype(LOW)
    pred = jnp.einsum("gsd,dp->gsp", final_in, head_full, preferred_element_type=jnp.float32)
    diff = pred - jnp.concatenate([noise, var_target], -1)
    loss = lax.psum(jnp.sum(diff * diff), ("fsdp", "ctx"))
    d_pred = (2.0 * diff).astype(LOW)
    d_head = jnp.einsum("gsd,gsp->dp", final_in, d_pred, preferred_element_type=jnp.float32)
    d_final = jnp.einsum("gsp,dp->gsd", d_pred, head_full, preferred_element_type=jnp.float32)
    _, norm_back = jax.vjp(modln, h, mods[:, 6 * layers, None], mods[:, 6 * layers + 1, None])
    d_h, d_shift_f, d_scale_f = norm_back(d_final)
    d_h, layer_mods, grads, squares = backward(mesh, d_h, spread_mods, full, saved)
    layer_mods = jnp.moveaxis(layer_mods, 2, 0).reshape(count, 6 * layers, width)
    d_mods = jnp.concatenate([layer_mods, d_shift_f, d_scale_f], 1).reshape(count, -1)
    grads = jnp.swapaxes(
        grads.reshape(layers, low.shape[1], shard, -1).astype(jnp.float32), 1, 2
    )
    d_cols = lax.dynamic_slice_in_dim(d_mods, lax.axis_index("tp") * columns, columns, 1)
    d_cols = lax.all_gather(lax.psum(d_cols, "ctx"), "fsdp", axis=0, tiled=True)
    d_silu = lax.psum(
        jnp.dot(d_cols, cond_low.astype(jnp.float32).T, precision=HIGH), "tp"
    )
    _, silu_back = jax.vjp(jax.nn.silu, cvec)
    d_cvec = silu_back(d_silu)[0]
    d_swish = lax.psum_scatter(
        jnp.dot(d_cvec, time_low.astype(jnp.float32), precision=HIGH),
        "fsdp",
        scatter_dimension=1,
        tiled=True,
    )
    _, act_back = jax.vjp(jax.nn.silu, act)
    d_act = act_back(d_swish)[0]
    d_patch = jnp.einsum("gsd,gsp->dp", d_h, noisy.astype(jnp.float32), precision=HIGH)
    d_small = lax.psum(
        lax.psum_scatter(
            jnp.concatenate([d_patch, d_head], 1), "fsdp", scatter_dimension=0, tiled=True
        ),
        "ctx",
    )
    lefts = {"freq": d_act, "time": d_cvec, "label": d_cvec, "cond": cond_in.astype(jnp.float32)}
    rights = {
        "freq": freqs.astype(jnp.float32),
        "time": swish.astype(jnp.float32),
        "label": onehot.astype(jnp.float32),
        "cond": d_cols,
    }

    chips = lax.axis_size("ctx") // 2
    split_sq = lax.psum(jnp.sum(squares), "ctx") / chips + rank_square(lefts["cond"], rights["cond"])
    copied_sq = jnp.sum(d_small * d_small) + sum(
        rank_square(lefts[k], rights[k]) for k in ("freq", "time", "label")
    )
    total_sq = lax.psum(split_sq + copied_sq / lax.axis_size("tp"), ("fsdp", "tp"))
    grad_norm = jnp.sqrt(total_sq)
    clip = jnp.minimum(1.0, CLIP / (grad_norm + 1e-06))
    grads_all = (
        grads[:, :, 0:3],
        grads[:, :, 3:7],
        grads[:, :, 7:12],
        d_small[:, :patch_in],
        rank_sum(lefts["freq"], rights["freq"]),
        rank_sum(lefts["time"], rights["time"]),
        rank_sum(lefts["label"], rights["label"]),
        rank_sum(lefts["cond"], rights["cond"]),
        d_small[:, patch_in:],
    )
    olds = (
        (attend_weight, attend_mean, attend_square),
        (hidden_weight, hidden_mean, hidden_square),
        (output_weight, output_mean, output_square),
        (patch_weight, patch_mean, patch_square),
        (freq_weight, freq_mean, freq_square),
        (time_weight, time_mean, time_square),
        (label_table, label_mean, label_square),
        (cond_weight, cond_mean, cond_square),
        (head_weight, head_mean, head_square),
    )
    updated = []
    for trio, grad in zip(olds, grads_all):
        updated.extend(adamw(trio[0], trio[1], trio[2], grad * clip))
    return (loss, grad_norm, *updated)


def solution(mesh):
    image = P("fsdp", "ctx", None)
    layer = P(None, "fsdp", None, "tp")
    rows = P("fsdp", None)
    cond = P("fsdp", "tp")
    weights = (layer,) * 9 + (rows,) * 12 + (cond,) * 3 + (rows,) * 3
    return jax.shard_map(
        functools.partial(per_device, mesh),
        mesh=mesh,
        in_specs=(image, image, image, P("fsdp"), P("fsdp")) + weights,
        out_specs=(P(), P()) + weights,
        check_vma=False,
    )
```

```python
import functools
import math

import jax
import jax.numpy as jnp
from jax import lax
from jax.experimental import pallas as pl
from jax.experimental.pallas import tpu as pltpu
from jax.sharding import PartitionSpec as P

HEAD_DIM = 64
FREQ = 256
GRID = 16
STEP = 5


HIGH = lax.Precision.HIGHEST
RATE = 0.05
DECAY = 0.1
BETA = 0.5
EPSILON = 1e-08
CLIP = 1.0
LOW = jnp.bfloat16


def modln(h, shift, scale):
    mean = jnp.mean(h, -1, keepdims=True)
    cent = h - mean
    var = jnp.mean(cent * cent, -1, keepdims=True)
    return cent * lax.rsqrt(var + 1e-06) * (1.0 + scale) + shift


def gelu_tanh(v):
    return jax.nn.gelu(v, approximate=True)


def noise_level(steps):
    phase = (steps.astype(jnp.float32) / 1000.0 + 0.008) / 1.008 * (0.5 * math.pi)
    return jnp.cos(phase) ** 2


def time_freqs(steps):
    half = FREQ // 2
    rates = jnp.exp(-math.log(10000.0) * jnp.arange(half, dtype=jnp.float32) / half)
    angles = steps.astype(jnp.float32)[:, None] * rates[None, :]
    return jnp.concatenate([jnp.cos(angles), jnp.sin(angles)], -1)


def positions(first, count, width):
    index = first + jnp.arange(count, dtype=jnp.int32)
    row = (index // GRID).astype(jnp.float32)
    column = (index % GRID).astype(jnp.float32)
    quarter = width // 4
    rates = jnp.power(10000.0, -jnp.arange(quarter, dtype=jnp.float32) / quarter)
    across = column[:, None] * rates[None, :]
    down = row[:, None] * rates[None, :]
    return jnp.concatenate([jnp.sin(across), jnp.cos(across), jnp.sin(down), jnp.cos(down)], -1)


def adamw(weight, mean, square, grad):
    mean_next = BETA * mean + (1.0 - BETA) * grad
    square_next = BETA * square + (1.0 - BETA) * grad * grad
    fixed_mean = mean_next / (1.0 - BETA**STEP)
    fixed_square = square_next / (1.0 - BETA**STEP)
    weight_next = weight - RATE * (fixed_mean / (jnp.sqrt(fixed_square) + EPSILON) + DECAY * weight)
    return [weight_next, mean_next, square_next]


def rank_sum(left, right):
    total = left[0][:, None] * right[0][None, :]
    for k in range(1, left.shape[0]):
        total = total + left[k][:, None] * right[k][None, :]
    return total


MESH = pl.DeviceIdType.MESH
GROUPS = ((4, 4), (0, 4), (8, 4))
QUERY, KEY, VALUE, OUT, HIDDEN, MLP = 4, 5, 6, 7, 0, 8
LANES = 128


def dot(left, right):
    return jnp.dot(left, right, preferred_element_type=jnp.float32)


def dot_nt(left, right):
    return lax.dot_general(left, right, (((1,), (1,)), ((), ())), preferred_element_type=jnp.float32)


def dot_tn(left, right):
    return lax.dot_general(left, right, (((0,), (0,)), ((), ())), preferred_element_type=jnp.float32)


def remote(src, dst, sems, where, **device):
    send, recv = (sems.at[(0, *where)], sems.at[(1, *where)])
    return pltpu.make_async_remote_copy(
        src_ref=src, dst_ref=dst, send_sem=send, recv_sem=recv, device_id=device, device_id_type=MESH
    )


def meet(sizes):
    barrier = pltpu.get_barrier_semaphore()
    count = 0
    for axis, size in sizes.items():
        for step in range(1, size):
            peer = lax.rem(lax.axis_index(axis) + step, size)
            pl.semaphore_signal(barrier, inc=1, device_id={axis: peer}, device_id_type=MESH)
            count += 1
    pl.semaphore_wait(barrier, count)


def norm_parts(h):
    mean = jnp.mean(h, -1, keepdims=True)
    cent = h - mean
    var = jnp.mean(cent * cent, -1, keepdims=True)
    inv = lax.rsqrt(var + 1e-06)
    return cent * inv, inv


def norm_back(grad, normed, inv, scale):
    grad_shift = jnp.sum(grad, 0, keepdims=True)
    grad_scale = jnp.sum(grad * normed, 0, keepdims=True)
    inner = grad * (1.0 + scale)
    mean = jnp.mean(inner, -1, keepdims=True)
    along = jnp.mean(inner * normed, -1, keepdims=True)
    return inv * (inner - mean - normed * along), grad_shift, grad_scale


class Total:
    def __init__(self, size, g, send, first, full, sems):
        self.size, self.g, self.sems = size, g, sems
        self.send, self.first, self.full = send.at[g], first.at[g], full.at[g]
        self.me = lax.axis_index("tp")

    def peer(self, ahead):
        return lax.rem(self.me + ahead, self.size)

    def one(self, ahead):
        peer = self.peer(ahead)
        return remote(
            self.send.at[peer], self.first.at[ahead - 1], self.sems, (0, self.g, ahead - 1), tp=peer
        )

    def two(self, block, ahead):
        block = self.full.at[block]
        return remote(block, block, self.sems, (1, self.g, ahead - 1), tp=self.peer(ahead))

    def scatter(self, part):
        self.send[...] = part.astype(LOW).reshape(self.send.shape)
        for ahead in range(1, self.size):
            self.one(ahead).start()

    def share(self):
        total = self.send[self.me].astype(jnp.float32)
        for ahead in range(1, self.size):
            self.one(ahead).wait()
            total = total + self.first[ahead - 1].astype(jnp.float32)
        self.full[self.me] = total.astype(LOW)
        for ahead in range(1, self.size):
            self.two(self.me, ahead).start()

    def get(self):
        for ahead in range(1, self.size):
            self.two(self.me, ahead).wait_send()
            self.two(lax.rem(self.me + self.size - ahead, self.size), ahead).wait_recv()
        size, rows, width = self.full.shape
        return self.full[...].reshape(size * rows, width)


def spread(block, heads):
    lane = lax.broadcasted_iota(jnp.int32, block.shape, 1) // HEAD_DIM
    zero = jnp.zeros_like(block)
    return jnp.concatenate([jnp.where(lane == k, block, zero) for k in range(heads)], 0)


def pick(stacked, heads):
    rows = stacked.shape[0] // heads
    lane = lax.broadcasted_iota(jnp.int32, (rows, stacked.shape[1]), 1) // HEAD_DIM
    total = jnp.zeros((rows, stacked.shape[1]), stacked.dtype)
    for k in range(heads):
        total = jnp.where(lane == k, stacked[k * rows : (k + 1) * rows], total)
    return total


ROOT_2_PI = math.sqrt(2.0 / math.pi)


def gelu_parts(v):
    inside = jnp.tanh(ROOT_2_PI * (v + 0.044715 * (v * v * v)))
    value = v * (0.5 * (1.0 + inside))
    slope = 0.5 * (1.0 + inside) + 0.5 * v * (1.0 - inside * inside) * ROOT_2_PI * (
        1.0 + 3 * 0.044715 * v * v
    )
    return value, slope


def row(ref, g, index, width):
    return ref[g : g + 1, pl.ds(pl.multiple_of(index * width, LANES), width)]


def put_row(ref, g, index, width, value):
    ref[g : g + 1, pl.ds(pl.multiple_of(index * width, LANES), width)] = value


def interleave(blocks, tiles, back=False):
    size = blocks * tiles * 16
    to = lax.broadcasted_iota(jnp.int32, (size, size), 1 if back else 0)
    source = lax.broadcasted_iota(jnp.int32, (size, size), 0 if back else 1)
    block, tile, at = to % blocks, (to // blocks) % tiles, to // (blocks * tiles)
    return jnp.where(source == (block * tiles + tile) * 16 + at, 1.0, 0.0).astype(LOW)


def forward_kernel(
    sizes, h0_ref, part_ref, hidden_ref, attend_ref, output_ref, h_out, mods_out, full_ref,
    keep_h, keep_mid, keep_a, keep_m, keep_q, keep_kv, keep_p, keep_att, keep_pre,
    weights, stage_h, stage_a, stage_o, kv, h_ref, q_ref, mods_ref, mods_got, send_a, first_a, full_a, send_m, first_m, full_m,
    x_sems, y_sems, pair_sems, own_sems, kv_sems, a_sems, m_sems, mods_x_sems, mods_t_sems,
):
    nf, nc, nt = sizes["fsdp"], sizes["ctx"], sizes["tp"]
    chips = nc // 2
    step = pl.program_id(0)
    layers = attend_ref.shape[0]
    f, c, t = lax.axis_index("fsdp"), lax.axis_index("ctx"), lax.axis_index("tp")
    core, chip = lax.rem(c, 2), c // 2
    sibling = c + 1 - 2 * core
    count, rows, width = h_ref.shape
    local = weights.shape[-1]
    heads = local // HEAD_DIM
    scale = 1.0 / math.sqrt(HEAD_DIM)
    columns = part_ref.shape[-1]

    def blocks(k):
        return pl.ds(*GROUPS[k])

    def x_copy(layer, k, ahead):
        return remote(
            weights.at[layer, blocks(k), f, chip, core],
            weights.at[layer, blocks(k), f, chip, core],
            x_sems,
            (layer, k, ahead - 1),
            fsdp=lax.rem(f + ahead, nf),
        )

    def x_arrived(layer, k, ahead):
        source = lax.rem(f + nf - ahead, nf)
        block = weights.at[layer, blocks(k), source, chip, core]
        remote(block, block, x_sems, (layer, k, ahead - 1), fsdp=source).wait_recv()

    def y_copy(layer, k, ahead, over, at):
        source = lax.rem(f + nf - ahead, nf)
        block = weights.at[layer, blocks(k), source, at, core]
        peer = lax.rem(chip + over, chips) * 2 + core
        return remote(block, block, y_sems, (layer, k, ahead - 1, over - 1), ctx=peer)

    def pair_copy(layer, k, ahead, half):
        source = lax.rem(f + nf - ahead, nf)
        block = weights.at[layer, blocks(k), source, :, half]
        return remote(block, block, pair_sems, (layer, k, ahead - 1), ctx=sibling)

    def pass_y(layer, k):
        for ahead in range(1, nf):
            x_arrived(layer, k, ahead)
            for over in range(1, chips):
                y_copy(layer, k, ahead, over, chip).start()

    def pass_pair(layer, k):
        for ahead in range(1, nf):
            for over in range(1, chips):
                y_copy(layer, k, ahead, over, lax.rem(chip + chips - over, chips)).wait_recv()
            pair_copy(layer, k, ahead, core).start()

    def arrived(layer, k):
        for ahead in range(1, nf):
            pair_copy(layer, k, ahead, 1 - core).wait_recv()

    def stage_copies(layer):
        return [
            pltpu.make_async_copy(source.at[layer], stage, own_sems.at[1 + k])
            for k, (source, stage) in enumerate(
                ((attend_ref, stage_a), (hidden_ref, stage_h), (output_ref, stage_o))
            )
        ]

    def quarters(value):
        return value.astype(LOW).reshape(chips, 2, -1, local)

    def send_x(layer, k):
        for ahead in range(1, nf):
            x_copy(layer, k, ahead).start()

    def lower(layer):
        copies = stage_copies(layer)
        copies[0].wait()
        copies[2].wait()
        for k in range(3):
            weights[layer, QUERY + k, f] = quarters(stage_a[k])
        weights[layer, OUT, f] = quarters(stage_o[0])
        send_x(layer, 0)
        copies[1].wait()
        tiles = local // LANES
        size = 4 * tiles * 16
        order = interleave(4, tiles, back=True)
        quarter = weights.shape[-2]

        def split(r, carry):
            rows_in = pl.ds(pl.multiple_of(r * size, size), size)
            value = dot(order, stage_h[rows_in].astype(LOW)).astype(LOW)
            part = (r * 16) // quarter
            at = pl.ds(pl.multiple_of(lax.rem(r * 16, quarter), 16), 16)
            for k in range(4):
                for n in range(tiles):
                    first = (k * tiles + n) * 16
                    weights[
                        layer, HIDDEN + k, f, part // 2, lax.rem(part, 2), at, n * LANES : (n + 1) * LANES
                    ] = value[first : first + 16]
            return carry

        lax.fori_loop(0, stage_h.shape[0] // size, split, 0, unroll=2)
        send_x(layer, 1)
        for k in range(4):
            weights[layer, MLP + k, f] = quarters(stage_o[1 + k])
        send_x(layer, 2)

    def store_copy(layer):
        return pltpu.make_async_copy(weights.at[layer], full_ref.at[layer], own_sems.at[4 + layer])

    def share_mods():
        for ahead in range(1, nf):
            peer = lax.rem(f + ahead, nf)
            remote(part_ref.at[peer], mods_got.at[ahead - 1], mods_x_sems, (ahead - 1,), fsdp=peer).start()

    def finish_mods():
        total = part_ref[f]
        for ahead in range(1, nf):
            peer = lax.rem(f + ahead, nf)
            remote(part_ref.at[peer], mods_got.at[ahead - 1], mods_x_sems, (ahead - 1,), fsdp=peer).wait()
            total = total + mods_got[ahead - 1]

        def at(k):
            return mods_ref.at[:, pl.ds(pl.multiple_of(k * columns, LANES), columns)]

        mods_ref[:, pl.ds(pl.multiple_of(t * columns, LANES), columns)] = total
        for ahead in range(1, nt):
            remote(at(t), at(t), mods_t_sems, (ahead - 1,), tp=lax.rem(t + ahead, nt)).start()
        for ahead in range(1, nt):
            source = lax.rem(t + nt - ahead, nt)
            remote(at(t), at(t), mods_t_sems, (ahead - 1,), tp=source).wait_send()
            remote(at(source), at(source), mods_t_sems, (ahead - 1,), tp=source).wait_recv()

    def mod(k, g, layer):
        return row(mods_ref, g, 6 * layer + k, width)

    def total_a(g):
        return Total(nt, g, send_a, first_a, full_a, a_sems)

    def total_m(g):
        return Total(nt, g, send_m, first_m, full_m, m_sems)

    def kv_copy(layer, g, ahead, at):
        block = kv.at[layer, g, at]
        return remote(block, block, kv_sems, (layer, g, ahead - 1), ctx=lax.rem(c + ahead, nc))

    @pl.when(step == 0)
    def _():
        for copy in stage_copies(0):
            copy.start()
        meet(sizes)
        share_mods()
        lower(0)
        for copy in stage_copies(1):
            copy.start()
        h_ref[...] = h0_ref[...]
        finish_mods()
        pass_y(0, 0)
        pass_pair(0, 0)
        pass_y(0, 1)

    def matrix(k):
        return weights[step, k].reshape(width, local)

    def begin(g):
        h = h_ref[g]
        keep_h[0, g] = h
        normed, _ = norm_parts(h)
        u_in = (normed * (1.0 + mod(1, g, step)) + mod(0, g, step)).astype(LOW)
        kv[step, g, c, :, :local] = dot(u_in, matrix(KEY)).astype(LOW)
        kv[step, g, c, :, local:] = dot(u_in, matrix(VALUE)).astype(LOW)
        for ahead in range(1, nc):
            kv_copy(step, g, ahead, c).start()
        q_ref[g] = dot(u_in, matrix(QUERY)).astype(LOW)

    def last_branch(g):
        branch = total_m(g).get()
        keep_m[0, g] = branch
        h_ref[g] = h_ref[g] + mod(5, g, step - 1) * branch.astype(jnp.float32)

    @pl.when(step < layers)
    def _():
        arrived(step, 0)

    for g in range(count):

        @pl.when(step >= 1)
        def _():
            last_branch(g)

        @pl.when(step < layers)
        def _():
            begin(g)

    @pl.when(step + 1 < layers)
    def _():
        lower(step + 1)

    @pl.when(step + 2 < layers)
    def _():
        for copy in stage_copies(step + 2):
            copy.start()

    @pl.when(step < layers)
    def _():
        pass_y(step, 2)
        pass_pair(step, 1)
        for g in range(count):
            for ahead in range(1, nc):
                kv_copy(step, g, ahead, c).wait_send()
                kv_copy(step, g, ahead, lax.rem(c + nc - ahead, nc)).wait_recv()
            keep_q[0, g] = q_ref[g]
            keep_kv[0, g] = kv[step, g]
            keys = kv[step, g, :, :, :local].reshape(nc * rows, local)
            values = kv[step, g, :, :, local:].reshape(nc * rows, local)
            scores = dot_nt(spread(q_ref[g], heads), keys) * scale
            expo = jnp.exp(scores - jnp.max(scores, -1, keepdims=True))
            probs = expo / jnp.sum(expo, -1, keepdims=True)
            keep_p[0, g] = probs
            attended = pick(dot(probs.astype(LOW), values), heads).astype(LOW)
            keep_att[0, g] = attended
            total_a(g).scatter(dot_nt(attended, matrix(OUT)))
        pass_pair(step, 2)
        for g in range(count):
            total_a(g).share()
        arrived(step, 1)

    @pl.when(step + 1 < layers)
    def _():
        pass_y(step + 1, 0)

    @pl.when(step < layers)
    def _():
        for g in range(count):
            branch = total_a(g).get()
            keep_a[0, g] = branch
            h_mid = h_ref[g] + mod(2, g, step) * branch.astype(jnp.float32)
            keep_mid[0, g] = h_mid
            h_ref[g] = h_mid
            normed, _ = norm_parts(h_mid)
            w_in = (normed * (1.0 + mod(4, g, step)) + mod(3, g, step)).astype(LOW)
            if g == 0:
                arrived(step, 2)
                store_copy(step).start()
            part = jnp.zeros((rows, width), jnp.float32)
            for k in range(4):
                pre = dot(w_in, matrix(HIDDEN + k))
                keep_pre[0, g, k] = pre
                part = part + dot_nt(gelu_parts(pre)[0].astype(LOW), matrix(MLP + k))
            total_m(g).scatter(part)

    @pl.when(step + 1 < layers)
    def _():
        pass_pair(step + 1, 0)
        pass_y(step + 1, 1)

    @pl.when(step < layers)
    def _():
        for g in range(count):
            total_m(g).share()

    @pl.when(step == layers)
    def _():
        h_out[...] = h_ref[...]
        mods_out[...] = mods_ref[...]

        def drain(layer, carry):
            store_copy(layer).wait()
            for k in range(len(GROUPS)):
                for ahead in range(1, nf):
                    x_copy(layer, k, ahead).wait_send()
                    for over in range(1, chips):
                        y_copy(layer, k, ahead, over, chip).wait_send()
                    pair_copy(layer, k, ahead, core).wait_send()
            return carry

        lax.fori_loop(0, layers, drain, 0)


def forward(mesh, h0, part, hidden, attend, output):
    sizes = dict(mesh.shape)
    nf, nc, nt = sizes["fsdp"], sizes["ctx"], sizes["tp"]
    chips = nc // 2
    count, rows, width = h0.shape
    layers, _, shard, local = attend.shape
    blocks, quarter = 4 + attend.shape[1] + output.shape[1], shard // nc
    heads = local // HEAD_DIM
    tokens = count * rows
    others, overs = max(nf - 1, 1), max(chips - 1, 1)
    f32 = jnp.float32

    def kept(shape, dtype, late=0):
        spec = pl.BlockSpec(
            (1, *shape), lambda i: (jnp.clip(i - late, 0, layers - 1),) + (0,) * len(shape)
        )
        return jax.ShapeDtypeStruct((layers, *shape), dtype), spec

    saves = [
        kept((count, rows, width), f32),
        kept((count, rows, width), f32),
        kept((count, rows, width), LOW),
        kept((count, rows, width), LOW, 1),
        kept((count, rows, local), LOW),
        kept((count, nc, rows, 2 * local), LOW),
        kept((count, heads * rows, nc * rows), f32),
        kept((count, rows, local), LOW),
        kept((count, 4, rows, local), f32),
    ]
    anywhere = pl.BlockSpec(memory_space=pl.ANY)
    vmem = pl.BlockSpec(memory_space=pltpu.VMEM)
    whole = pltpu.VMEM((count, nt, rows // nt, width), LOW)
    first = pltpu.VMEM((count, nt - 1, rows // nt, width), LOW)
    dma = pltpu.SemaphoreType.DMA
    return pl.pallas_call(
        functools.partial(forward_kernel, sizes),
        grid=(layers + 1,),
        out_shape=[
            jax.ShapeDtypeStruct(h0.shape, f32),
            jax.ShapeDtypeStruct((count, nt * part.shape[-1]), f32),
            jax.ShapeDtypeStruct((layers, blocks, nf, chips, 2, quarter, local), LOW),
            *(shape for shape, _ in saves),
        ],
        in_specs=[vmem, vmem, anywhere, anywhere, anywhere],
        out_specs=[vmem, vmem, anywhere, *(spec for _, spec in saves)],
        scratch_shapes=[
            pltpu.VMEM((layers, blocks, nf, chips, 2, quarter, local), LOW),
            *(pltpu.VMEM(w.shape[1:], f32) for w in (hidden, attend, output)),
            pltpu.VMEM((layers, count, nc, rows, 2 * local), LOW),
            pltpu.VMEM((count, rows, width), f32),
            pltpu.VMEM((count, rows, local), LOW),
            pltpu.VMEM((count, nt * part.shape[-1]), f32),
            pltpu.VMEM((others, count, part.shape[-1]), f32),
            whole, first, whole, whole, first, whole,
            dma((2, layers, 3, others)),
            dma((2, layers, 3, others, overs)),
            dma((2, layers, 3, others)),
            dma((4 + layers,)),
            dma((2, layers, count, nc - 1)),
            dma((2, 2, count, nt - 1)),
            dma((2, 2, count, nt - 1)),
            dma((2, others)),
            dma((2, nt - 1)),
        ],
        compiler_params=pltpu.CompilerParams(
            collective_id=1, has_side_effects=True, vmem_limit_bytes=56 * 2**20
        ),
        cost_estimate=pl.CostEstimate(
            flops=2 * tokens * width * blocks * local * layers,
            bytes_accessed=layers * blocks * width * local * 4,
            transcendentals=0,
        ),
        name="forward_layers",
    )(h0, part, hidden, attend, output)


def halves(value):
    high = value.astype(LOW).astype(jnp.float32)
    return high, value - high


def backward_kernel(
    sizes, images, dh0_ref, mods_ref, dmods_end_ref, loss_ref, noisy_ref, dpred_ref, final_ref,
    slope_c_ref, slope_a_ref, gram_c_ref, gram_t_ref, gram_f_ref, time_ref, cond_ref,
    w_ref, keep_h, keep_mid, keep_a, keep_m, keep_q, keep_kv, keep_p, keep_att, keep_pre,
    grads_ref, small_ref, dcols_out, dcvec_ref, dact_ref, stat_ref,
    dh_ref, dmid_ref, h_ref, act_ref, dpre_ref, branch_ref, dba_ref, dqkv_ref, dm_ref,
    send_w, first_w, full_w, send_u, first_u, full_u, kv_send, kv_got,
    grads, pair_got, x_send, x_got, y_send, y_got, done, square,
    s_grads, s_pair, s_send, s_x, s_y_send, s_y, s_done,
    c_got, dcols_ref, cond_buf, product, gram, silu_got, swish_got, stat_got,
    w_sems, u_sems, kv_sems, pair_sems, x_sems, y_sems, end_sems, own_sems,
    s_sems, s_x_sems, s_y_sems, s_own_sems, c_sems, f_sems, cond_sems, t_sems, a_sems, n_sems,
):
    nf, nc, nt = sizes["fsdp"], sizes["ctx"], sizes["tp"]
    chips = nc // 2
    layers, _, _, half, local = grads_ref.shape
    step = pl.program_id(0)
    new = lax.rem(step, 2)
    old = 1 - new
    f, c, t = lax.axis_index("fsdp"), lax.axis_index("ctx"), lax.axis_index("tp")
    core, chip = lax.rem(c, 2), c // 2
    sibling = c + 1 - 2 * core
    count, rows, width = dh_ref.shape
    heads = local // HEAD_DIM
    scale = 1.0 / math.sqrt(HEAD_DIM)
    piece = min(64, half)
    columns = cond_ref.shape[1]
    f32 = jnp.float32
    A, H, M = 0, 1, 2
    layer = layers - 1 - step

    def blocks(k):
        return pl.ds(*GROUPS[k])

    def pieces(k, body):
        parts = half // piece

        def one(j, carry):
            body(j // parts, pl.ds(pl.multiple_of(lax.rem(j, parts) * piece, piece), piece))
            return carry

        low, size = GROUPS[k]
        lax.fori_loop(low * parts, (low + size) * parts, one, 0)

    def pair_copy(k, at):
        return remote(
            grads.at[blocks(k), :, 1 - core], pair_got.at[at, blocks(k)], pair_sems, (at, k), ctx=sibling
        )

    def x_copy(k, at, ahead):
        return remote(
            x_send.at[ahead - 1, blocks(k)], x_got.at[at, ahead - 1, blocks(k)],
            x_sems, (at, k, ahead - 1), fsdp=lax.rem(f + ahead, nf),
        )

    def y_copy(k, at, ahead):
        return remote(
            y_send.at[blocks(k)], y_got.at[at, ahead - 1, blocks(k)],
            y_sems, (at, k, ahead - 1), ctx=lax.rem(chip + ahead, chips) * 2 + core,
        )

    def end_copy(k, at, layer, to):
        return remote(done.at[blocks(k)], grads_ref.at[layer, blocks(k), to], end_sems, (at, k), ctx=sibling)

    def own_copy(k, layer):
        return pltpu.make_async_copy(done.at[blocks(k)], grads_ref.at[layer, blocks(k), core], own_sems.at[k])

    def stage_2(k, at):
        pair_copy(k, at).wait()
        for ahead in range(1, nf):
            peer = lax.rem(f + ahead, nf)

            def add(b, r):
                total = grads[b, peer, core, r].astype(f32) + pair_got[at, b, peer, r].astype(f32)
                x_send[ahead - 1, b, r] = total.astype(LOW)

            pieces(k, add)
            x_copy(k, at, ahead).start()

    def stage_3(k, at):
        for ahead in range(1, nf):
            x_copy(k, at, ahead).wait()

        def add(b, r):
            total = grads[b, f, core, r].astype(f32) + pair_got[at, b, f, r].astype(f32)
            for ahead in range(1, nf):
                total = total + x_got[at, ahead - 1, b, r].astype(f32)
            y_send[b, r] = total.astype(LOW)

        pieces(k, add)
        for ahead in range(1, chips):
            y_copy(k, at, ahead).start()

    def end_wait(k, at, layer):
        own_copy(k, layer).wait()
        end_copy(k, at, layer, core).wait_send()
        end_copy(k, at, layer, 1 - core).wait_recv()

    def stage_4(k, at, layer):
        for ahead in range(1, chips):
            y_copy(k, at, ahead).wait()

        def add(b, r):
            total = y_send[b, r].astype(f32)
            for ahead in range(1, chips):
                total = total + y_got[at, ahead - 1, b, r].astype(f32)
            low = total.astype(LOW)
            done[b, r] = low
            total = low.astype(f32)
            square[...] += jnp.sum((total * total).reshape(piece // 8, 8, local), 0)

        pieces(k, add)
        own_copy(k, layer).start()
        end_copy(k, at, layer, core).start()

    def when(low, high, body):
        pl.when((step >= low) & (step <= high))(body)

    def matrix(k):
        return w_ref[0, k].reshape(width, local)

    def mod(k, g, layer):
        return row(mods_ref, g, 6 * layer + k, width)

    def put_dmod(k, g, layer, value):
        put_row(dm_ref, g, 6 * layer + k, width, value)

    def keep_grad(k, value):
        grads[k] = value.astype(LOW).reshape(nf, 2, half, local)

    def total_w(g):
        return Total(nt, g, send_w, first_w, full_w, w_sems)

    def total_u(g):
        return Total(nt, g, send_u, first_u, full_u, u_sems)

    def both(ref):
        value = ref[...]
        return value.reshape(count * rows, value.shape[-1])

    @pl.when(step == 0)
    def _():
        meet(sizes)
        dh_ref[...] = dh0_ref[...]
        square[...] = jnp.zeros_like(square)
        for g in range(count):
            put_row(dm_ref, g, 3 * layers, 2 * width, dmods_end_ref[g : g + 1])

    def finish_input(g):
        normed, inv = norm_parts(h_ref[g])
        d_h, d_shift, d_scale = norm_back(
            total_u(g).get().astype(f32), normed, inv, mod(1, g, layer + 1)
        )
        put_dmod(0, g, layer + 1, d_shift)
        put_dmod(1, g, layer + 1, d_scale)
        dh_ref[g] = d_h + dmid_ref[g]

    def mlp_back(g):
        grad = dh_ref[g]
        put_dmod(5, g, layer, jnp.sum(grad * keep_m[0, g].astype(f32), 0, keepdims=True))
        branch = (mod(5, g, layer) * grad).astype(LOW)
        branch_ref[g] = branch
        part = jnp.zeros((rows, width), f32)
        for k in range(4):
            value, slope = gelu_parts(keep_pre[0, g, k])
            act_ref[k, g] = value.astype(LOW)
            d_pre = (dot(branch, matrix(MLP + k)) * slope).astype(LOW)
            dpre_ref[k, g] = d_pre
            part = part + dot_nt(d_pre, matrix(HIDDEN + k))
        total_w(g).scatter(part)

    for g in range(count):
        when(1, layers, lambda: finish_input(g))
        when(0, layers - 1, lambda: mlp_back(g))

    def share(own, slots, sems, axis, size, where=()):
        me = lax.axis_index(axis)
        for ahead in range(1, size):
            remote(own, slots.at[me], sems, (*where, ahead - 1), **{axis: lax.rem(me + ahead, size)}).start()

    def shared(own, slots, sems, axis, size, where=()):
        me = lax.axis_index(axis)
        for ahead in range(1, size):
            remote(own, slots.at[me], sems, (*where, ahead - 1), **{axis: lax.rem(me + ahead, size)}).wait_send()
            source = lax.rem(me + size - ahead, size)
            remote(slots.at[source], slots.at[source], sems, (*where, ahead - 1), **{axis: source}).wait_recv()

    def slot_sum(slots, size):
        total = slots[0]
        for k in range(1, size):
            total = total + slots[k]
        return total

    chunk = cond_buf.shape[-1]

    def cond_copy(j):
        return pltpu.make_async_copy(
            cond_ref.at[:, pl.ds(pl.multiple_of(j * chunk, LANES), chunk)],
            cond_buf.at[lax.rem(j, 2)],
            cond_sems.at[lax.rem(j, 2)],
        )

    def small_pair():
        return remote(s_grads.at[:, 1 - core], s_pair, s_sems, (0,), ctx=sibling)

    def small_x(ahead):
        return remote(
            s_send.at[ahead - 1], s_x.at[ahead - 1], s_x_sems, (ahead - 1,), fsdp=lax.rem(f + ahead, nf)
        )

    def small_y(ahead):
        return remote(
            s_y_send, s_y.at[ahead - 1], s_y_sems, (ahead - 1,), ctx=lax.rem(chip + ahead, chips) * 2 + core
        )

    def small_end(to):
        return remote(s_done, small_ref.at[to], s_sems, (1,), ctx=sibling)

    @pl.when(step == layers)
    def _():
        cond_copy(0).start()
        c_got[c] = dm_ref[:, pl.ds(pl.multiple_of(t * columns, LANES), columns)]
        share(c_got.at[c], c_got, c_sems, "ctx", nc)
        high, low = halves(both(dh_ref))
        noisy = noisy_ref[...]
        small = dot_tn(high.astype(LOW), noisy) + dot_tn(low.astype(LOW), noisy)
        small = small + dot_tn(final_ref[...], dpred_ref[...])
        s_grads[...] = small.reshape(s_grads.shape)
        small_pair().start()

    when(1, layers, lambda: stage_2(A, old))
    when(2, layers, lambda: (pl.when(step >= 3)(lambda: end_wait(A, old, layer + 3)), stage_4(A, new, layer + 2))[1])
    when(1, layers, lambda: stage_3(M, old))

    @pl.when(step == layers)
    def _():
        small_pair().wait()
        for ahead in range(1, nf):
            peer = lax.rem(f + ahead, nf)
            s_send[ahead - 1] = s_grads[peer, core] + s_pair[peer]
            small_x(ahead).start()
        shared(c_got.at[c], c_got, c_sems, "ctx", nc)
        dcols_ref[f] = slot_sum(c_got, nc)
        share(dcols_ref.at[f], dcols_ref, f_sems, "fsdp", nf)

    def stacked_input(ref, first):
        normed, _ = norm_parts(ref[0])
        parts = [
            normed[g] * (1.0 + mod(first + 1, g, layer)) + mod(first, g, layer) for g in range(count)
        ]
        return jnp.concatenate(parts, 0).astype(LOW)

    def mlp_grads():
        w_in = stacked_input(keep_mid, 3)
        for k in range(4):
            keep_grad(HIDDEN + k, dot_tn(w_in, dpre_ref[k].reshape(count * rows, local)))
        pair_copy(H, new).start()
        branch = both(branch_ref)
        for k in range(4):
            keep_grad(MLP + k, dot_tn(branch, act_ref[k].reshape(count * rows, local)))
        pair_copy(M, new).start()
        for g in range(count):
            total_w(g).share()
        stage_2(H, new)
        stage_2(M, new)

    when(0, layers - 1, mlp_grads)
    when(1, layers, lambda: (pl.when(step >= 2)(lambda: end_wait(H, new, layer + 2)), stage_4(H, old, layer + 1))[1])

    def attention_back(g):
        normed, inv = norm_parts(keep_mid[0, g])
        d_mid, d_shift, d_scale = norm_back(total_w(g).get().astype(f32), normed, inv, mod(4, g, layer))
        d_mid = d_mid + dh_ref[g]
        dmid_ref[g] = d_mid
        put_dmod(3, g, layer, d_shift)
        put_dmod(4, g, layer, d_scale)
        put_dmod(2, g, layer, jnp.sum(d_mid * keep_a[0, g].astype(f32), 0, keepdims=True))
        branch = (mod(2, g, layer) * d_mid).astype(LOW)
        dba_ref[g] = branch
        grad = spread(dot(branch, matrix(OUT)).astype(LOW), heads)
        query = spread(keep_q[0, g], heads)
        keys = keep_kv[0, g, :, :, :local].reshape(nc * rows, local)
        values = keep_kv[0, g, :, :, local:].reshape(nc * rows, local)
        probs = keep_p[0, g]
        d_probs = dot_nt(grad, values)
        d_scores = (probs * (d_probs - jnp.sum(d_probs * probs, -1, keepdims=True))).astype(LOW)
        d_values = dot_tn(probs.astype(LOW), grad)
        d_keys = dot_tn(d_scores, query) * scale
        kv_send[g, :, :, :local] = d_keys.astype(LOW).reshape(nc, rows, local)
        kv_send[g, :, :, local:] = d_values.astype(LOW).reshape(nc, rows, local)
        for ahead in range(1, nc):
            kv_copy(g, ahead).start()
        d_query = pick(dot(d_scores, keys), heads) * scale
        dqkv_ref[0, g] = d_query.astype(LOW)

    def kv_copy(g, ahead):
        peer = lax.rem(c + ahead, nc)
        return remote(kv_send.at[g, peer], kv_got.at[new, g, ahead - 1], kv_sems, (new, g, ahead - 1), ctx=peer)

    @pl.when(step < layers)
    def _():
        for g in range(count):
            attention_back(g)

    when(1, layers, lambda: stage_3(A, old))

    @pl.when(step < layers)
    def _():
        for g in range(count):
            total = kv_send[g, c].astype(f32)
            for ahead in range(1, nc):
                kv_copy(g, ahead).wait()
                total = total + kv_got[new, g, ahead - 1].astype(f32)
            dqkv_ref[1, g] = total[:, :local].astype(LOW)
            dqkv_ref[2, g] = total[:, local:].astype(LOW)
            part = dot_nt(dqkv_ref[0, g], matrix(QUERY))
            part = part + dot_nt(dqkv_ref[1, g], matrix(KEY))
            part = part + dot_nt(dqkv_ref[2, g], matrix(VALUE))
            total_u(g).scatter(part)
        h_ref[...] = keep_h[0]
        u_in = stacked_input(keep_h, 0)
        for k in range(3):
            keep_grad(QUERY + k, dot_tn(u_in, dqkv_ref[k].reshape(count * rows, local)))
        keep_grad(OUT, dot_tn(both(dba_ref), keep_att[0].reshape(count * rows, local)))
        pair_copy(A, new).start()
        for g in range(count):
            total_u(g).share()
        stage_3(H, new)

    images_row = max(8, images)

    @pl.when(step == layers)
    def _():
        shared(dcols_ref.at[f], dcols_ref, f_sems, "fsdp", nf)
        dcols_out[...] = dcols_ref[...]
        product[...] = jnp.zeros_like(product)
        gram[...] = jnp.zeros_like(gram)
        index = lax.broadcasted_iota(jnp.int32, (LANES, chunk), 0)

        def multiply(j, carry):
            @pl.when(j + 1 < columns // chunk)
            def _():
                cond_copy(j + 1).start()

            pair = jnp.zeros((LANES, chunk), f32)
            for n in range(images):
                source = dcols_ref[
                    n // count, n % count : n % count + 1, pl.ds(pl.multiple_of(j * chunk, LANES), chunk)
                ]
                high, low = halves(source)
                pair = jnp.where(index == n, high, pair)
                pair = jnp.where(index == images + n, low, pair)
            pair = pair.astype(LOW)
            gram[...] += dot_nt(pair, pair)
            cond_copy(j).wait()
            product[...] += dot_nt(cond_buf[lax.rem(j, 2)].astype(LOW), pair)
            return carry

        lax.fori_loop(0, columns // chunk, multiply, 0)
        total = product[...]
        total = jnp.transpose(total + pltpu.roll(total, LANES - images, 1))[:images_row]
        silu_got[t] = total
        share(silu_got.at[t], silu_got, t_sems, "tp", nt)
        for ahead in range(1, nf):
            small_x(ahead).wait()
        total = s_grads[f, core] + s_pair[f]
        for ahead in range(1, nf):
            total = total + s_x[ahead - 1]
        s_y_send[...] = total
        for ahead in range(1, chips):
            small_y(ahead).start()
        shared(silu_got.at[t], silu_got, t_sems, "tp", nt)
        d_cvec = slot_sum(silu_got, nt) * slope_c_ref[...]
        dcvec_ref[...] = d_cvec
        high, low = halves(d_cvec)
        pair = jnp.concatenate([high, low], 0).astype(LOW)
        time_label = jnp.sum(dot_nt(pair, pair) * gram_t_ref[...])
        total = dot(pair, time_ref[...])
        swish_got[f] = total[:images_row] + total[images_row:]
        share(swish_got.at[f], swish_got, a_sems, "fsdp", nf)
        shared(swish_got.at[f], swish_got, a_sems, "fsdp", nf)
        d_act = slot_sum(swish_got, nf) * slope_a_ref[...]
        dact_ref[...] = d_act
        high, low = halves(d_act)
        pair = jnp.concatenate([high, low], 0).astype(LOW)
        freq = jnp.sum(dot_nt(pair, pair) * gram_f_ref[...])
        cond = jnp.sum(gram[...] * gram_c_ref[...])
        stat_ref[...] = jnp.full(
            stat_ref.shape, cond / nc + time_label / (nt * nc) + freq / (nf * nt * nc), f32
        )

    when(1, layers, lambda: (pl.when(step >= 2)(lambda: end_wait(M, new, layer + 2)), stage_4(M, old, layer + 1))[1])

    @pl.when(step == layers)
    def _():
        end_wait(A, new, 1)
        stage_4(A, old, 0)
        total = s_y_send[...]
        for ahead in range(1, chips):
            small_y(ahead).wait()
            total = total + s_y[ahead - 1]
        s_done[...] = total
        own = pltpu.make_async_copy(s_done, small_ref.at[core], s_own_sems.at[0])
        own.start()
        small_end(core).start()
        part = jnp.sum(square[...]) / chips + jnp.sum(total * total) / (nt * chips)
        index = lax.broadcasted_iota(jnp.int32, stat_ref.shape, 0)
        stat_ref[...] = jnp.where(index < 8, stat_ref[...] + part, loss_ref[0:1] / nt)
        for k, (axis, size) in enumerate((("ctx", nc), ("fsdp", nf), ("tp", nt))):
            me = lax.axis_index(axis)
            slots = stat_got.at[k]
            slots[me] = stat_ref[...]
            share(slots.at[me], slots, n_sems, axis, size, (k,))
            shared(slots.at[me], slots, n_sems, axis, size, (k,))
            stat_ref[...] = slot_sum(slots, size)
        for k in range(3):
            end_wait(k, old, 0)
        own.wait()
        small_end(core).wait_send()
        small_end(1 - core).wait_recv()


def backward(mesh, images, dh0, mods, dmods_end, loss, noisy, dpred, final_in, slopes, grams, time_low, cond, full, saved):
    sizes = dict(mesh.shape)
    nf, nc, nt = sizes["fsdp"], sizes["ctx"], sizes["tp"]
    chips = nc // 2
    others, overs = max(nf - 1, 1), max(chips - 1, 1)
    count, rows, width = dh0.shape
    layers, blocks, _, local = full.shape
    shard, columns = cond.shape
    half = shard // 2
    tokens = count * rows
    padded = max(8, images)
    f32 = jnp.float32

    def per_layer(array):
        shape = array.shape[1:]
        return pl.BlockSpec(
            (1, *shape), lambda i: (jnp.maximum(layers - 1 - i, 0),) + (0,) * len(shape)
        )

    anywhere = pl.BlockSpec(memory_space=pl.ANY)
    vmem = pl.BlockSpec(memory_space=pltpu.VMEM)
    whole = pltpu.VMEM((count, nt, rows // nt, width), LOW)
    first = pltpu.VMEM((count, nt - 1, rows // nt, width), LOW)
    image = pltpu.VMEM((count, rows, width), f32)
    image_low = pltpu.VMEM((count, rows, width), LOW)
    mlp = pltpu.VMEM((4, count, rows, local), LOW)
    small = (half, LANES)
    dma = pltpu.SemaphoreType.DMA
    return pl.pallas_call(
        functools.partial(backward_kernel, sizes, images),
        grid=(layers + 1,),
        out_shape=[
            jax.ShapeDtypeStruct((layers, blocks, 2, half, local), LOW),
            jax.ShapeDtypeStruct((2, half, LANES), f32),
            jax.ShapeDtypeStruct((nf, count, columns), f32),
            jax.ShapeDtypeStruct((padded, shard), f32),
            jax.ShapeDtypeStruct((padded, width), f32),
            jax.ShapeDtypeStruct((16, LANES), f32),
        ],
        in_specs=[vmem] * 13 + [anywhere, per_layer(full), *(per_layer(s) for s in saved)],
        out_specs=[anywhere, anywhere, vmem, vmem, vmem, vmem],
        scratch_shapes=[
            image, image, image, mlp, mlp, image_low, image_low,
            pltpu.VMEM((3, count, rows, local), LOW),
            pltpu.VMEM(mods.shape, f32),
            whole, first, whole, whole, first, whole,
            pltpu.VMEM((count, nc, rows, 2 * local), LOW),
            pltpu.VMEM((2, count, nc - 1, rows, 2 * local), LOW),
            pltpu.VMEM((blocks, nf, 2, half, local), LOW),
            pltpu.VMEM((2, blocks, nf, half, local), LOW),
            pltpu.VMEM((others, blocks, half, local), LOW),
            pltpu.VMEM((2, others, blocks, half, local), LOW),
            pltpu.VMEM((blocks, half, local), LOW),
            pltpu.VMEM((2, overs, blocks, half, local), LOW),
            pltpu.VMEM((blocks, half, local), LOW),
            pltpu.VMEM((8, local), f32),
            pltpu.VMEM((nf, 2, *small), f32),
            pltpu.VMEM((nf, *small), f32),
            pltpu.VMEM((others, *small), f32),
            pltpu.VMEM((others, *small), f32),
            pltpu.VMEM(small, f32),
            pltpu.VMEM((overs, *small), f32),
            pltpu.VMEM(small, f32),
            pltpu.VMEM((nc, count, columns), f32),
            pltpu.VMEM((nf, count, columns), f32),
            pltpu.VMEM((2, shard, 512), f32),
            pltpu.VMEM((shard, LANES), f32),
            pltpu.VMEM((LANES, LANES), f32),
            pltpu.VMEM((nt, padded, shard), f32),
            pltpu.VMEM((nf, padded, width), f32),
            pltpu.VMEM((3, max(sizes.values()), 16, LANES), f32),
            dma((2, 2, count, nt - 1)),
            dma((2, 2, count, nt - 1)),
            dma((2, 2, count, nc - 1)),
            dma((2, 2, 3)),
            dma((2, 2, 3, others)),
            dma((2, 2, 3, overs)),
            dma((2, 2, 3)),
            dma((3,)),
            dma((2, 2)),
            dma((2, others)),
            dma((2, overs)),
            dma((1,)),
            dma((2, nc - 1)),
            dma((2, others)),
            dma((2,)),
            dma((2, nt - 1)),
            dma((2, others)),
            dma((2, 3, max(sizes.values()))),
        ],
        compiler_params=pltpu.CompilerParams(
            collective_id=2, has_side_effects=True, vmem_limit_bytes=60 * 2**20
        ),
        cost_estimate=pl.CostEstimate(
            flops=4 * tokens * width * blocks * local * layers,
            bytes_accessed=layers * blocks * width * local * 4,
            transcendentals=0,
        ),
        name="backward_layers",
    )(dh0, mods, dmods_end, loss, noisy, dpred, final_in, *slopes, *grams, time_low, cond, full, *saved)


FIX = 1.0 / (1.0 - BETA**STEP)


def update_block(weight, mean, square, grad, outs, where):
    mean_next = BETA * mean[where] + (1.0 - BETA) * grad
    square_next = BETA * square[where] + (1.0 - BETA) * (grad * grad)
    moved = (mean_next * FIX) / (jnp.sqrt(square_next * FIX) + EPSILON)
    outs[0][where] = weight[where] - RATE * (moved + DECAY * weight[where])
    outs[1][where] = mean_next
    outs[2][where] = square_next


def update_plain_kernel(clip_ref, grad_ref, weight, mean, square, *outs):
    clip = clip_ref[0, 0]
    rows = weight.shape[-2]
    piece = min(64, rows)
    for r in range(0, rows, piece):
        where = (0, 0, pl.ds(r, piece))
        update_block(weight, mean, square, grad_ref[where].astype(jnp.float32) * clip, outs, where)


def update_mixed_kernel(clip_ref, grad_ref, weight, mean, square, *outs):
    clip = clip_ref[0, 0]
    _, blocks, rows, columns = grad_ref.shape
    tiles = columns // LANES
    size = blocks * tiles * 16
    order = interleave(blocks, tiles)
    for r in range(rows // 16):
        parts = [
            grad_ref[0, k, 16 * r : 16 * r + 16, n * LANES : (n + 1) * LANES]
            for k in range(blocks)
            for n in range(tiles)
        ]
        grad = dot(order, jnp.concatenate(parts, 0)) * clip
        update_block(weight, mean, square, grad, outs, (0, pl.ds(r * size, size)))


def update_rank_kernel(clip_ref, left_ref, right_ref, weight, mean, square, *outs):
    clip = clip_ref[0, 0]
    rows = weight.shape[0]
    piece = min(64, rows)
    for r in range(0, rows, piece):
        where = (pl.ds(r, piece),)
        grad = dot_tn(left_ref[:, r : r + piece], right_ref[...]) * clip
        update_block(weight, mean, square, grad, outs, where)


def update(kernel, clip, factors, factor_specs, trio, spec, grid, name):
    shape = jax.ShapeDtypeStruct(trio[0].shape, jnp.float32)
    size = trio[0].size
    return pl.pallas_call(
        kernel,
        grid=grid,
        out_shape=[shape] * 3,
        in_specs=[pl.BlockSpec(memory_space=pltpu.SMEM), *factor_specs, spec, spec, spec],
        out_specs=[spec] * 3,
        compiler_params=pltpu.CompilerParams(vmem_limit_bytes=48 * 2**20),
        cost_estimate=pl.CostEstimate(flops=20 * size, bytes_accessed=26 * size, transcendentals=2 * size),
        name=name,
    )(clip, *factors, *trio)


def update_plain(clip, grads, trio, first):
    trio = [jnp.swapaxes(a, 1, 2) for a in trio]
    layers, blocks, rows, columns = trio[0].shape
    block = (1, 1, rows, columns)
    spec = pl.BlockSpec(block, lambda i, j: (i, j, 0, 0))
    grad_spec = pl.BlockSpec(block, lambda i, j: (i, first + j, 0, 0))
    outs = update(
        update_plain_kernel, clip, [grads], [grad_spec], trio, spec, (layers, blocks), "update_plain"
    )
    return [jnp.swapaxes(a, 1, 2) for a in outs]


def mixed(a):
    layers, rows, blocks, columns = a.shape
    a = a.reshape(layers, rows, blocks, columns // LANES, LANES)
    return jnp.swapaxes(a, 2, 3).reshape(layers, -1, LANES)


def update_mixed(clip, grads, trio):
    layers, rows, blocks, columns = trio[0].shape
    tiles = columns // LANES

    def back(a):
        a = a.reshape(layers, rows, tiles, blocks, LANES)
        return jnp.swapaxes(a, 2, 3).reshape(layers, rows, blocks, columns)

    step = min(rows, 128)
    spec = pl.BlockSpec((1, step * blocks * tiles, LANES), lambda i, j: (i, j, 0))
    grad_spec = pl.BlockSpec((1, blocks, step, columns), lambda i, j: (i, 0, j, 0))
    outs = update(
        update_mixed_kernel,
        clip,
        [grads],
        [grad_spec],
        [mixed(a) for a in trio],
        spec,
        (layers, rows // step),
        "update_mixed",
    )
    return [back(a) for a in outs]


def update_rank(clip, left, right, trio):
    rows, columns = trio[0].shape
    step = 512 if columns % 512 == 0 else columns
    spec = pl.BlockSpec((rows, step), lambda i: (0, i))
    left_spec = pl.BlockSpec(left.shape, lambda i: (0, 0))
    right_spec = pl.BlockSpec((right.shape[0], step), lambda i: (0, i))
    return update(
        update_rank_kernel,
        clip,
        [left, right],
        [left_spec, right_spec],
        trio,
        spec,
        (columns // step,),
        "update_rank",
    )


def split_rows(value, other):
    rounded = lax.reduce_precision(value, 8, 7)
    high, low = rounded.astype(LOW), (value - rounded).astype(LOW)
    pad = -2 * value.shape[0] % 16
    return (
        jnp.pad(jnp.concatenate([high, low]), ((0, pad), (0, 0))),
        jnp.pad(jnp.concatenate([other, other]).astype(LOW), ((0, pad), (0, 0))),
    )


def per_device(
    mesh,
    latents,
    noise,
    var_target,
    timesteps,
    labels,
    attend_weight,
    attend_mean,
    attend_square,
    hidden_weight,
    hidden_mean,
    hidden_square,
    output_weight,
    output_mean,
    output_square,
    patch_weight,
    patch_mean,
    patch_square,
    freq_weight,
    freq_mean,
    freq_square,
    time_weight,
    time_mean,
    time_square,
    label_table,
    label_mean,
    label_square,
    cond_weight,
    cond_mean,
    cond_square,
    head_weight,
    head_mean,
    head_square,
):
    count, rows, patch_in = latents.shape
    layers, shard = attend_weight.shape[:2]
    columns = cond_weight.shape[1]

    steps_all = lax.all_gather(timesteps, "fsdp", axis=0, tiled=True)
    labels_all = lax.all_gather(labels, "fsdp", axis=0, tiled=True)
    freqs = time_freqs(steps_all).astype(LOW)
    act = jnp.dot(freqs, freq_weight.astype(LOW).T, preferred_element_type=jnp.float32)
    act = lax.all_gather(act, "fsdp", axis=1, tiled=True)
    swish = jax.nn.silu(act).astype(LOW)
    time_low = time_weight.astype(LOW)
    temb = jnp.dot(swish, time_low.T, preferred_element_type=jnp.float32)
    onehot = (labels_all[:, None] == jnp.arange(label_table.shape[1], dtype=jnp.int32)[None]).astype(
        LOW
    )
    cvec = temb + jnp.dot(onehot, label_table.astype(LOW).T, preferred_element_type=jnp.float32)
    cond_in = jax.nn.silu(cvec).astype(LOW)
    cond_low = cond_weight.astype(LOW)
    mods_part = jnp.dot(cond_in, cond_low, preferred_element_type=jnp.float32)
    patch_head = lax.all_gather(
        jnp.concatenate([patch_weight, head_weight], 1).astype(LOW), "fsdp", axis=0, tiled=True
    )
    patch_full, head_full = patch_head[:, :patch_in], patch_head[:, patch_in:]
    width = patch_full.shape[0]

    level = noise_level(timesteps)[:, None, None]
    noisy = (jnp.sqrt(level) * latents + jnp.sqrt(1.0 - level) * noise).astype(LOW)
    first = lax.axis_index("ctx") * rows
    h = (
        jnp.einsum("gsp,dp->gsd", noisy, patch_full, preferred_element_type=jnp.float32)
        + positions(first, rows, width)[None]
    )
    h, flat_mods, full, *saved = forward(
        mesh,
        h,
        mods_part.reshape(-1, count, columns),
        mixed(hidden_weight),
        jnp.swapaxes(attend_weight, 1, 2),
        jnp.swapaxes(output_weight, 1, 2),
    )
    blocks = full.shape[1]
    full = full.reshape(layers, blocks, width, -1)
    mods = flat_mods.reshape(count, -1, width)
    final_in = modln(h, mods[:, 6 * layers, None], mods[:, 6 * layers + 1, None]).astype(LOW)
    pred = jnp.einsum("gsd,dp->gsp", final_in, head_full, preferred_element_type=jnp.float32)
    diff = pred - jnp.concatenate([noise, var_target], -1)
    loss_part = jnp.full((8, LANES), jnp.sum(diff * diff))
    d_pred = (2.0 * diff).astype(LOW)
    d_final = jnp.einsum("gsp,dp->gsd", d_pred, head_full, preferred_element_type=jnp.float32)
    _, norm_back = jax.vjp(modln, h, mods[:, 6 * layers, None], mods[:, 6 * layers + 1, None])
    d_h, d_shift_f, d_scale_f = norm_back(d_final)
    images = freqs.shape[0]
    padded = max(8, images) - images
    tokens = count * rows

    def slope(value):
        _, back = jax.vjp(jax.nn.silu, value)
        return jnp.pad(back(jnp.ones_like(value))[0], ((0, padded), (0, 0)))

    def gram(value):
        value = value.astype(jnp.float32)
        return jnp.einsum("nd,md->nm", value, value, precision=HIGH)

    def doubled(value):
        return jnp.tile(jnp.pad(value, ((0, padded), (0, padded))), (2, 2))

    beyond = LANES - 2 * images
    grams = (
        jnp.pad(jnp.tile(gram(cond_in), (2, 2)), ((0, beyond), (0, beyond))),
        doubled(gram(swish) + gram(onehot)),
        doubled(gram(freqs)),
    )
    patch_out = d_pred.shape[-1]
    grads, d_small, d_cols, d_cvec, d_act, stat = backward(
        mesh,
        images,
        d_h,
        flat_mods,
        jnp.concatenate([d_shift_f, d_scale_f], 2).reshape(count, -1),
        loss_part,
        jnp.pad(noisy.reshape(tokens, -1), ((0, 0), (0, LANES - patch_in))),
        jnp.pad(d_pred.reshape(tokens, -1), ((0, 0), (patch_in, LANES - patch_in - patch_out))),
        final_in.reshape(tokens, -1),
        (slope(cvec), slope(act)),
        grams,
        time_low,
        cond_weight,
        full,
        saved,
    )
    grads = grads.reshape(layers, blocks, shard, -1)
    d_small = d_small.reshape(shard, -1)
    d_cols = d_cols.reshape(images, columns)
    d_cvec = d_cvec[:images]
    d_act = lax.dynamic_slice_in_dim(
        d_act[:images], lax.axis_index("fsdp") * shard, shard, 1
    )
    total_sq, loss = stat[0, 0], stat[8, 0]
    grad_norm = jnp.sqrt(total_sq)
    clip = jnp.minimum(1.0, CLIP / (grad_norm + 1e-06))
    factor = clip.reshape(1, 1)
    cols_parts, cond_parts = split_rows(d_cols, cond_in)
    cvec_parts, swish_parts = split_rows(d_cvec, swish)
    act_parts, freq_parts = split_rows(d_act, freqs)
    updated = [
        *update_plain(factor, grads, (attend_weight, attend_mean, attend_square), QUERY),
        *update_mixed(factor, grads, (hidden_weight, hidden_mean, hidden_square)),
        *update_plain(factor, grads, (output_weight, output_mean, output_square), OUT),
        *adamw(patch_weight, patch_mean, patch_square, d_small[:, :patch_in] * clip),
        *update_rank(factor, act_parts, freq_parts, (freq_weight, freq_mean, freq_square)),
        *update_rank(factor, cvec_parts, swish_parts, (time_weight, time_mean, time_square)),
        *adamw(
            label_table,
            label_mean,
            label_square,
            rank_sum(d_cvec, onehot.astype(jnp.float32)) * clip,
        ),
        *update_rank(factor, cond_parts, cols_parts, (cond_weight, cond_mean, cond_square)),
        *adamw(
            head_weight, head_mean, head_square, d_small[:, patch_in : patch_in + patch_out] * clip
        ),
    ]
    return (loss, grad_norm, *updated)


def solution(mesh):
    image = P("fsdp", "ctx", None)
    layer = P(None, "fsdp", None, "tp")
    rows = P("fsdp", None)
    cond = P("fsdp", "tp")
    weights = (layer,) * 9 + (rows,) * 12 + (cond,) * 3 + (rows,) * 3
    return jax.shard_map(
        functools.partial(per_device, mesh),
        mesh=mesh,
        in_specs=(image, image, image, P("fsdp"), P("fsdp")) + weights,
        out_specs=(P(), P()) + weights,
        check_vma=False,
    )
```

```python
import functools
import math

import jax
import jax.numpy as jnp
from jax import lax
from jax.experimental import pallas as pl
from jax.experimental.pallas import tpu as pltpu
from jax.sharding import PartitionSpec as P

HEAD_DIM = 64
FREQ = 256
GRID = 16
STEP = 5


HIGH = lax.Precision.HIGHEST
RATE = 0.05
DECAY = 0.1
BETA = 0.5
EPSILON = 1e-08
CLIP = 1.0
LOW = jnp.bfloat16


def noise_level(steps):
    phase = (steps.astype(jnp.float32) / 1000.0 + 0.008) / 1.008 * (0.5 * math.pi)
    return jnp.cos(phase) ** 2


def time_freqs(steps):
    half = FREQ // 2
    rates = jnp.exp(-math.log(10000.0) * jnp.arange(half, dtype=jnp.float32) / half)
    angles = steps.astype(jnp.float32)[:, None] * rates[None, :]
    return jnp.concatenate([jnp.cos(angles), jnp.sin(angles)], -1)


def positions(first, count, width):
    index = first + jnp.arange(count, dtype=jnp.int32)
    row = (index // GRID).astype(jnp.float32)
    column = (index % GRID).astype(jnp.float32)
    quarter = width // 4
    rates = jnp.power(10000.0, -jnp.arange(quarter, dtype=jnp.float32) / quarter)
    across = column[:, None] * rates[None, :]
    down = row[:, None] * rates[None, :]
    return jnp.concatenate([jnp.sin(across), jnp.cos(across), jnp.sin(down), jnp.cos(down)], -1)


MESH = pl.DeviceIdType.MESH
GROUPS = ((4, 4), (0, 4), (8, 4))
QUERY, KEY, VALUE, OUT, HIDDEN, MLP = 4, 5, 6, 7, 0, 8
LANES = 128


def dot(left, right):
    return jnp.dot(left, right, preferred_element_type=jnp.float32)


def dot_nt(left, right):
    return lax.dot_general(left, right, (((1,), (1,)), ((), ())), preferred_element_type=jnp.float32)


def dot_tn(left, right):
    return lax.dot_general(left, right, (((0,), (0,)), ((), ())), preferred_element_type=jnp.float32)


def remote(src, dst, sems, where, **device):
    send, recv = (sems.at[(0, *where)], sems.at[(1, *where)])
    return pltpu.make_async_remote_copy(
        src_ref=src, dst_ref=dst, send_sem=send, recv_sem=recv, device_id=device, device_id_type=MESH
    )


def meet(sizes):
    barrier = pltpu.get_barrier_semaphore()
    count = 0
    for axis, size in sizes.items():
        for step in range(1, size):
            peer = lax.rem(lax.axis_index(axis) + step, size)
            pl.semaphore_signal(barrier, inc=1, device_id={axis: peer}, device_id_type=MESH)
            count += 1
    pl.semaphore_wait(barrier, count)


def norm_parts(h):
    mean = jnp.mean(h, -1, keepdims=True)
    cent = h - mean
    var = jnp.mean(cent * cent, -1, keepdims=True)
    inv = lax.rsqrt(var + 1e-06)
    return cent * inv, inv


def norm_back(grad, normed, inv, scale):
    grad_shift = jnp.sum(grad, 0, keepdims=True)
    grad_scale = jnp.sum(grad * normed, 0, keepdims=True)
    inner = grad * (1.0 + scale)
    mean = jnp.mean(inner, -1, keepdims=True)
    along = jnp.mean(inner * normed, -1, keepdims=True)
    return inv * (inner - mean - normed * along), grad_shift, grad_scale


class Total:
    def __init__(self, size, g, send, first, full, sems):
        self.size, self.g, self.sems = size, g, sems
        self.send, self.first, self.full = send.at[g], first.at[g], full.at[g]
        self.me = lax.axis_index("tp")

    def peer(self, ahead):
        return lax.rem(self.me + ahead, self.size)

    def one(self, ahead):
        peer = self.peer(ahead)
        return remote(
            self.send.at[peer], self.first.at[ahead - 1], self.sems, (0, self.g, ahead - 1), tp=peer
        )

    def two(self, block, ahead):
        block = self.full.at[block]
        return remote(block, block, self.sems, (1, self.g, ahead - 1), tp=self.peer(ahead))

    def scatter(self, part):
        self.send[...] = part.astype(LOW).reshape(self.send.shape)
        for ahead in range(1, self.size):
            self.one(ahead).start()

    def share(self):
        total = self.send[self.me].astype(jnp.float32)
        for ahead in range(1, self.size):
            self.one(ahead).wait()
            total = total + self.first[ahead - 1].astype(jnp.float32)
        self.full[self.me] = total.astype(LOW)
        for ahead in range(1, self.size):
            self.two(self.me, ahead).start()

    def get(self):
        for ahead in range(1, self.size):
            self.two(self.me, ahead).wait_send()
            self.two(lax.rem(self.me + self.size - ahead, self.size), ahead).wait_recv()
        size, rows, width = self.full.shape
        return self.full[...].reshape(size * rows, width)


def spread(block, heads):
    lane = lax.broadcasted_iota(jnp.int32, block.shape, 1) // HEAD_DIM
    zero = jnp.zeros_like(block)
    return jnp.concatenate([jnp.where(lane == k, block, zero) for k in range(heads)], 0)


def pick(stacked, heads):
    rows = stacked.shape[0] // heads
    lane = lax.broadcasted_iota(jnp.int32, (rows, stacked.shape[1]), 1) // HEAD_DIM
    total = jnp.zeros((rows, stacked.shape[1]), stacked.dtype)
    for k in range(heads):
        total = jnp.where(lane == k, stacked[k * rows : (k + 1) * rows], total)
    return total


ROOT_2_PI = math.sqrt(2.0 / math.pi)


def gelu_parts(v):
    inside = jnp.tanh(ROOT_2_PI * (v + 0.044715 * (v * v * v)))
    value = v * (0.5 * (1.0 + inside))
    slope = 0.5 * (1.0 + inside) + 0.5 * v * (1.0 - inside * inside) * ROOT_2_PI * (
        1.0 + 3 * 0.044715 * v * v
    )
    return value, slope


def row(ref, g, index, width):
    return ref[g : g + 1, pl.ds(pl.multiple_of(index * width, LANES), width)]


def put_row(ref, g, index, width, value):
    ref[g : g + 1, pl.ds(pl.multiple_of(index * width, LANES), width)] = value


def interleave(blocks, tiles, back=False):
    size = blocks * tiles * 16
    to = lax.broadcasted_iota(jnp.int32, (size, size), 1 if back else 0)
    source = lax.broadcasted_iota(jnp.int32, (size, size), 0 if back else 1)
    block, tile, at = to % blocks, (to // blocks) % tiles, to // (blocks * tiles)
    return jnp.where(source == (block * tiles + tile) * 16 + at, 1.0, 0.0).astype(LOW)


def forward_kernel(
    sizes, images, target_first, target_count, cond_in_ref, cond_ref, ends_ref, noisy_ref, pos_ref, target_ref, hidden_ref, attend_ref, output_ref,
    dh_out, mods_out, dmods_out, loss_out, dpred_out, final_out, full_ref,
    keep_h, keep_mid, keep_a, keep_m, keep_q, keep_kv, keep_p, keep_att, keep_pre,
    weights, stage_h, stage_a, stage_o, part_ref, cond_buf, ends, kv, h_ref, q_ref, mods_ref, mods_got, send_a, first_a, full_a, send_m, first_m, full_m,
    x_sems, y_sems, pair_sems, own_sems, kv_sems, a_sems, m_sems, mods_x_sems, mods_t_sems, cond_sems, ends_sems,
):
    nf, nc, nt = sizes["fsdp"], sizes["ctx"], sizes["tp"]
    chips = nc // 2
    step = pl.program_id(0)
    layers = attend_ref.shape[0]
    f, c, t = lax.axis_index("fsdp"), lax.axis_index("ctx"), lax.axis_index("tp")
    core, chip = lax.rem(c, 2), c // 2
    sibling = c + 1 - 2 * core
    count, rows, width = h_ref.shape
    local = weights.shape[-1]
    heads = local // HEAD_DIM
    scale = 1.0 / math.sqrt(HEAD_DIM)
    columns = part_ref.shape[-1]

    def blocks(k):
        return pl.ds(*GROUPS[k])

    def x_copy(layer, k, ahead):
        return remote(
            weights.at[layer, blocks(k), f, chip, core],
            weights.at[layer, blocks(k), f, chip, core],
            x_sems,
            (layer, k, ahead - 1),
            fsdp=lax.rem(f + ahead, nf),
        )

    def x_arrived(layer, k, ahead):
        source = lax.rem(f + nf - ahead, nf)
        block = weights.at[layer, blocks(k), source, chip, core]
        remote(block, block, x_sems, (layer, k, ahead - 1), fsdp=source).wait_recv()

    def y_copy(layer, k, ahead, over, at):
        source = lax.rem(f + nf - ahead, nf)
        block = weights.at[layer, blocks(k), source, at, core]
        peer = lax.rem(chip + over, chips) * 2 + core
        return remote(block, block, y_sems, (layer, k, ahead - 1, over - 1), ctx=peer)

    def pair_copy(layer, k, ahead, half):
        source = lax.rem(f + nf - ahead, nf)
        block = weights.at[layer, blocks(k), source, :, half]
        return remote(block, block, pair_sems, (layer, k, ahead - 1), ctx=sibling)

    def pass_y(layer, k):
        for ahead in range(1, nf):
            x_arrived(layer, k, ahead)
            for over in range(1, chips):
                y_copy(layer, k, ahead, over, chip).start()

    def pass_pair(layer, k):
        for ahead in range(1, nf):
            for over in range(1, chips):
                y_copy(layer, k, ahead, over, lax.rem(chip + chips - over, chips)).wait_recv()
            pair_copy(layer, k, ahead, core).start()

    def arrived(layer, k):
        for ahead in range(1, nf):
            pair_copy(layer, k, ahead, 1 - core).wait_recv()

    def stage_copies(layer):
        return [
            pltpu.make_async_copy(source.at[layer], stage, own_sems.at[1 + k])
            for k, (source, stage) in enumerate(
                ((attend_ref, stage_a), (hidden_ref, stage_h), (output_ref, stage_o))
            )
        ]

    def quarters(value):
        return value.astype(LOW).reshape(chips, 2, -1, local)

    def send_x(layer, k):
        for ahead in range(1, nf):
            x_copy(layer, k, ahead).start()

    def lower_attend(layer):
        copies = stage_copies(layer)
        copies[0].wait()
        copies[2].wait()
        for k in range(3):
            weights[layer, QUERY + k, f] = quarters(stage_a[k])
        weights[layer, OUT, f] = quarters(stage_o[0])
        send_x(layer, 0)

    def lower_rest(layer):
        stage_copies(layer)[1].wait()
        tiles = local // LANES
        size = 4 * tiles * 16
        order = interleave(4, tiles, back=True)
        quarter = weights.shape[-2]

        def split(r, carry):
            rows_in = pl.ds(pl.multiple_of(r * size, size), size)
            value = dot(order, stage_h[rows_in].astype(LOW)).astype(LOW)
            part = (r * 16) // quarter
            at = pl.ds(pl.multiple_of(lax.rem(r * 16, quarter), 16), 16)
            for k in range(4):
                for n in range(tiles):
                    first = (k * tiles + n) * 16
                    weights[
                        layer, HIDDEN + k, f, part // 2, lax.rem(part, 2), at, n * LANES : (n + 1) * LANES
                    ] = value[first : first + 16]
            return carry

        lax.fori_loop(0, stage_h.shape[0] // size, split, 0, unroll=2)
        send_x(layer, 1)
        for k in range(4):
            weights[layer, MLP + k, f] = quarters(stage_o[1 + k])
        send_x(layer, 2)

    chunk = cond_buf.shape[-1]

    def cond_copy(j):
        return pltpu.make_async_copy(
            cond_ref.at[:, pl.ds(pl.multiple_of(j * chunk, LANES), chunk)],
            cond_buf.at[lax.rem(j, 2)],
            cond_sems.at[lax.rem(j, 2)],
        )

    def multiply(j, carry):
        @pl.when(j + 1 < columns // chunk)
        def _():
            cond_copy(j + 1).start()

        cond_copy(j).wait()
        product = dot(cond_in_ref[...], cond_buf[lax.rem(j, 2)].astype(LOW))
        for n in range(images):
            part_ref[
                n // count, n % count : n % count + 1, pl.ds(pl.multiple_of(j * chunk, LANES), chunk)
            ] = product[n : n + 1]
        return carry

    def ends_copy(ahead, at):
        return remote(ends.at[at], ends.at[at], ends_sems, (ahead - 1,), fsdp=lax.rem(f + ahead, nf))

    def both_ends():
        return ends[...].reshape(width, LANES)

    def store_copy(layer):
        return pltpu.make_async_copy(weights.at[layer], full_ref.at[layer], own_sems.at[4 + layer])

    def share_mods():
        for ahead in range(1, nf):
            peer = lax.rem(f + ahead, nf)
            remote(part_ref.at[peer], mods_got.at[ahead - 1], mods_x_sems, (ahead - 1,), fsdp=peer).start()

    def finish_mods():
        total = part_ref[f]
        for ahead in range(1, nf):
            peer = lax.rem(f + ahead, nf)
            remote(part_ref.at[peer], mods_got.at[ahead - 1], mods_x_sems, (ahead - 1,), fsdp=peer).wait()
            total = total + mods_got[ahead - 1]

        def at(k):
            return mods_ref.at[:, pl.ds(pl.multiple_of(k * columns, LANES), columns)]

        mods_ref[:, pl.ds(pl.multiple_of(t * columns, LANES), columns)] = total
        for ahead in range(1, nt):
            remote(at(t), at(t), mods_t_sems, (ahead - 1,), tp=lax.rem(t + ahead, nt)).start()
        for ahead in range(1, nt):
            source = lax.rem(t + nt - ahead, nt)
            remote(at(t), at(t), mods_t_sems, (ahead - 1,), tp=source).wait_send()
            remote(at(source), at(source), mods_t_sems, (ahead - 1,), tp=source).wait_recv()

    def mod(k, g, layer):
        return row(mods_ref, g, 6 * layer + k, width)

    def total_a(g):
        return Total(nt, g, send_a, first_a, full_a, a_sems)

    def total_m(g):
        return Total(nt, g, send_m, first_m, full_m, m_sems)

    def kv_copy(layer, g, ahead, at):
        block = kv.at[layer, g, at]
        return remote(block, block, kv_sems, (layer, g, ahead - 1), ctx=lax.rem(c + ahead, nc))

    @pl.when(step == 0)
    def _():
        for copy in stage_copies(0):
            copy.start()
        cond_copy(0).start()
        ends[f] = ends_ref[...]
        meet(sizes)
        for ahead in range(1, nf):
            ends_copy(ahead, f).start()
        lower_attend(0)
        lax.fori_loop(0, columns // chunk, multiply, 0)
        share_mods()
        pass_y(0, 0)
        lower_rest(0)
        for copy in stage_copies(1):
            copy.start()
        pass_pair(0, 0)
        for ahead in range(1, nf):
            ends_copy(ahead, f).wait_send()
            ends_copy(ahead, lax.rem(f + nf - ahead, nf)).wait_recv()
        for g in range(count):
            h_ref[g] = dot_nt(noisy_ref[g], both_ends()) + pos_ref[...]
        finish_mods()
        pass_y(0, 1)

    def matrix(k):
        return weights[step, k].reshape(width, local)

    def begin(g):
        h = h_ref[g]
        keep_h[0, g] = h
        normed, _ = norm_parts(h)
        u_in = (normed * (1.0 + mod(1, g, step)) + mod(0, g, step)).astype(LOW)
        kv[step, g, c, :, :local] = dot(u_in, matrix(KEY)).astype(LOW)
        kv[step, g, c, :, local:] = dot(u_in, matrix(VALUE)).astype(LOW)
        for ahead in range(1, nc):
            kv_copy(step, g, ahead, c).start()
        q_ref[g] = dot(u_in, matrix(QUERY)).astype(LOW)

    def last_branch(g):
        branch = total_m(g).get()
        keep_m[0, g] = branch
        h_ref[g] = h_ref[g] + mod(5, g, step - 1) * branch.astype(jnp.float32)

    @pl.when(step < layers)
    def _():
        arrived(step, 0)

    def finish(g):
        normed, inv = norm_parts(h_ref[g])
        shift, scale_row = (row(mods_ref, g, 6 * layers + k, width) for k in range(2))
        final_in = (normed * (1.0 + scale_row) + shift).astype(LOW)
        final_out[g] = final_in
        lane = lax.broadcasted_iota(jnp.int32, (rows, LANES), 1)
        inside = (lane >= target_first) & (lane < target_first + target_count)
        diff = jnp.where(inside, dot(final_in, both_ends()) - target_ref[g], 0.0)
        squares = jnp.sum((diff * diff).reshape(rows // 8, 8, LANES), 0)
        loss_out[...] = squares if g == 0 else loss_out[...] + squares
        d_pred = (2.0 * diff).astype(LOW)
        dpred_out[g] = d_pred
        d_h, d_shift, d_scale = norm_back(dot_nt(d_pred, both_ends()), normed, inv, scale_row)
        dh_out[g] = d_h
        put_row(dmods_out, g, 0, width, d_shift)
        put_row(dmods_out, g, 1, width, d_scale)

    for g in range(count):

        @pl.when(step >= 1)
        def _():
            last_branch(g)

        @pl.when(step == layers)
        def _():
            finish(g)

        @pl.when(step < layers)
        def _():
            begin(g)

    @pl.when(step + 1 < layers)
    def _():
        lower_attend(step + 1)
        lower_rest(step + 1)

    @pl.when(step + 2 < layers)
    def _():
        for copy in stage_copies(step + 2):
            copy.start()

    @pl.when(step < layers)
    def _():
        pass_y(step, 2)
        pass_pair(step, 1)
        for g in range(count):
            for ahead in range(1, nc):
                kv_copy(step, g, ahead, c).wait_send()
                kv_copy(step, g, ahead, lax.rem(c + nc - ahead, nc)).wait_recv()
            keep_q[0, g] = q_ref[g]
            keep_kv[0, g] = kv[step, g]
            keys = kv[step, g, :, :, :local].reshape(nc * rows, local)
            values = kv[step, g, :, :, local:].reshape(nc * rows, local)
            scores = dot_nt(spread(q_ref[g], heads), keys) * scale
            expo = jnp.exp(scores - jnp.max(scores, -1, keepdims=True))
            probs = expo / jnp.sum(expo, -1, keepdims=True)
            keep_p[0, g] = probs
            attended = pick(dot(probs.astype(LOW), values), heads).astype(LOW)
            keep_att[0, g] = attended
            total_a(g).scatter(dot_nt(attended, matrix(OUT)))
        pass_pair(step, 2)
        for g in range(count):
            total_a(g).share()
        arrived(step, 1)

    @pl.when(step + 1 < layers)
    def _():
        pass_y(step + 1, 0)

    @pl.when(step < layers)
    def _():
        for g in range(count):
            branch = total_a(g).get()
            keep_a[0, g] = branch
            h_mid = h_ref[g] + mod(2, g, step) * branch.astype(jnp.float32)
            keep_mid[0, g] = h_mid
            h_ref[g] = h_mid
            normed, _ = norm_parts(h_mid)
            w_in = (normed * (1.0 + mod(4, g, step)) + mod(3, g, step)).astype(LOW)
            if g == 0:
                arrived(step, 2)
                store_copy(step).start()
            part = jnp.zeros((rows, width), jnp.float32)
            for k in range(4):
                pre = dot(w_in, matrix(HIDDEN + k))
                keep_pre[0, g, k] = pre
                part = part + dot_nt(gelu_parts(pre)[0].astype(LOW), matrix(MLP + k))
            total_m(g).scatter(part)

    @pl.when(step + 1 < layers)
    def _():
        pass_pair(step + 1, 0)
        pass_y(step + 1, 1)

    @pl.when(step < layers)
    def _():
        for g in range(count):
            total_m(g).share()

    @pl.when(step == layers)
    def _():
        mods_out[...] = mods_ref[...]

        def drain(layer, carry):
            store_copy(layer).wait()
            for k in range(len(GROUPS)):
                for ahead in range(1, nf):
                    x_copy(layer, k, ahead).wait_send()
                    for over in range(1, chips):
                        y_copy(layer, k, ahead, over, chip).wait_send()
                    pair_copy(layer, k, ahead, core).wait_send()
            return carry

        lax.fori_loop(0, layers, drain, 0)


def forward(mesh, images, target_at, cond_in, cond, ends, noisy, pos, target, hidden, attend, output):
    sizes = dict(mesh.shape)
    nf, nc, nt = sizes["fsdp"], sizes["ctx"], sizes["tp"]
    chips = nc // 2
    count, rows, _ = noisy.shape
    width, columns = pos.shape[1], cond.shape[1]
    layers, _, shard, local = attend.shape
    blocks, quarter = 4 + attend.shape[1] + output.shape[1], shard // nc
    heads = local // HEAD_DIM
    tokens = count * rows
    others, overs = max(nf - 1, 1), max(chips - 1, 1)
    f32 = jnp.float32

    def kept(shape, dtype, late=0):
        spec = pl.BlockSpec(
            (1, *shape), lambda i: (jnp.clip(i - late, 0, layers - 1),) + (0,) * len(shape)
        )
        return jax.ShapeDtypeStruct((layers, *shape), dtype), spec

    saves = [
        kept((count, rows, width), f32),
        kept((count, rows, width), f32),
        kept((count, rows, width), LOW),
        kept((count, rows, width), LOW, 1),
        kept((count, rows, local), LOW),
        kept((count, nc, rows, 2 * local), LOW),
        kept((count, heads * rows, nc * rows), f32),
        kept((count, rows, local), LOW),
        kept((count, 4, rows, local), f32),
    ]
    anywhere = pl.BlockSpec(memory_space=pl.ANY)
    vmem = pl.BlockSpec(memory_space=pltpu.VMEM)
    whole = pltpu.VMEM((count, nt, rows // nt, width), LOW)
    first = pltpu.VMEM((count, nt - 1, rows // nt, width), LOW)
    dma = pltpu.SemaphoreType.DMA
    return pl.pallas_call(
        functools.partial(forward_kernel, sizes, images, *target_at),
        grid=(layers + 1,),
        out_shape=[
            jax.ShapeDtypeStruct((count, rows, width), f32),
            jax.ShapeDtypeStruct((count, nt * columns), f32),
            jax.ShapeDtypeStruct((count, 2 * width), f32),
            jax.ShapeDtypeStruct((8, LANES), f32),
            jax.ShapeDtypeStruct((count, rows, LANES), LOW),
            jax.ShapeDtypeStruct((count, rows, width), LOW),
            jax.ShapeDtypeStruct((layers, blocks, nf, chips, 2, quarter, local), LOW),
            *(shape for shape, _ in saves),
        ],
        in_specs=[vmem, anywhere, *[vmem] * 4, anywhere, anywhere, anywhere],
        out_specs=[*[vmem] * 6, anywhere, *(spec for _, spec in saves)],
        scratch_shapes=[
            pltpu.VMEM((layers, blocks, nf, chips, 2, quarter, local), LOW),
            *(pltpu.VMEM(w.shape[1:], f32) for w in (hidden, attend, output)),
            pltpu.VMEM((nf, count, columns), f32),
            pltpu.VMEM((2, shard, 512), f32),
            pltpu.VMEM((nf, shard, LANES), LOW),
            pltpu.VMEM((layers, count, nc, rows, 2 * local), LOW),
            pltpu.VMEM((count, rows, width), f32),
            pltpu.VMEM((count, rows, local), LOW),
            pltpu.VMEM((count, nt * columns), f32),
            pltpu.VMEM((others, count, columns), f32),
            whole, first, whole, whole, first, whole,
            dma((2, layers, 3, others)),
            dma((2, layers, 3, others, overs)),
            dma((2, layers, 3, others)),
            dma((4 + layers,)),
            dma((2, layers, count, nc - 1)),
            dma((2, 2, count, nt - 1)),
            dma((2, 2, count, nt - 1)),
            dma((2, others)),
            dma((2, nt - 1)),
            dma((2,)),
            dma((2, others)),
        ],
        compiler_params=pltpu.CompilerParams(
            collective_id=1, has_side_effects=True, vmem_limit_bytes=56 * 2**20
        ),
        cost_estimate=pl.CostEstimate(
            flops=2 * tokens * width * blocks * local * layers,
            bytes_accessed=layers * blocks * width * local * 4,
            transcendentals=0,
        ),
        name="forward_layers",
    )(cond_in, cond, ends, noisy, pos, target, hidden, attend, output)


def halves(value):
    high = value.astype(LOW).astype(jnp.float32)
    return high, value - high


def backward_kernel(
    sizes, images, dh0_ref, mods_ref, dmods_end_ref, loss_ref, noisy_ref, dpred_ref, final_ref,
    slope_c_ref, slope_a_ref, gram_c_ref, gram_t_ref, gram_f_ref, time_ref, cond_ref,
    w_ref, keep_h, keep_mid, keep_a, keep_m, keep_q, keep_kv, keep_p, keep_att, keep_pre,
    grads_ref, small_ref, dcols_out, dcvec_ref, dact_ref, stat_ref,
    dh_ref, dmid_ref, h_ref, act_ref, dpre_ref, branch_ref, dba_ref, dqkv_ref, dm_ref,
    send_w, first_w, full_w, send_u, first_u, full_u, kv_send, kv_got,
    grads, pair_got, x_send, x_got, y_send, y_got, done, square,
    s_grads, s_pair, s_send, s_x, s_y_send, s_y, s_done,
    c_got, dcols_ref, cond_buf, product, gram, silu_got, swish_got, stat_got,
    w_sems, u_sems, kv_sems, pair_sems, x_sems, y_sems, end_sems, own_sems,
    s_sems, s_x_sems, s_y_sems, s_own_sems, c_sems, f_sems, cond_sems, t_sems, a_sems, n_sems,
):
    nf, nc, nt = sizes["fsdp"], sizes["ctx"], sizes["tp"]
    chips = nc // 2
    layers, _, _, half, local = grads_ref.shape
    step = pl.program_id(0)
    new = lax.rem(step, 2)
    old = 1 - new
    f, c, t = lax.axis_index("fsdp"), lax.axis_index("ctx"), lax.axis_index("tp")
    core, chip = lax.rem(c, 2), c // 2
    sibling = c + 1 - 2 * core
    count, rows, width = dh_ref.shape
    heads = local // HEAD_DIM
    scale = 1.0 / math.sqrt(HEAD_DIM)
    piece = min(64, half)
    columns = cond_ref.shape[1]
    f32 = jnp.float32
    A, H, M = 0, 1, 2
    layer = layers - 1 - step

    def blocks(k):
        return pl.ds(*GROUPS[k])

    def pieces(k, body):
        parts = half // piece

        def one(j, carry):
            body(j // parts, pl.ds(pl.multiple_of(lax.rem(j, parts) * piece, piece), piece))
            return carry

        low, size = GROUPS[k]
        lax.fori_loop(low * parts, (low + size) * parts, one, 0)

    def pair_copy(k, at):
        return remote(
            grads.at[blocks(k), :, 1 - core], pair_got.at[at, blocks(k)], pair_sems, (at, k), ctx=sibling
        )

    def x_copy(k, at, ahead):
        return remote(
            x_send.at[ahead - 1, blocks(k)], x_got.at[at, ahead - 1, blocks(k)],
            x_sems, (at, k, ahead - 1), fsdp=lax.rem(f + ahead, nf),
        )

    def y_copy(k, at, ahead):
        return remote(
            y_send.at[blocks(k)], y_got.at[at, ahead - 1, blocks(k)],
            y_sems, (at, k, ahead - 1), ctx=lax.rem(chip + ahead, chips) * 2 + core,
        )

    def end_copy(k, at, layer, to):
        return remote(done.at[blocks(k)], grads_ref.at[layer, blocks(k), to], end_sems, (at, k), ctx=sibling)

    def own_copy(k, layer):
        return pltpu.make_async_copy(done.at[blocks(k)], grads_ref.at[layer, blocks(k), core], own_sems.at[k])

    def stage_2(k, at):
        pair_copy(k, at).wait()
        for ahead in range(1, nf):
            peer = lax.rem(f + ahead, nf)

            def add(b, r):
                total = grads[b, peer, core, r].astype(f32) + pair_got[at, b, peer, r].astype(f32)
                x_send[ahead - 1, b, r] = total.astype(LOW)

            pieces(k, add)
            x_copy(k, at, ahead).start()

    def stage_3(k, at):
        for ahead in range(1, nf):
            x_copy(k, at, ahead).wait()

        def add(b, r):
            total = grads[b, f, core, r].astype(f32) + pair_got[at, b, f, r].astype(f32)
            for ahead in range(1, nf):
                total = total + x_got[at, ahead - 1, b, r].astype(f32)
            y_send[b, r] = total.astype(LOW)

        pieces(k, add)
        for ahead in range(1, chips):
            y_copy(k, at, ahead).start()

    def end_wait(k, at, layer):
        own_copy(k, layer).wait()
        end_copy(k, at, layer, core).wait_send()
        end_copy(k, at, layer, 1 - core).wait_recv()

    def stage_4(k, at, layer):
        for ahead in range(1, chips):
            y_copy(k, at, ahead).wait()

        def add(b, r):
            total = y_send[b, r].astype(f32)
            for ahead in range(1, chips):
                total = total + y_got[at, ahead - 1, b, r].astype(f32)
            low = total.astype(LOW)
            done[b, r] = low
            total = low.astype(f32)
            square[...] += jnp.sum((total * total).reshape(piece // 8, 8, local), 0)

        pieces(k, add)
        own_copy(k, layer).start()
        end_copy(k, at, layer, core).start()

    def when(low, high, body):
        pl.when((step >= low) & (step <= high))(body)

    def matrix(k):
        return w_ref[0, k].reshape(width, local)

    def mod(k, g, layer):
        return row(mods_ref, g, 6 * layer + k, width)

    def put_dmod(k, g, layer, value):
        put_row(dm_ref, g, 6 * layer + k, width, value)

    def keep_grad(k, value):
        grads[k] = value.astype(LOW).reshape(nf, 2, half, local)

    def total_w(g):
        return Total(nt, g, send_w, first_w, full_w, w_sems)

    def total_u(g):
        return Total(nt, g, send_u, first_u, full_u, u_sems)

    def both(ref):
        value = ref[...]
        return value.reshape(count * rows, value.shape[-1])

    @pl.when(step == 0)
    def _():
        meet(sizes)
        dh_ref[...] = dh0_ref[...]
        square[...] = jnp.zeros_like(square)
        for g in range(count):
            put_row(dm_ref, g, 3 * layers, 2 * width, dmods_end_ref[g : g + 1])

    def finish_input(g):
        normed, inv = norm_parts(h_ref[g])
        d_h, d_shift, d_scale = norm_back(
            total_u(g).get().astype(f32), normed, inv, mod(1, g, layer + 1)
        )
        put_dmod(0, g, layer + 1, d_shift)
        put_dmod(1, g, layer + 1, d_scale)
        dh_ref[g] = d_h + dmid_ref[g]

    def mlp_back(g):
        grad = dh_ref[g]
        put_dmod(5, g, layer, jnp.sum(grad * keep_m[0, g].astype(f32), 0, keepdims=True))
        branch = (mod(5, g, layer) * grad).astype(LOW)
        branch_ref[g] = branch
        part = jnp.zeros((rows, width), f32)
        for k in range(4):
            value, slope = gelu_parts(keep_pre[0, g, k])
            act_ref[k, g] = value.astype(LOW)
            d_pre = (dot(branch, matrix(MLP + k)) * slope).astype(LOW)
            dpre_ref[k, g] = d_pre
            part = part + dot_nt(d_pre, matrix(HIDDEN + k))
        total_w(g).scatter(part)

    for g in range(count):
        when(1, layers, lambda: finish_input(g))
        when(0, layers - 1, lambda: mlp_back(g))

    def share(own, slots, sems, axis, size, where=()):
        me = lax.axis_index(axis)
        for ahead in range(1, size):
            remote(own, slots.at[me], sems, (*where, ahead - 1), **{axis: lax.rem(me + ahead, size)}).start()

    def shared(own, slots, sems, axis, size, where=()):
        me = lax.axis_index(axis)
        for ahead in range(1, size):
            remote(own, slots.at[me], sems, (*where, ahead - 1), **{axis: lax.rem(me + ahead, size)}).wait_send()
            source = lax.rem(me + size - ahead, size)
            remote(slots.at[source], slots.at[source], sems, (*where, ahead - 1), **{axis: source}).wait_recv()

    def slot_sum(slots, size):
        total = slots[0]
        for k in range(1, size):
            total = total + slots[k]
        return total

    chunk = cond_buf.shape[-1]

    def cond_copy(j):
        return pltpu.make_async_copy(
            cond_ref.at[:, pl.ds(pl.multiple_of(j * chunk, LANES), chunk)],
            cond_buf.at[lax.rem(j, 2)],
            cond_sems.at[lax.rem(j, 2)],
        )

    def small_pair():
        return remote(s_grads.at[:, 1 - core], s_pair, s_sems, (0,), ctx=sibling)

    def small_x(ahead):
        return remote(
            s_send.at[ahead - 1], s_x.at[ahead - 1], s_x_sems, (ahead - 1,), fsdp=lax.rem(f + ahead, nf)
        )

    def small_y(ahead):
        return remote(
            s_y_send, s_y.at[ahead - 1], s_y_sems, (ahead - 1,), ctx=lax.rem(chip + ahead, chips) * 2 + core
        )

    def small_end(to):
        return remote(s_done, small_ref.at[to], s_sems, (1,), ctx=sibling)

    @pl.when(step == layers)
    def _():
        cond_copy(0).start()
        c_got[c] = dm_ref[:, pl.ds(pl.multiple_of(t * columns, LANES), columns)]
        share(c_got.at[c], c_got, c_sems, "ctx", nc)
        high, low = halves(both(dh_ref))
        noisy = noisy_ref[...]
        small = dot_tn(high.astype(LOW), noisy) + dot_tn(low.astype(LOW), noisy)
        small = small + dot_tn(final_ref[...], dpred_ref[...])
        s_grads[...] = small.reshape(s_grads.shape)
        small_pair().start()

    when(1, layers, lambda: stage_2(A, old))
    when(2, layers, lambda: (pl.when(step >= 3)(lambda: end_wait(A, old, layer + 3)), stage_4(A, new, layer + 2))[1])
    when(2, layers, lambda: stage_3(M, old))

    @pl.when(step == layers)
    def _():
        small_pair().wait()
        for ahead in range(1, nf):
            peer = lax.rem(f + ahead, nf)
            s_send[ahead - 1] = s_grads[peer, core] + s_pair[peer]
            small_x(ahead).start()
        shared(c_got.at[c], c_got, c_sems, "ctx", nc)
        dcols_ref[f] = slot_sum(c_got, nc)
        share(dcols_ref.at[f], dcols_ref, f_sems, "fsdp", nf)

    def stacked_input(ref, first):
        normed, _ = norm_parts(ref[0])
        parts = [
            normed[g] * (1.0 + mod(first + 1, g, layer)) + mod(first, g, layer) for g in range(count)
        ]
        return jnp.concatenate(parts, 0).astype(LOW)

    def mlp_grads():
        w_in = stacked_input(keep_mid, 3)
        for k in range(4):
            keep_grad(HIDDEN + k, dot_tn(w_in, dpre_ref[k].reshape(count * rows, local)))
        pair_copy(H, new).start()
        branch = both(branch_ref)
        for k in range(4):
            keep_grad(MLP + k, dot_tn(branch, act_ref[k].reshape(count * rows, local)))
        pair_copy(M, new).start()
        for g in range(count):
            total_w(g).share()
        stage_2(H, new)
        stage_2(M, new)

    when(0, layers - 1, mlp_grads)
    when(1, layers, lambda: (pl.when(step >= 2)(lambda: end_wait(H, new, layer + 2)), stage_4(H, old, layer + 1))[1])

    def attention_back(g):
        normed, inv = norm_parts(keep_mid[0, g])
        d_mid, d_shift, d_scale = norm_back(total_w(g).get().astype(f32), normed, inv, mod(4, g, layer))
        d_mid = d_mid + dh_ref[g]
        dmid_ref[g] = d_mid
        put_dmod(3, g, layer, d_shift)
        put_dmod(4, g, layer, d_scale)
        put_dmod(2, g, layer, jnp.sum(d_mid * keep_a[0, g].astype(f32), 0, keepdims=True))
        branch = (mod(2, g, layer) * d_mid).astype(LOW)
        dba_ref[g] = branch
        grad = spread(dot(branch, matrix(OUT)).astype(LOW), heads)
        query = spread(keep_q[0, g], heads)
        keys = keep_kv[0, g, :, :, :local].reshape(nc * rows, local)
        values = keep_kv[0, g, :, :, local:].reshape(nc * rows, local)
        probs = keep_p[0, g]
        d_probs = dot_nt(grad, values)
        d_scores = (probs * (d_probs - jnp.sum(d_probs * probs, -1, keepdims=True))).astype(LOW)
        d_values = dot_tn(probs.astype(LOW), grad)
        d_keys = dot_tn(d_scores, query) * scale
        kv_send[g, :, :, :local] = d_keys.astype(LOW).reshape(nc, rows, local)
        kv_send[g, :, :, local:] = d_values.astype(LOW).reshape(nc, rows, local)
        for ahead in range(1, nc):
            kv_copy(g, ahead).start()
        d_query = pick(dot(d_scores, keys), heads) * scale
        dqkv_ref[0, g] = d_query.astype(LOW)

    def kv_copy(g, ahead):
        peer = lax.rem(c + ahead, nc)
        return remote(kv_send.at[g, peer], kv_got.at[new, g, ahead - 1], kv_sems, (new, g, ahead - 1), ctx=peer)

    @pl.when(step < layers)
    def _():
        for g in range(count):
            attention_back(g)

    when(1, layers, lambda: stage_3(A, old))
    when(0, 0, lambda: stage_3(H, new))

    @pl.when(step < layers)
    def _():
        for g in range(count):
            total = kv_send[g, c].astype(f32)
            for ahead in range(1, nc):
                kv_copy(g, ahead).wait()
                total = total + kv_got[new, g, ahead - 1].astype(f32)
            dqkv_ref[1, g] = total[:, :local].astype(LOW)
            dqkv_ref[2, g] = total[:, local:].astype(LOW)
            part = dot_nt(dqkv_ref[0, g], matrix(QUERY))
            part = part + dot_nt(dqkv_ref[1, g], matrix(KEY))
            part = part + dot_nt(dqkv_ref[2, g], matrix(VALUE))
            total_u(g).scatter(part)
        h_ref[...] = keep_h[0]
        u_in = stacked_input(keep_h, 0)
        for k in range(3):
            keep_grad(QUERY + k, dot_tn(u_in, dqkv_ref[k].reshape(count * rows, local)))
        keep_grad(OUT, dot_tn(both(dba_ref), keep_att[0].reshape(count * rows, local)))
        pair_copy(A, new).start()
        for g in range(count):
            total_u(g).share()

    when(1, layers - 1, lambda: stage_3(H, new))
    when(0, 0, lambda: stage_3(M, new))

    images_row = max(8, images)

    @pl.when(step == layers)
    def _():
        shared(dcols_ref.at[f], dcols_ref, f_sems, "fsdp", nf)
        product[...] = jnp.zeros_like(product)
        gram[...] = jnp.zeros_like(gram)
        index = lax.broadcasted_iota(jnp.int32, (LANES, chunk), 0)

        def multiply(j, carry):
            @pl.when(j + 1 < columns // chunk)
            def _():
                cond_copy(j + 1).start()

            pair = jnp.zeros((LANES, chunk), f32)
            for n in range(images):
                source = dcols_ref[
                    n // count, n % count : n % count + 1, pl.ds(pl.multiple_of(j * chunk, LANES), chunk)
                ]
                high, low = halves(source)
                pair = jnp.where(index == n, high, pair)
                pair = jnp.where(index == images + n, low, pair)
            pair = pair.astype(LOW)
            dcols_out[:, pl.ds(pl.multiple_of(j * chunk, LANES), chunk)] = pair[: dcols_out.shape[0]]
            gram[...] += dot_nt(pair, pair)
            cond_copy(j).wait()
            product[...] += dot_nt(cond_buf[lax.rem(j, 2)].astype(LOW), pair)
            return carry

        lax.fori_loop(0, columns // chunk, multiply, 0)
        total = product[...]
        total = jnp.transpose(total + pltpu.roll(total, LANES - images, 1))[:images_row]
        silu_got[t] = total
        share(silu_got.at[t], silu_got, t_sems, "tp", nt)
        for ahead in range(1, nf):
            small_x(ahead).wait()
        total = s_grads[f, core] + s_pair[f]
        for ahead in range(1, nf):
            total = total + s_x[ahead - 1]
        s_y_send[...] = total
        for ahead in range(1, chips):
            small_y(ahead).start()
        shared(silu_got.at[t], silu_got, t_sems, "tp", nt)
        d_cvec = slot_sum(silu_got, nt) * slope_c_ref[...]
        high, low = halves(d_cvec)
        pair = jnp.concatenate([high, low], 0).astype(LOW)
        dcvec_ref[...] = pair
        time_label = jnp.sum(dot_nt(pair, pair) * gram_t_ref[...])
        total = dot(pair, time_ref[...])
        swish_got[f] = total[:images_row] + total[images_row:]
        share(swish_got.at[f], swish_got, a_sems, "fsdp", nf)
        shared(swish_got.at[f], swish_got, a_sems, "fsdp", nf)
        d_act = slot_sum(swish_got, nf) * slope_a_ref[...]
        high, low = halves(d_act)
        pair = jnp.concatenate([high, low], 0).astype(LOW)
        dact_ref[...] = pair
        freq = jnp.sum(dot_nt(pair, pair) * gram_f_ref[...])
        cond = jnp.sum(gram[...] * gram_c_ref[...])
        stat_ref[...] = jnp.full(
            stat_ref.shape, cond / nc + time_label / (nt * nc) + freq / (nf * nt * nc), f32
        )

    when(1, layers, lambda: (pl.when(step >= 2)(lambda: end_wait(M, new, layer + 2)), stage_4(M, old, layer + 1))[1])

    @pl.when(step == layers)
    def _():
        end_wait(A, new, 1)
        stage_4(A, old, 0)
        total = s_y_send[...]
        for ahead in range(1, chips):
            small_y(ahead).wait()
            total = total + s_y[ahead - 1]
        s_done[...] = total
        own = pltpu.make_async_copy(s_done, small_ref.at[core], s_own_sems.at[0])
        own.start()
        small_end(core).start()
        part = jnp.sum(square[...]) / chips + jnp.sum(total * total) / (nt * chips)
        index = lax.broadcasted_iota(jnp.int32, stat_ref.shape, 0)
        stat_ref[...] = jnp.where(index < 8, stat_ref[...] + part, jnp.sum(loss_ref[...]) / nt)
        for k, (axis, size) in enumerate((("ctx", nc), ("fsdp", nf), ("tp", nt))):
            me = lax.axis_index(axis)
            slots = stat_got.at[k]
            slots[me] = stat_ref[...]
            share(slots.at[me], slots, n_sems, axis, size, (k,))
            shared(slots.at[me], slots, n_sems, axis, size, (k,))
            stat_ref[...] = slot_sum(slots, size)
        for k in range(3):
            end_wait(k, old, 0)
        own.wait()
        small_end(core).wait_send()
        small_end(1 - core).wait_recv()


def backward(mesh, images, dh0, mods, dmods_end, loss, noisy, dpred, final_in, slopes, grams, time_low, cond, full, saved):
    sizes = dict(mesh.shape)
    nf, nc, nt = sizes["fsdp"], sizes["ctx"], sizes["tp"]
    chips = nc // 2
    others, overs = max(nf - 1, 1), max(chips - 1, 1)
    count, rows, width = dh0.shape
    layers, blocks, _, local = full.shape
    shard, columns = cond.shape
    half = shard // 2
    tokens = count * rows
    padded = max(8, images)
    f32 = jnp.float32

    def per_layer(array):
        shape = array.shape[1:]
        return pl.BlockSpec(
            (1, *shape), lambda i: (jnp.maximum(layers - 1 - i, 0),) + (0,) * len(shape)
        )

    anywhere = pl.BlockSpec(memory_space=pl.ANY)
    vmem = pl.BlockSpec(memory_space=pltpu.VMEM)
    whole = pltpu.VMEM((count, nt, rows // nt, width), LOW)
    first = pltpu.VMEM((count, nt - 1, rows // nt, width), LOW)
    image = pltpu.VMEM((count, rows, width), f32)
    image_low = pltpu.VMEM((count, rows, width), LOW)
    mlp = pltpu.VMEM((4, count, rows, local), LOW)
    small = (half, LANES)
    dma = pltpu.SemaphoreType.DMA
    return pl.pallas_call(
        functools.partial(backward_kernel, sizes, images),
        grid=(layers + 1,),
        out_shape=[
            jax.ShapeDtypeStruct((layers, blocks, 2, half, local), LOW),
            jax.ShapeDtypeStruct((2, half, LANES), f32),
            jax.ShapeDtypeStruct((-(-2 * images // 16) * 16, columns), LOW),
            jax.ShapeDtypeStruct((2 * padded, shard), LOW),
            jax.ShapeDtypeStruct((2 * padded, width), LOW),
            jax.ShapeDtypeStruct((16, LANES), f32),
        ],
        in_specs=[vmem] * 13 + [anywhere, per_layer(full), *(per_layer(s) for s in saved)],
        out_specs=[anywhere, anywhere, vmem, vmem, vmem, vmem],
        scratch_shapes=[
            image, image, image, mlp, mlp, image_low, image_low,
            pltpu.VMEM((3, count, rows, local), LOW),
            pltpu.VMEM(mods.shape, f32),
            whole, first, whole, whole, first, whole,
            pltpu.VMEM((count, nc, rows, 2 * local), LOW),
            pltpu.VMEM((2, count, nc - 1, rows, 2 * local), LOW),
            pltpu.VMEM((blocks, nf, 2, half, local), LOW),
            pltpu.VMEM((2, blocks, nf, half, local), LOW),
            pltpu.VMEM((others, blocks, half, local), LOW),
            pltpu.VMEM((2, others, blocks, half, local), LOW),
            pltpu.VMEM((blocks, half, local), LOW),
            pltpu.VMEM((2, overs, blocks, half, local), LOW),
            pltpu.VMEM((blocks, half, local), LOW),
            pltpu.VMEM((8, local), f32),
            pltpu.VMEM((nf, 2, *small), f32),
            pltpu.VMEM((nf, *small), f32),
            pltpu.VMEM((others, *small), f32),
            pltpu.VMEM((others, *small), f32),
            pltpu.VMEM(small, f32),
            pltpu.VMEM((overs, *small), f32),
            pltpu.VMEM(small, f32),
            pltpu.VMEM((nc, count, columns), f32),
            pltpu.VMEM((nf, count, columns), f32),
            pltpu.VMEM((2, shard, 512), f32),
            pltpu.VMEM((shard, LANES), f32),
            pltpu.VMEM((LANES, LANES), f32),
            pltpu.VMEM((nt, padded, shard), f32),
            pltpu.VMEM((nf, padded, width), f32),
            pltpu.VMEM((3, max(sizes.values()), 16, LANES), f32),
            dma((2, 2, count, nt - 1)),
            dma((2, 2, count, nt - 1)),
            dma((2, 2, count, nc - 1)),
            dma((2, 2, 3)),
            dma((2, 2, 3, others)),
            dma((2, 2, 3, overs)),
            dma((2, 2, 3)),
            dma((3,)),
            dma((2, 2)),
            dma((2, others)),
            dma((2, overs)),
            dma((1,)),
            dma((2, nc - 1)),
            dma((2, others)),
            dma((2,)),
            dma((2, nt - 1)),
            dma((2, others)),
            dma((2, 3, max(sizes.values()))),
        ],
        compiler_params=pltpu.CompilerParams(
            collective_id=2, has_side_effects=True, vmem_limit_bytes=60 * 2**20
        ),
        cost_estimate=pl.CostEstimate(
            flops=4 * tokens * width * blocks * local * layers,
            bytes_accessed=layers * blocks * width * local * 4,
            transcendentals=0,
        ),
        name="backward_layers",
    )(dh0, mods, dmods_end, loss, noisy, dpred, final_in, *slopes, *grams, time_low, cond, full, *saved)


FIX = math.sqrt(1.0 / (1.0 - BETA**STEP))


def update_block(weight, mean, square, grad, outs, where):
    mean_next = BETA * mean[where] + grad
    square_next = BETA * square[where] + (grad * grad) * (1.0 / (1.0 - BETA))
    moved = mean_next / (jnp.sqrt(square_next) + EPSILON / FIX)
    outs[0][where] = weight[where] * (1.0 - RATE * DECAY) - (RATE * FIX) * moved
    outs[1][where] = mean_next
    outs[2][where] = square_next


def mixed(a):
    layers, rows, blocks, columns = a.shape
    a = a.reshape(layers, rows, blocks, columns // LANES, LANES)
    return jnp.swapaxes(a, 2, 3).reshape(layers, -1, LANES)


def update_kernel(
    plan, clip_ref, grads_ref, small_ref, cond_left, cond_right, time_left, time_right, freq_left, freq_right,
    label_left, label_right, *refs,
):
    clip = clip_ref[0, 0] * (1.0 - BETA)
    step = pl.program_id(0) * pl.num_programs(1) + pl.program_id(1)
    names = ("attend", "hidden", "output", "cond", "time", "freq", "label", "patch", "head")
    trios = {name: refs[3 * k : 3 * k + 3] for k, name in enumerate(names)}
    outs = {name: refs[27 + 3 * k : 30 + 3 * k] for k, name in enumerate(names)}

    def change(name, grad, where):
        update_block(*trios[name], grad * clip, outs[name], where)

    for name, first in (("attend", QUERY), ("output", OUT)):
        _, blocks, rows, _ = trios[name][0].shape
        piece = min(64, rows)
        for b in range(blocks):
            for r in range(0, rows, piece):
                grad = grads_ref[0, first + b, r : r + piece].astype(jnp.float32)
                change(name, grad, (0, b, pl.ds(r, piece)))

    _, _, rows, columns = grads_ref.shape
    tiles = columns // LANES
    size = 4 * tiles * 16
    order = interleave(4, tiles)
    for r in range(rows // 16):
        parts = [
            grads_ref[0, HIDDEN + k, 16 * r : 16 * r + 16, n * LANES : (n + 1) * LANES]
            for k in range(4)
            for n in range(tiles)
        ]
        change("hidden", dot(order, jnp.concatenate(parts, 0)), (0, pl.ds(r * size, size)))

    def outer(name, left, right):
        first, count = plan[name]

        @pl.when((step >= first) & (step < first + count))
        def _():
            rows = trios[name][0].shape[0]
            for r in range(0, rows, 64):
                high = min(r + 64, rows)
                change(name, dot_tn(left[:, r:high], right[...]), (pl.ds(r, high - r),))

    outer("cond", cond_left, cond_right)
    outer("time", time_left, time_right)
    outer("freq", freq_left, freq_right)
    outer("label", label_left, label_right)

    @pl.when(step == 0)
    def _():
        small = jnp.transpose(small_ref[...])
        at = 0
        for name in ("patch", "head"):
            rows = trios[name][0].shape[0]
            change(name, small[at : at + rows], (pl.ds(0, rows),))
            at += rows


def update(clip, grads, small, factors, trios):
    attend, hidden, output, patch, freq, time, label, cond, head = trios
    layers, _, rows, local = grads.shape
    parts = 4
    steps = layers * parts
    inner = rows // parts

    def turned(trio):
        return [jnp.swapaxes(a, -1, -2) for a in trio]

    def outward(trio):
        return [jnp.swapaxes(a, 1, 2) for a in trio]

    arrays = {
        "attend": outward(attend),
        "hidden": [mixed(a) for a in hidden],
        "output": outward(output),
        "cond": list(cond),
        "time": list(time),
        "freq": list(freq),
        "label": turned(label),
        "patch": turned(patch),
        "head": turned(head),
    }
    chunks = {"cond": 512, "time": LANES, "freq": LANES, "label": min(LANES, rows)}
    plan, specs = {}, {}
    for name, width in chunks.items():
        count = arrays[name][0].shape[1] // width
        plan[name] = (0 if name == "cond" else steps - count, count)

    def at(name):
        first, count = plan[name]
        return lambda i, j: (0, jnp.clip(i * parts + j - first, 0, count - 1))

    for name, (array, *_) in arrays.items():
        if name in chunks:
            specs[name] = pl.BlockSpec((array.shape[0], chunks[name]), at(name))
        elif name == "hidden":
            specs[name] = pl.BlockSpec((1, array.shape[1] // parts, LANES), lambda i, j: (i, j, 0))
        elif array.ndim == 4:
            specs[name] = pl.BlockSpec((1, array.shape[1], inner, local), lambda i, j: (i, 0, j, 0))
        else:
            specs[name] = pl.BlockSpec(array.shape, lambda i, j: (0, 0))
    factor_specs = []
    for name in ("cond", "time", "freq", "label"):
        left, right = factors[name]
        factor_specs.append(pl.BlockSpec(left.shape, lambda i, j: (0, 0)))
        factor_specs.append(pl.BlockSpec((right.shape[0], chunks[name]), at(name)))
    whole = [specs[name] for name in arrays for _ in range(3)]
    flat = [a for name in arrays for a in arrays[name]]
    size = sum(a.size for a in flat) // 3
    outs = pl.pallas_call(
        functools.partial(update_kernel, plan),
        grid=(layers, parts),
        out_shape=[jax.ShapeDtypeStruct(a.shape, jnp.float32) for a in flat],
        in_specs=[
            pl.BlockSpec(memory_space=pltpu.SMEM),
            pl.BlockSpec((1, grads.shape[1], inner, local), lambda i, j: (i, 0, j, 0)),
            pl.BlockSpec(small.shape, lambda i, j: (0, 0)),
            *factor_specs,
            *whole,
        ],
        out_specs=whole,
        compiler_params=pltpu.CompilerParams(vmem_limit_bytes=60 * 2**20),
        cost_estimate=pl.CostEstimate(flops=20 * size, bytes_accessed=26 * size, transcendentals=2 * size),
        name="update",
    )(clip, grads, small, *(f for name in ("cond", "time", "freq", "label") for f in factors[name]), *flat)
    made = {name: outs[3 * k : 3 * k + 3] for k, name in enumerate(arrays)}
    blocks = hidden[0].shape[2]

    def back(a):
        a = a.reshape(layers, rows, local // LANES, blocks, LANES)
        return jnp.swapaxes(a, 2, 3).reshape(layers, rows, blocks, local)

    return [
        *outward(made["attend"]),
        *(back(a) for a in made["hidden"]),
        *outward(made["output"]),
        *turned(made["patch"]),
        *made["freq"],
        *made["time"],
        *turned(made["label"]),
        *made["cond"],
        *turned(made["head"]),
    ]


def per_device(
    mesh,
    latents,
    noise,
    var_target,
    timesteps,
    labels,
    attend_weight,
    attend_mean,
    attend_square,
    hidden_weight,
    hidden_mean,
    hidden_square,
    output_weight,
    output_mean,
    output_square,
    patch_weight,
    patch_mean,
    patch_square,
    freq_weight,
    freq_mean,
    freq_square,
    time_weight,
    time_mean,
    time_square,
    label_table,
    label_mean,
    label_square,
    cond_weight,
    cond_mean,
    cond_square,
    head_weight,
    head_mean,
    head_square,
):
    count, rows, patch_in = latents.shape
    layers, shard = attend_weight.shape[:2]
    columns = cond_weight.shape[1]

    steps_all = lax.all_gather(timesteps, "fsdp", axis=0, tiled=True)
    labels_all = lax.all_gather(labels, "fsdp", axis=0, tiled=True)
    freqs = time_freqs(steps_all).astype(LOW)
    act = jnp.dot(freqs, freq_weight.astype(LOW).T, preferred_element_type=jnp.float32)
    act = lax.all_gather(act, "fsdp", axis=1, tiled=True)
    swish = jax.nn.silu(act).astype(LOW)
    time_low = time_weight.astype(LOW)
    temb = jnp.dot(swish, time_low.T, preferred_element_type=jnp.float32)
    onehot = (labels_all[:, None] == jnp.arange(label_table.shape[1], dtype=jnp.int32)[None]).astype(
        LOW
    )
    cvec = temb + jnp.dot(onehot, label_table.astype(LOW).T, preferred_element_type=jnp.float32)
    cond_in = jax.nn.silu(cvec).astype(LOW)
    level = noise_level(timesteps)[:, None, None]
    noisy = (jnp.sqrt(level) * latents + jnp.sqrt(1.0 - level) * noise).astype(LOW)
    images = freqs.shape[0]
    width = time_weight.shape[1]
    patch_out = head_weight.shape[1]
    after = LANES - patch_in - patch_out

    def twice(value, each):
        value = jnp.pad(value.astype(LOW), ((0, each - images), (0, 0)))
        return jnp.pad(jnp.concatenate([value, value]), ((0, -2 * each % 16), (0, 0)))

    cond_parts = twice(cond_in, images)
    noisy_wide = jnp.pad(noisy, ((0, 0), (0, 0), (0, LANES - patch_in)))
    d_h, flat_mods, d_mods_end, loss_part, d_pred, final_in, full, *saved = forward(
        mesh,
        images,
        (patch_in, patch_out),
        cond_parts,
        cond_weight,
        jnp.pad(jnp.concatenate([patch_weight, head_weight], 1).astype(LOW), ((0, 0), (0, after))),
        noisy_wide,
        positions(lax.axis_index("ctx") * rows, rows, width),
        jnp.pad(jnp.concatenate([noise, var_target], 2), ((0, 0), (0, 0), (patch_in, after))),
        mixed(hidden_weight),
        jnp.swapaxes(attend_weight, 1, 2),
        jnp.swapaxes(output_weight, 1, 2),
    )
    blocks = full.shape[1]
    full = full.reshape(layers, blocks, width, -1)
    padded = max(8, images) - images
    tokens = count * rows

    def slope(value):
        _, back = jax.vjp(jax.nn.silu, value)
        return jnp.pad(back(jnp.ones_like(value))[0], ((0, padded), (0, 0)))

    def gram(value):
        value = value.astype(jnp.float32)
        return jnp.einsum("nd,md->nm", value, value, precision=HIGH)

    def doubled(value):
        return jnp.tile(jnp.pad(value, ((0, padded), (0, padded))), (2, 2))

    beyond = LANES - 2 * images
    grams = (
        jnp.pad(jnp.tile(gram(cond_in), (2, 2)), ((0, beyond), (0, beyond))),
        doubled(gram(swish) + gram(onehot)),
        doubled(gram(freqs)),
    )
    grads, d_small, d_cols, d_cvec, d_act, stat = backward(
        mesh,
        images,
        d_h,
        flat_mods,
        d_mods_end,
        loss_part,
        noisy_wide.reshape(tokens, -1),
        d_pred.reshape(tokens, -1),
        final_in.reshape(tokens, -1),
        (slope(cvec), slope(act)),
        grams,
        time_low,
        cond_weight,
        full,
        saved,
    )
    grads = grads.reshape(layers, blocks, shard, -1)
    d_small = d_small.reshape(shard, -1)
    d_act = lax.dynamic_slice_in_dim(d_act, lax.axis_index("fsdp") * shard, shard, 1)
    total_sq, loss = stat[0, 0], stat[8, 0]
    grad_norm = jnp.sqrt(total_sq)
    clip = jnp.minimum(1.0, CLIP / (grad_norm + 1e-06))
    factor = clip.reshape(1, 1)
    each = max(8, images)
    updated = update(
        factor,
        grads,
        d_small,
        {
            "cond": (cond_parts, d_cols),
            "time": (d_cvec, twice(swish, each)),
            "freq": (d_act, twice(freqs, each)),
            "label": (twice(onehot, each), d_cvec),
        },
        (
            (attend_weight, attend_mean, attend_square),
            (hidden_weight, hidden_mean, hidden_square),
            (output_weight, output_mean, output_square),
            (patch_weight, patch_mean, patch_square),
            (freq_weight, freq_mean, freq_square),
            (time_weight, time_mean, time_square),
            (label_table, label_mean, label_square),
            (cond_weight, cond_mean, cond_square),
            (head_weight, head_mean, head_square),
        ),
    )
    return (loss, grad_norm, *updated)


def solution(mesh):
    image = P("fsdp", "ctx", None)
    layer = P(None, "fsdp", None, "tp")
    rows = P("fsdp", None)
    cond = P("fsdp", "tp")
    weights = (layer,) * 9 + (rows,) * 12 + (cond,) * 3 + (rows,) * 3
    return jax.shard_map(
        functools.partial(per_device, mesh),
        mesh=mesh,
        in_specs=(image, image, image, P("fsdp"), P("fsdp")) + weights,
        out_specs=(P(), P()) + weights,
        check_vma=False,
    )
```

```python
import functools
import math

import jax
import jax.numpy as jnp
from jax import lax
from jax.experimental import pallas as pl
from jax.experimental.pallas import tpu as pltpu
from jax.sharding import PartitionSpec as P

HEAD_DIM = 64
FREQ = 256
GRID = 16
STEP = 5


HIGH = lax.Precision.HIGHEST
RATE = 0.05
DECAY = 0.1
BETA = 0.5
EPSILON = 1e-08
CLIP = 1.0
LOW = jnp.bfloat16


def noise_level(steps):
    phase = (steps.astype(jnp.float32) / 1000.0 + 0.008) / 1.008 * (0.5 * math.pi)
    return jnp.cos(phase) ** 2


def time_freqs(steps):
    half = FREQ // 2
    rates = jnp.exp(-math.log(10000.0) * jnp.arange(half, dtype=jnp.float32) / half)
    angles = steps.astype(jnp.float32)[:, None] * rates[None, :]
    return jnp.concatenate([jnp.cos(angles), jnp.sin(angles)], -1)


def positions(first, count, width):
    index = first + jnp.arange(count, dtype=jnp.int32)
    row = (index // GRID).astype(jnp.float32)
    column = (index % GRID).astype(jnp.float32)
    quarter = width // 4
    rates = jnp.power(10000.0, -jnp.arange(quarter, dtype=jnp.float32) / quarter)
    across = column[:, None] * rates[None, :]
    down = row[:, None] * rates[None, :]
    return jnp.concatenate([jnp.sin(across), jnp.cos(across), jnp.sin(down), jnp.cos(down)], -1)


MESH = pl.DeviceIdType.MESH
GROUPS = ((4, 4), (0, 4), (8, 4))
QUERY, KEY, VALUE, OUT, HIDDEN, MLP = 4, 5, 6, 7, 0, 8
LANES = 128


def dot(left, right):
    return jnp.dot(left, right, preferred_element_type=jnp.float32)


def dot_nt(left, right):
    return lax.dot_general(left, right, (((1,), (1,)), ((), ())), preferred_element_type=jnp.float32)


def dot_tn(left, right):
    return lax.dot_general(left, right, (((0,), (0,)), ((), ())), preferred_element_type=jnp.float32)


def remote(src, dst, sems, where, **device):
    send, recv = (sems.at[(0, *where)], sems.at[(1, *where)])
    return pltpu.make_async_remote_copy(
        src_ref=src, dst_ref=dst, send_sem=send, recv_sem=recv, device_id=device, device_id_type=MESH
    )


def meet(sizes):
    barrier = pltpu.get_barrier_semaphore()
    count = 0
    for axis, size in sizes.items():
        for step in range(1, size):
            peer = lax.rem(lax.axis_index(axis) + step, size)
            pl.semaphore_signal(barrier, inc=1, device_id={axis: peer}, device_id_type=MESH)
            count += 1
    pl.semaphore_wait(barrier, count)


def norm_parts(h):
    mean = jnp.mean(h, -1, keepdims=True)
    cent = h - mean
    var = jnp.mean(cent * cent, -1, keepdims=True)
    inv = lax.rsqrt(var + 1e-06)
    return cent * inv, inv


def norm_back(grad, normed, inv, scale):
    grad_shift = jnp.sum(grad, 0, keepdims=True)
    grad_scale = jnp.sum(grad * normed, 0, keepdims=True)
    inner = grad * (1.0 + scale)
    mean = jnp.mean(inner, -1, keepdims=True)
    along = jnp.mean(inner * normed, -1, keepdims=True)
    return inv * (inner - mean - normed * along), grad_shift, grad_scale


class Total:
    def __init__(self, size, g, send, first, full, sems):
        self.size, self.g, self.sems = size, g, sems
        self.send, self.first, self.full = send.at[g], first.at[g], full.at[g]
        self.me = lax.axis_index("tp")

    def peer(self, ahead):
        return lax.rem(self.me + ahead, self.size)

    def one(self, ahead):
        peer = self.peer(ahead)
        return remote(
            self.send.at[peer], self.first.at[ahead - 1], self.sems, (0, self.g, ahead - 1), tp=peer
        )

    def two(self, block, ahead):
        block = self.full.at[block]
        return remote(block, block, self.sems, (1, self.g, ahead - 1), tp=self.peer(ahead))

    def scatter(self, part):
        self.send[...] = part.astype(LOW).reshape(self.send.shape)
        for ahead in range(1, self.size):
            self.one(ahead).start()

    def share(self):
        total = self.send[self.me].astype(jnp.float32)
        for ahead in range(1, self.size):
            self.one(ahead).wait()
            total = total + self.first[ahead - 1].astype(jnp.float32)
        self.full[self.me] = total.astype(LOW)
        for ahead in range(1, self.size):
            self.two(self.me, ahead).start()

    def get(self):
        for ahead in range(1, self.size):
            self.two(self.me, ahead).wait_send()
            self.two(lax.rem(self.me + self.size - ahead, self.size), ahead).wait_recv()
        size, rows, width = self.full.shape
        return self.full[...].reshape(size * rows, width)


def spread(block, heads):
    lane = lax.broadcasted_iota(jnp.int32, block.shape, 1) // HEAD_DIM
    zero = jnp.zeros_like(block)
    return jnp.concatenate([jnp.where(lane == k, block, zero) for k in range(heads)], 0)


def pick(stacked, heads):
    rows = stacked.shape[0] // heads
    lane = lax.broadcasted_iota(jnp.int32, (rows, stacked.shape[1]), 1) // HEAD_DIM
    total = jnp.zeros((rows, stacked.shape[1]), stacked.dtype)
    for k in range(heads):
        total = jnp.where(lane == k, stacked[k * rows : (k + 1) * rows], total)
    return total


ROOT_2_PI = math.sqrt(2.0 / math.pi)


def gelu_parts(v):
    inside = jnp.tanh(ROOT_2_PI * (v + 0.044715 * (v * v * v)))
    value = v * (0.5 * (1.0 + inside))
    slope = 0.5 * (1.0 + inside) + 0.5 * v * (1.0 - inside * inside) * ROOT_2_PI * (
        1.0 + 3 * 0.044715 * v * v
    )
    return value, slope


def row(ref, g, index, width):
    return ref[g : g + 1, pl.ds(pl.multiple_of(index * width, LANES), width)]


def put_row(ref, g, index, width, value):
    ref[g : g + 1, pl.ds(pl.multiple_of(index * width, LANES), width)] = value


def interleave(blocks, tiles, back=False):
    size = blocks * tiles * 16
    to = lax.broadcasted_iota(jnp.int32, (size, size), 1 if back else 0)
    source = lax.broadcasted_iota(jnp.int32, (size, size), 0 if back else 1)
    block, tile, at = to % blocks, (to // blocks) % tiles, to // (blocks * tiles)
    return jnp.where(source == (block * tiles + tile) * 16 + at, 1.0, 0.0).astype(LOW)


def forward_kernel(
    sizes, images, target_first, target_count, cond_in_ref, cond_ref, patch_ref, head_ref, noisy_ref, pos_ref, target_ref, hidden_ref, attend_ref, output_ref,
    dh_out, mods_out, dmods_out, loss_out, dpred_out, final_out, full_ref,
    keep_h, keep_mid, keep_a, keep_m, keep_q, keep_kv, keep_p, keep_att, keep_pre,
    weights, stage_h, stage_a, stage_o, part_ref, cond_buf, ends, kv, h_ref, q_ref, mods_ref, mods_got, send_a, first_a, full_a, send_m, first_m, full_m,
    x_sems, y_sems, pair_sems, own_sems, kv_sems, a_sems, m_sems, mods_x_sems, mods_t_sems, cond_sems, ends_sems,
):
    nf, nc, nt = sizes["fsdp"], sizes["ctx"], sizes["tp"]
    chips = nc // 2
    step = pl.program_id(0)
    layers = attend_ref.shape[0]
    f, c, t = lax.axis_index("fsdp"), lax.axis_index("ctx"), lax.axis_index("tp")
    core, chip = lax.rem(c, 2), c // 2
    sibling = c + 1 - 2 * core
    count, rows, width = h_ref.shape
    local = weights.shape[-1]
    heads = local // HEAD_DIM
    scale = 1.0 / math.sqrt(HEAD_DIM)
    columns = part_ref.shape[-1]

    def blocks(k):
        return pl.ds(*GROUPS[k])

    def x_copy(layer, k, ahead):
        return remote(
            weights.at[layer, blocks(k), f, chip, core],
            weights.at[layer, blocks(k), f, chip, core],
            x_sems,
            (layer, k, ahead - 1),
            fsdp=lax.rem(f + ahead, nf),
        )

    def x_arrived(layer, k, ahead):
        source = lax.rem(f + nf - ahead, nf)
        block = weights.at[layer, blocks(k), source, chip, core]
        remote(block, block, x_sems, (layer, k, ahead - 1), fsdp=source).wait_recv()

    def y_copy(layer, k, ahead, over, at):
        source = lax.rem(f + nf - ahead, nf)
        block = weights.at[layer, blocks(k), source, at, core]
        peer = lax.rem(chip + over, chips) * 2 + core
        return remote(block, block, y_sems, (layer, k, ahead - 1, over - 1), ctx=peer)

    def pair_copy(layer, k, ahead, half):
        source = lax.rem(f + nf - ahead, nf)
        block = weights.at[layer, blocks(k), source, :, half]
        return remote(block, block, pair_sems, (layer, k, ahead - 1), ctx=sibling)

    def pass_y(layer, k):
        for ahead in range(1, nf):
            x_arrived(layer, k, ahead)
            for over in range(1, chips):
                y_copy(layer, k, ahead, over, chip).start()

    def pass_pair(layer, k):
        for ahead in range(1, nf):
            for over in range(1, chips):
                y_copy(layer, k, ahead, over, lax.rem(chip + chips - over, chips)).wait_recv()
            pair_copy(layer, k, ahead, core).start()

    def arrived(layer, k):
        for ahead in range(1, nf):
            pair_copy(layer, k, ahead, 1 - core).wait_recv()

    def stage_copies(layer):
        return [
            pltpu.make_async_copy(source.at[layer], stage, own_sems.at[1 + k])
            for k, (source, stage) in enumerate(
                ((attend_ref, stage_a), (hidden_ref, stage_h), (output_ref, stage_o))
            )
        ]

    def quarters(value):
        return value.astype(LOW).reshape(chips, 2, -1, local)

    def send_x(layer, k):
        for ahead in range(1, nf):
            x_copy(layer, k, ahead).start()

    def lower_attend(layer):
        copies = stage_copies(layer)
        copies[0].wait()
        copies[2].wait()
        for k in range(3):
            weights[layer, QUERY + k, f] = quarters(stage_a[k])
        weights[layer, OUT, f] = quarters(stage_o[0])
        send_x(layer, 0)

    def lower_rest(layer):
        stage_copies(layer)[1].wait()
        tiles = local // LANES
        size = 4 * tiles * 16
        order = interleave(4, tiles, back=True)
        quarter = weights.shape[-2]

        def split(r, carry):
            rows_in = pl.ds(pl.multiple_of(r * size, size), size)
            value = dot(order, stage_h[rows_in].astype(LOW)).astype(LOW)
            part = (r * 16) // quarter
            at = pl.ds(pl.multiple_of(lax.rem(r * 16, quarter), 16), 16)
            for k in range(4):
                for n in range(tiles):
                    first = (k * tiles + n) * 16
                    weights[
                        layer, HIDDEN + k, f, part // 2, lax.rem(part, 2), at, n * LANES : (n + 1) * LANES
                    ] = value[first : first + 16]
            return carry

        lax.fori_loop(0, stage_h.shape[0] // size, split, 0, unroll=2)
        send_x(layer, 1)
        for k in range(4):
            weights[layer, MLP + k, f] = quarters(stage_o[1 + k])
        send_x(layer, 2)

    chunk = cond_buf.shape[-1]

    def cond_copy(j):
        return pltpu.make_async_copy(
            cond_ref.at[:, pl.ds(pl.multiple_of(j * chunk, LANES), chunk)],
            cond_buf.at[lax.rem(j, 2)],
            cond_sems.at[lax.rem(j, 2)],
        )

    def multiply(j, carry):
        @pl.when(j + 1 < columns // chunk)
        def _():
            cond_copy(j + 1).start()

        cond_copy(j).wait()
        product = dot(cond_in_ref[...], cond_buf[lax.rem(j, 2)].astype(LOW))
        for n in range(images):
            part_ref[
                n // count, n % count : n % count + 1, pl.ds(pl.multiple_of(j * chunk, LANES), chunk)
            ] = product[n : n + 1]
        return carry

    def ends_copy(ahead, at):
        return remote(ends.at[at], ends.at[at], ends_sems, (ahead - 1,), fsdp=lax.rem(f + ahead, nf))

    def both_ends():
        return ends[...].reshape(width, LANES)

    def store_copy(layer):
        return pltpu.make_async_copy(weights.at[layer], full_ref.at[layer], own_sems.at[4 + layer])

    def share_mods():
        for ahead in range(1, nf):
            peer = lax.rem(f + ahead, nf)
            remote(part_ref.at[peer], mods_got.at[ahead - 1], mods_x_sems, (ahead - 1,), fsdp=peer).start()

    def finish_mods():
        total = part_ref[f]
        for ahead in range(1, nf):
            peer = lax.rem(f + ahead, nf)
            remote(part_ref.at[peer], mods_got.at[ahead - 1], mods_x_sems, (ahead - 1,), fsdp=peer).wait()
            total = total + mods_got[ahead - 1]

        def at(k):
            return mods_ref.at[:, pl.ds(pl.multiple_of(k * columns, LANES), columns)]

        mods_ref[:, pl.ds(pl.multiple_of(t * columns, LANES), columns)] = total
        for ahead in range(1, nt):
            remote(at(t), at(t), mods_t_sems, (ahead - 1,), tp=lax.rem(t + ahead, nt)).start()
        for ahead in range(1, nt):
            source = lax.rem(t + nt - ahead, nt)
            remote(at(t), at(t), mods_t_sems, (ahead - 1,), tp=source).wait_send()
            remote(at(source), at(source), mods_t_sems, (ahead - 1,), tp=source).wait_recv()

    def mod(k, g, layer):
        return row(mods_ref, g, 6 * layer + k, width)

    def total_a(g):
        return Total(nt, g, send_a, first_a, full_a, a_sems)

    def total_m(g):
        return Total(nt, g, send_m, first_m, full_m, m_sems)

    def kv_copy(layer, g, ahead, at):
        block = kv.at[layer, g, at]
        return remote(block, block, kv_sems, (layer, g, ahead - 1), ctx=lax.rem(c + ahead, nc))

    @pl.when(step == 0)
    def _():
        for copy in stage_copies(0):
            copy.start()
        cond_copy(0).start()
        used = jnp.concatenate([patch_ref[...], head_ref[...]], 0)
        unused = jnp.zeros((LANES - used.shape[0], used.shape[1]), jnp.float32)
        ends[f] = jnp.transpose(jnp.concatenate([used, unused], 0)).astype(LOW)
        meet(sizes)
        for ahead in range(1, nf):
            ends_copy(ahead, f).start()
        lower_attend(0)
        lax.fori_loop(0, columns // chunk, multiply, 0)
        share_mods()
        pass_y(0, 0)
        lower_rest(0)
        for copy in stage_copies(1):
            copy.start()
        pass_pair(0, 0)
        for ahead in range(1, nf):
            ends_copy(ahead, f).wait_send()
            ends_copy(ahead, lax.rem(f + nf - ahead, nf)).wait_recv()
        for g in range(count):
            h_ref[g] = dot_nt(noisy_ref[g], both_ends()) + pos_ref[...]
        finish_mods()
        pass_y(0, 1)

    def matrix(k):
        return weights[step, k].reshape(width, local)

    def begin(g):
        h = h_ref[g]
        keep_h[0, g] = h
        normed, _ = norm_parts(h)
        u_in = (normed * (1.0 + mod(1, g, step)) + mod(0, g, step)).astype(LOW)
        kv[step, g, c, :, :local] = dot(u_in, matrix(KEY)).astype(LOW)
        kv[step, g, c, :, local:] = dot(u_in, matrix(VALUE)).astype(LOW)
        for ahead in range(1, nc):
            kv_copy(step, g, ahead, c).start()
        q_ref[g] = dot(u_in, matrix(QUERY)).astype(LOW)

    def last_branch(g):
        branch = total_m(g).get()
        keep_m[0, g] = branch
        h_ref[g] = h_ref[g] + mod(5, g, step - 1) * branch.astype(jnp.float32)

    @pl.when(step < layers)
    def _():
        arrived(step, 0)

    def finish(g):
        normed, inv = norm_parts(h_ref[g])
        shift, scale_row = (row(mods_ref, g, 6 * layers + k, width) for k in range(2))
        final_in = (normed * (1.0 + scale_row) + shift).astype(LOW)
        final_out[g] = final_in
        lane = lax.broadcasted_iota(jnp.int32, (rows, LANES), 1)
        inside = (lane >= target_first) & (lane < target_first + target_count)
        diff = jnp.where(inside, dot(final_in, both_ends()) - target_ref[g], 0.0)
        squares = jnp.sum((diff * diff).reshape(rows // 8, 8, LANES), 0)
        loss_out[...] = squares if g == 0 else loss_out[...] + squares
        d_pred = (2.0 * diff).astype(LOW)
        dpred_out[g] = d_pred
        d_h, d_shift, d_scale = norm_back(dot_nt(d_pred, both_ends()), normed, inv, scale_row)
        dh_out[g] = d_h
        put_row(dmods_out, g, 0, width, d_shift)
        put_row(dmods_out, g, 1, width, d_scale)

    for g in range(count):

        @pl.when(step >= 1)
        def _():
            last_branch(g)

        @pl.when(step == layers)
        def _():
            finish(g)

        @pl.when(step < layers)
        def _():
            begin(g)

    @pl.when(step + 1 < layers)
    def _():
        lower_attend(step + 1)
        lower_rest(step + 1)

    @pl.when(step + 2 < layers)
    def _():
        for copy in stage_copies(step + 2):
            copy.start()

    @pl.when(step < layers)
    def _():
        pass_y(step, 2)
        pass_pair(step, 1)
        for g in range(count):
            for ahead in range(1, nc):
                kv_copy(step, g, ahead, c).wait_send()
                kv_copy(step, g, ahead, lax.rem(c + nc - ahead, nc)).wait_recv()
            keep_q[0, g] = q_ref[g]
            keep_kv[0, g] = kv[step, g]
            keys = kv[step, g, :, :, :local].reshape(nc * rows, local)
            values = kv[step, g, :, :, local:].reshape(nc * rows, local)
            scores = dot_nt(spread(q_ref[g], heads), keys) * scale
            expo = jnp.exp(scores - jnp.max(scores, -1, keepdims=True))
            probs = expo / jnp.sum(expo, -1, keepdims=True)
            keep_p[0, g] = probs
            attended = pick(dot(probs.astype(LOW), values), heads).astype(LOW)
            keep_att[0, g] = attended
            total_a(g).scatter(dot_nt(attended, matrix(OUT)))
        pass_pair(step, 2)
        for g in range(count):
            total_a(g).share()
        arrived(step, 1)

    @pl.when(step + 1 < layers)
    def _():
        pass_y(step + 1, 0)

    @pl.when(step < layers)
    def _():
        for g in range(count):
            branch = total_a(g).get()
            keep_a[0, g] = branch
            h_mid = h_ref[g] + mod(2, g, step) * branch.astype(jnp.float32)
            keep_mid[0, g] = h_mid
            h_ref[g] = h_mid
            normed, _ = norm_parts(h_mid)
            w_in = (normed * (1.0 + mod(4, g, step)) + mod(3, g, step)).astype(LOW)
            if g == 0:
                arrived(step, 2)
                store_copy(step).start()
            part = jnp.zeros((rows, width), jnp.float32)
            for k in range(4):
                pre = dot(w_in, matrix(HIDDEN + k))
                keep_pre[0, g, k] = pre
                part = part + dot_nt(gelu_parts(pre)[0].astype(LOW), matrix(MLP + k))
            total_m(g).scatter(part)

    @pl.when(step + 1 < layers)
    def _():
        pass_pair(step + 1, 0)
        pass_y(step + 1, 1)

    @pl.when(step < layers)
    def _():
        for g in range(count):
            total_m(g).share()

    @pl.when(step == layers)
    def _():
        mods_out[...] = mods_ref[...]

        def drain(layer, carry):
            store_copy(layer).wait()
            for k in range(len(GROUPS)):
                for ahead in range(1, nf):
                    x_copy(layer, k, ahead).wait_send()
                    for over in range(1, chips):
                        y_copy(layer, k, ahead, over, chip).wait_send()
                    pair_copy(layer, k, ahead, core).wait_send()
            return carry

        lax.fori_loop(0, layers, drain, 0)


def forward(mesh, images, target_at, cond_in, cond, patch, head, noisy, pos, target, hidden, attend, output):
    sizes = dict(mesh.shape)
    nf, nc, nt = sizes["fsdp"], sizes["ctx"], sizes["tp"]
    chips = nc // 2
    count, rows, _ = noisy.shape
    width, columns = pos.shape[1], cond.shape[1]
    layers, _, shard, local = attend.shape
    blocks, quarter = 4 + attend.shape[1] + output.shape[1], shard // nc
    heads = local // HEAD_DIM
    tokens = count * rows
    others, overs = max(nf - 1, 1), max(chips - 1, 1)
    f32 = jnp.float32

    def kept(shape, dtype, late=0):
        spec = pl.BlockSpec(
            (1, *shape), lambda i: (jnp.clip(i - late, 0, layers - 1),) + (0,) * len(shape)
        )
        return jax.ShapeDtypeStruct((layers, *shape), dtype), spec

    saves = [
        kept((count, rows, width), f32),
        kept((count, rows, width), f32),
        kept((count, rows, width), LOW),
        kept((count, rows, width), LOW, 1),
        kept((count, rows, local), LOW),
        kept((count, nc, rows, 2 * local), LOW),
        kept((count, heads * rows, nc * rows), f32),
        kept((count, rows, local), LOW),
        kept((count, 4, rows, local), f32),
    ]
    anywhere = pl.BlockSpec(memory_space=pl.ANY)
    vmem = pl.BlockSpec(memory_space=pltpu.VMEM)
    whole = pltpu.VMEM((count, nt, rows // nt, width), LOW)
    first = pltpu.VMEM((count, nt - 1, rows // nt, width), LOW)
    dma = pltpu.SemaphoreType.DMA
    return pl.pallas_call(
        functools.partial(forward_kernel, sizes, images, *target_at),
        grid=(layers + 1,),
        out_shape=[
            jax.ShapeDtypeStruct((count, rows, width), f32),
            jax.ShapeDtypeStruct((count, nt * columns), f32),
            jax.ShapeDtypeStruct((count, 2 * width), f32),
            jax.ShapeDtypeStruct((8, LANES), f32),
            jax.ShapeDtypeStruct((count, rows, LANES), LOW),
            jax.ShapeDtypeStruct((count, rows, width), LOW),
            jax.ShapeDtypeStruct((layers, blocks, nf, chips, 2, quarter, local), LOW),
            *(shape for shape, _ in saves),
        ],
        in_specs=[vmem, anywhere, *[vmem] * 5, anywhere, anywhere, anywhere],
        out_specs=[*[vmem] * 6, anywhere, *(spec for _, spec in saves)],
        scratch_shapes=[
            pltpu.VMEM((layers, blocks, nf, chips, 2, quarter, local), LOW),
            *(pltpu.VMEM(w.shape[1:], f32) for w in (hidden, attend, output)),
            pltpu.VMEM((nf, count, columns), f32),
            pltpu.VMEM((2, shard, 512), f32),
            pltpu.VMEM((nf, shard, LANES), LOW),
            pltpu.VMEM((layers, count, nc, rows, 2 * local), LOW),
            pltpu.VMEM((count, rows, width), f32),
            pltpu.VMEM((count, rows, local), LOW),
            pltpu.VMEM((count, nt * columns), f32),
            pltpu.VMEM((others, count, columns), f32),
            whole, first, whole, whole, first, whole,
            dma((2, layers, 3, others)),
            dma((2, layers, 3, others, overs)),
            dma((2, layers, 3, others)),
            dma((4 + layers,)),
            dma((2, layers, count, nc - 1)),
            dma((2, 2, count, nt - 1)),
            dma((2, 2, count, nt - 1)),
            dma((2, others)),
            dma((2, nt - 1)),
            dma((2,)),
            dma((2, others)),
        ],
        compiler_params=pltpu.CompilerParams(
            collective_id=1, has_side_effects=True, vmem_limit_bytes=56 * 2**20
        ),
        cost_estimate=pl.CostEstimate(
            flops=2 * tokens * width * blocks * local * layers,
            bytes_accessed=layers * blocks * width * local * 4,
            transcendentals=0,
        ),
        name="forward_layers",
    )(cond_in, cond, patch, head, noisy, pos, target, hidden, attend, output)


def halves(value):
    high = value.astype(LOW).astype(jnp.float32)
    return high, value - high


def backward_kernel(
    sizes, images, dh0_ref, mods_ref, dmods_end_ref, loss_ref, noisy_ref, dpred_ref, final_ref,
    slope_c_ref, slope_a_ref, cond_in_ref, swish_ref, onehot_ref, freqs_ref, time_ref, cond_ref,
    w_ref, keep_h, keep_mid, keep_a, keep_m, keep_q, keep_kv, keep_p, keep_att, keep_pre,
    grads_ref, small_ref, dcols_out, dcvec_ref, dact_ref, stat_ref,
    dh_ref, dmid_ref, h_ref, act_ref, dpre_ref, branch_ref, dba_ref, dqkv_ref, dm_ref,
    send_w, first_w, full_w, send_u, first_u, full_u, kv_send, kv_got,
    grads, pair_got, x_send, x_got, y_send, y_got, done, square,
    s_grads, s_pair, s_send, s_x, s_y_send, s_y, s_done,
    c_got, dcols_ref, cond_buf, product, gram, silu_got, swish_got, stat_got,
    w_sems, u_sems, kv_sems, pair_sems, x_sems, y_sems, end_sems, own_sems,
    s_sems, s_x_sems, s_y_sems, s_own_sems, c_sems, f_sems, cond_sems, t_sems, a_sems, n_sems,
):
    nf, nc, nt = sizes["fsdp"], sizes["ctx"], sizes["tp"]
    chips = nc // 2
    layers, _, _, half, local = grads_ref.shape
    step = pl.program_id(0)
    new = lax.rem(step, 2)
    old = 1 - new
    f, c, t = lax.axis_index("fsdp"), lax.axis_index("ctx"), lax.axis_index("tp")
    core, chip = lax.rem(c, 2), c // 2
    sibling = c + 1 - 2 * core
    count, rows, width = dh_ref.shape
    heads = local // HEAD_DIM
    scale = 1.0 / math.sqrt(HEAD_DIM)
    piece = min(64, half)
    columns = cond_ref.shape[1]
    f32 = jnp.float32
    A, H, M = 0, 1, 2
    layer = layers - 1 - step

    def blocks(k):
        return pl.ds(*GROUPS[k])

    def pieces(k, body):
        parts = half // piece

        def one(j, carry):
            body(j // parts, pl.ds(pl.multiple_of(lax.rem(j, parts) * piece, piece), piece))
            return carry

        low, size = GROUPS[k]
        lax.fori_loop(low * parts, (low + size) * parts, one, 0)

    def pair_copy(k, at):
        return remote(
            grads.at[blocks(k), :, 1 - core], pair_got.at[at, blocks(k)], pair_sems, (at, k), ctx=sibling
        )

    def x_copy(k, at, ahead):
        return remote(
            x_send.at[ahead - 1, blocks(k)], x_got.at[at, ahead - 1, blocks(k)],
            x_sems, (at, k, ahead - 1), fsdp=lax.rem(f + ahead, nf),
        )

    def y_copy(k, at, ahead):
        return remote(
            y_send.at[blocks(k)], y_got.at[at, ahead - 1, blocks(k)],
            y_sems, (at, k, ahead - 1), ctx=lax.rem(chip + ahead, chips) * 2 + core,
        )

    def end_copy(k, at, layer, to):
        return remote(done.at[blocks(k)], grads_ref.at[layer, blocks(k), to], end_sems, (at, k), ctx=sibling)

    def own_copy(k, layer):
        return pltpu.make_async_copy(done.at[blocks(k)], grads_ref.at[layer, blocks(k), core], own_sems.at[k])

    def stage_2(k, at):
        pair_copy(k, at).wait()
        for ahead in range(1, nf):
            peer = lax.rem(f + ahead, nf)

            def add(b, r):
                total = grads[b, peer, core, r].astype(f32) + pair_got[at, b, peer, r].astype(f32)
                x_send[ahead - 1, b, r] = total.astype(LOW)

            pieces(k, add)
            x_copy(k, at, ahead).start()

    def stage_3(k, at):
        for ahead in range(1, nf):
            x_copy(k, at, ahead).wait()

        def add(b, r):
            total = grads[b, f, core, r].astype(f32) + pair_got[at, b, f, r].astype(f32)
            for ahead in range(1, nf):
                total = total + x_got[at, ahead - 1, b, r].astype(f32)
            y_send[b, r] = total.astype(LOW)

        pieces(k, add)
        for ahead in range(1, chips):
            y_copy(k, at, ahead).start()

    def end_wait(k, at, layer):
        own_copy(k, layer).wait()
        end_copy(k, at, layer, core).wait_send()
        end_copy(k, at, layer, 1 - core).wait_recv()

    def stage_4(k, at, layer):
        for ahead in range(1, chips):
            y_copy(k, at, ahead).wait()

        def add(b, r):
            total = y_send[b, r].astype(f32)
            for ahead in range(1, chips):
                total = total + y_got[at, ahead - 1, b, r].astype(f32)
            low = total.astype(LOW)
            done[b, r] = low
            total = low.astype(f32)
            square[...] += jnp.sum((total * total).reshape(piece // 8, 8, local), 0)

        pieces(k, add)
        own_copy(k, layer).start()
        end_copy(k, at, layer, core).start()

    def when(low, high, body):
        pl.when((step >= low) & (step <= high))(body)

    def matrix(k):
        return w_ref[0, k].reshape(width, local)

    def mod(k, g, layer):
        return row(mods_ref, g, 6 * layer + k, width)

    def put_dmod(k, g, layer, value):
        put_row(dm_ref, g, 6 * layer + k, width, value)

    def keep_grad(k, value):
        grads[k] = value.astype(LOW).reshape(nf, 2, half, local)

    def total_w(g):
        return Total(nt, g, send_w, first_w, full_w, w_sems)

    def total_u(g):
        return Total(nt, g, send_u, first_u, full_u, u_sems)

    def both(ref):
        value = ref[...]
        return value.reshape(count * rows, value.shape[-1])

    @pl.when(step == 0)
    def _():
        meet(sizes)
        dh_ref[...] = dh0_ref[...]
        square[...] = jnp.zeros_like(square)
        for g in range(count):
            put_row(dm_ref, g, 3 * layers, 2 * width, dmods_end_ref[g : g + 1])

    def finish_input(g):
        normed, inv = norm_parts(h_ref[g])
        d_h, d_shift, d_scale = norm_back(
            total_u(g).get().astype(f32), normed, inv, mod(1, g, layer + 1)
        )
        put_dmod(0, g, layer + 1, d_shift)
        put_dmod(1, g, layer + 1, d_scale)
        dh_ref[g] = d_h + dmid_ref[g]

    def mlp_back(g):
        grad = dh_ref[g]
        put_dmod(5, g, layer, jnp.sum(grad * keep_m[0, g].astype(f32), 0, keepdims=True))
        branch = (mod(5, g, layer) * grad).astype(LOW)
        branch_ref[g] = branch
        part = jnp.zeros((rows, width), f32)
        for k in range(4):
            value, slope = gelu_parts(keep_pre[0, g, k])
            act_ref[k, g] = value.astype(LOW)
            d_pre = (dot(branch, matrix(MLP + k)) * slope).astype(LOW)
            dpre_ref[k, g] = d_pre
            part = part + dot_nt(d_pre, matrix(HIDDEN + k))
        total_w(g).scatter(part)

    for g in range(count):
        when(1, layers, lambda: finish_input(g))
        when(0, layers - 1, lambda: mlp_back(g))

    def share(own, slots, sems, axis, size, where=()):
        me = lax.axis_index(axis)
        for ahead in range(1, size):
            remote(own, slots.at[me], sems, (*where, ahead - 1), **{axis: lax.rem(me + ahead, size)}).start()

    def shared(own, slots, sems, axis, size, where=()):
        me = lax.axis_index(axis)
        for ahead in range(1, size):
            remote(own, slots.at[me], sems, (*where, ahead - 1), **{axis: lax.rem(me + ahead, size)}).wait_send()
            source = lax.rem(me + size - ahead, size)
            remote(slots.at[source], slots.at[source], sems, (*where, ahead - 1), **{axis: source}).wait_recv()

    def slot_sum(slots, size):
        total = slots[0]
        for k in range(1, size):
            total = total + slots[k]
        return total

    chunk = cond_buf.shape[-1]

    def cond_copy(j):
        return pltpu.make_async_copy(
            cond_ref.at[:, pl.ds(pl.multiple_of(j * chunk, LANES), chunk)],
            cond_buf.at[lax.rem(j, 2)],
            cond_sems.at[lax.rem(j, 2)],
        )

    def small_pair():
        return remote(s_grads.at[:, 1 - core], s_pair, s_sems, (0,), ctx=sibling)

    def small_x(ahead):
        return remote(
            s_send.at[ahead - 1], s_x.at[ahead - 1], s_x_sems, (ahead - 1,), fsdp=lax.rem(f + ahead, nf)
        )

    def small_y(ahead):
        return remote(
            s_y_send, s_y.at[ahead - 1], s_y_sems, (ahead - 1,), ctx=lax.rem(chip + ahead, chips) * 2 + core
        )

    def small_end(to):
        return remote(s_done, small_ref.at[to], s_sems, (1,), ctx=sibling)

    @pl.when(step == layers)
    def _():
        cond_copy(0).start()
        c_got[c] = dm_ref[:, pl.ds(pl.multiple_of(t * columns, LANES), columns)]
        share(c_got.at[c], c_got, c_sems, "ctx", nc)
        high, low = halves(both(dh_ref))
        noisy = noisy_ref[...]
        small = dot_tn(high.astype(LOW), noisy) + dot_tn(low.astype(LOW), noisy)
        small = small + dot_tn(final_ref[...], dpred_ref[...])
        s_grads[...] = small.reshape(s_grads.shape)
        small_pair().start()

    when(1, layers, lambda: stage_2(A, old))
    when(2, layers, lambda: (pl.when(step >= 3)(lambda: end_wait(A, old, layer + 3)), stage_4(A, new, layer + 2))[1])
    when(2, layers, lambda: stage_3(M, old))

    @pl.when(step == layers)
    def _():
        small_pair().wait()
        for ahead in range(1, nf):
            peer = lax.rem(f + ahead, nf)
            s_send[ahead - 1] = s_grads[peer, core] + s_pair[peer]
            small_x(ahead).start()
        shared(c_got.at[c], c_got, c_sems, "ctx", nc)
        dcols_ref[f] = slot_sum(c_got, nc)
        share(dcols_ref.at[f], dcols_ref, f_sems, "fsdp", nf)

    def stacked_input(ref, first):
        normed, _ = norm_parts(ref[0])
        parts = [
            normed[g] * (1.0 + mod(first + 1, g, layer)) + mod(first, g, layer) for g in range(count)
        ]
        return jnp.concatenate(parts, 0).astype(LOW)

    def mlp_grads():
        w_in = stacked_input(keep_mid, 3)
        for k in range(4):
            keep_grad(HIDDEN + k, dot_tn(w_in, dpre_ref[k].reshape(count * rows, local)))
        pair_copy(H, new).start()
        branch = both(branch_ref)
        for k in range(4):
            keep_grad(MLP + k, dot_tn(branch, act_ref[k].reshape(count * rows, local)))
        pair_copy(M, new).start()
        for g in range(count):
            total_w(g).share()
        stage_2(H, new)
        stage_2(M, new)

    when(0, layers - 1, mlp_grads)
    when(1, layers, lambda: (pl.when(step >= 2)(lambda: end_wait(H, new, layer + 2)), stage_4(H, old, layer + 1))[1])

    def attention_back(g):
        normed, inv = norm_parts(keep_mid[0, g])
        d_mid, d_shift, d_scale = norm_back(total_w(g).get().astype(f32), normed, inv, mod(4, g, layer))
        d_mid = d_mid + dh_ref[g]
        dmid_ref[g] = d_mid
        put_dmod(3, g, layer, d_shift)
        put_dmod(4, g, layer, d_scale)
        put_dmod(2, g, layer, jnp.sum(d_mid * keep_a[0, g].astype(f32), 0, keepdims=True))
        branch = (mod(2, g, layer) * d_mid).astype(LOW)
        dba_ref[g] = branch
        grad = spread(dot(branch, matrix(OUT)).astype(LOW), heads)
        query = spread(keep_q[0, g], heads)
        keys = keep_kv[0, g, :, :, :local].reshape(nc * rows, local)
        values = keep_kv[0, g, :, :, local:].reshape(nc * rows, local)
        probs = keep_p[0, g]
        d_probs = dot_nt(grad, values)
        d_scores = (probs * (d_probs - jnp.sum(d_probs * probs, -1, keepdims=True))).astype(LOW)
        d_values = dot_tn(probs.astype(LOW), grad)
        d_keys = dot_tn(d_scores, query) * scale
        kv_send[g, :, :, :local] = d_keys.astype(LOW).reshape(nc, rows, local)
        kv_send[g, :, :, local:] = d_values.astype(LOW).reshape(nc, rows, local)
        for ahead in range(1, nc):
            kv_copy(g, ahead).start()
        d_query = pick(dot(d_scores, keys), heads) * scale
        dqkv_ref[0, g] = d_query.astype(LOW)

    def kv_copy(g, ahead):
        peer = lax.rem(c + ahead, nc)
        return remote(kv_send.at[g, peer], kv_got.at[new, g, ahead - 1], kv_sems, (new, g, ahead - 1), ctx=peer)

    @pl.when(step < layers)
    def _():
        for g in range(count):
            attention_back(g)

    when(1, layers, lambda: stage_3(A, old))
    when(0, 0, lambda: stage_3(H, new))

    @pl.when(step < layers)
    def _():
        for g in range(count):
            total = kv_send[g, c].astype(f32)
            for ahead in range(1, nc):
                kv_copy(g, ahead).wait()
                total = total + kv_got[new, g, ahead - 1].astype(f32)
            dqkv_ref[1, g] = total[:, :local].astype(LOW)
            dqkv_ref[2, g] = total[:, local:].astype(LOW)
            part = dot_nt(dqkv_ref[0, g], matrix(QUERY))
            part = part + dot_nt(dqkv_ref[1, g], matrix(KEY))
            part = part + dot_nt(dqkv_ref[2, g], matrix(VALUE))
            total_u(g).scatter(part)
        h_ref[...] = keep_h[0]
        u_in = stacked_input(keep_h, 0)
        for k in range(3):
            keep_grad(QUERY + k, dot_tn(u_in, dqkv_ref[k].reshape(count * rows, local)))
        keep_grad(OUT, dot_tn(both(dba_ref), keep_att[0].reshape(count * rows, local)))
        pair_copy(A, new).start()
        for g in range(count):
            total_u(g).share()

    when(1, layers - 1, lambda: stage_3(H, new))
    when(0, 0, lambda: stage_3(M, new))

    images_row = max(8, images)

    def own_gram(ref):
        return dot_nt(ref[...], ref[...])

    @pl.when(step == layers)
    def _():
        shared(dcols_ref.at[f], dcols_ref, f_sems, "fsdp", nf)
        product[...] = jnp.zeros_like(product)
        gram[...] = jnp.zeros_like(gram)
        index = lax.broadcasted_iota(jnp.int32, (LANES, chunk), 0)

        def multiply(j, carry):
            @pl.when(j + 1 < columns // chunk)
            def _():
                cond_copy(j + 1).start()

            pair = jnp.zeros((LANES, chunk), f32)
            for n in range(images):
                source = dcols_ref[
                    n // count, n % count : n % count + 1, pl.ds(pl.multiple_of(j * chunk, LANES), chunk)
                ]
                high, low = halves(source)
                pair = jnp.where(index == n, high, pair)
                pair = jnp.where(index == images + n, low, pair)
            pair = pair.astype(LOW)
            dcols_out[:, pl.ds(pl.multiple_of(j * chunk, LANES), chunk)] = pair[: dcols_out.shape[0]]
            gram[...] += dot_nt(pair, pair)
            cond_copy(j).wait()
            product[...] += dot_nt(cond_buf[lax.rem(j, 2)].astype(LOW), pair)
            return carry

        lax.fori_loop(0, columns // chunk, multiply, 0)
        total = product[...]
        total = jnp.transpose(total + pltpu.roll(total, LANES - images, 1))[:images_row]
        silu_got[t] = total
        share(silu_got.at[t], silu_got, t_sems, "tp", nt)
        for ahead in range(1, nf):
            small_x(ahead).wait()
        total = s_grads[f, core] + s_pair[f]
        for ahead in range(1, nf):
            total = total + s_x[ahead - 1]
        s_y_send[...] = total
        for ahead in range(1, chips):
            small_y(ahead).start()
        shared(silu_got.at[t], silu_got, t_sems, "tp", nt)
        d_cvec = slot_sum(silu_got, nt) * slope_c_ref[...]
        high, low = halves(d_cvec)
        pair = jnp.concatenate([high, low], 0).astype(LOW)
        dcvec_ref[...] = pair
        fixed = own_gram(swish_ref) + own_gram(onehot_ref)
        time_label = jnp.sum(dot_nt(pair, pair) * fixed)
        total = dot(pair, time_ref[...].astype(LOW))
        swish_got[f] = total[:images_row] + total[images_row:]
        share(swish_got.at[f], swish_got, a_sems, "fsdp", nf)
        shared(swish_got.at[f], swish_got, a_sems, "fsdp", nf)
        d_act = slot_sum(swish_got, nf) * slope_a_ref[...]
        high, low = halves(d_act)
        pair = jnp.concatenate([high, low], 0).astype(LOW)
        dact_ref[...] = pair
        freq = jnp.sum(dot_nt(pair, pair) * own_gram(freqs_ref))
        size = cond_in_ref.shape[0]
        cond = jnp.sum(gram[:size, :size] * own_gram(cond_in_ref))
        stat_ref[...] = jnp.full(
            stat_ref.shape, cond / nc + time_label / (nt * nc) + freq / (nf * nt * nc), f32
        )

    when(1, layers, lambda: (pl.when(step >= 2)(lambda: end_wait(M, new, layer + 2)), stage_4(M, old, layer + 1))[1])

    @pl.when(step == layers)
    def _():
        end_wait(A, new, 1)
        stage_4(A, old, 0)
        total = s_y_send[...]
        for ahead in range(1, chips):
            small_y(ahead).wait()
            total = total + s_y[ahead - 1]
        s_done[...] = total
        own = pltpu.make_async_copy(s_done, small_ref.at[core], s_own_sems.at[0])
        own.start()
        small_end(core).start()
        part = jnp.sum(square[...]) / chips + jnp.sum(total * total) / (nt * chips)
        index = lax.broadcasted_iota(jnp.int32, stat_ref.shape, 0)
        stat_ref[...] = jnp.where(index < 8, stat_ref[...] + part, jnp.sum(loss_ref[...]) / nt)
        for k, (axis, size) in enumerate((("ctx", nc), ("fsdp", nf), ("tp", nt))):
            me = lax.axis_index(axis)
            slots = stat_got.at[k]
            slots[me] = stat_ref[...]
            share(slots.at[me], slots, n_sems, axis, size, (k,))
            shared(slots.at[me], slots, n_sems, axis, size, (k,))
            stat_ref[...] = slot_sum(slots, size)
        for k in range(3):
            end_wait(k, old, 0)
        own.wait()
        small_end(core).wait_send()
        small_end(1 - core).wait_recv()


def backward(mesh, images, dh0, mods, dmods_end, loss, noisy, dpred, final_in, slopes, rights, time, cond, full, saved):
    sizes = dict(mesh.shape)
    nf, nc, nt = sizes["fsdp"], sizes["ctx"], sizes["tp"]
    chips = nc // 2
    others, overs = max(nf - 1, 1), max(chips - 1, 1)
    count, rows, width = dh0.shape
    layers, blocks, _, local = full.shape
    shard, columns = cond.shape
    half = shard // 2
    tokens = count * rows
    padded = max(8, images)
    f32 = jnp.float32

    def per_layer(array):
        shape = array.shape[1:]
        return pl.BlockSpec(
            (1, *shape), lambda i: (jnp.maximum(layers - 1 - i, 0),) + (0,) * len(shape)
        )

    anywhere = pl.BlockSpec(memory_space=pl.ANY)
    vmem = pl.BlockSpec(memory_space=pltpu.VMEM)
    whole = pltpu.VMEM((count, nt, rows // nt, width), LOW)
    first = pltpu.VMEM((count, nt - 1, rows // nt, width), LOW)
    image = pltpu.VMEM((count, rows, width), f32)
    image_low = pltpu.VMEM((count, rows, width), LOW)
    mlp = pltpu.VMEM((4, count, rows, local), LOW)
    small = (half, LANES)
    dma = pltpu.SemaphoreType.DMA
    return pl.pallas_call(
        functools.partial(backward_kernel, sizes, images),
        grid=(layers + 1,),
        out_shape=[
            jax.ShapeDtypeStruct((layers, blocks, 2, half, local), LOW),
            jax.ShapeDtypeStruct((2, half, LANES), f32),
            jax.ShapeDtypeStruct((-(-2 * images // 16) * 16, columns), LOW),
            jax.ShapeDtypeStruct((2 * padded, shard), LOW),
            jax.ShapeDtypeStruct((2 * padded, width), LOW),
            jax.ShapeDtypeStruct((16, LANES), f32),
        ],
        in_specs=[vmem] * 14 + [anywhere, per_layer(full), *(per_layer(s) for s in saved)],
        out_specs=[anywhere, anywhere, vmem, vmem, vmem, vmem],
        scratch_shapes=[
            image, image, image, mlp, mlp, image_low, image_low,
            pltpu.VMEM((3, count, rows, local), LOW),
            pltpu.VMEM(mods.shape, f32),
            whole, first, whole, whole, first, whole,
            pltpu.VMEM((count, nc, rows, 2 * local), LOW),
            pltpu.VMEM((2, count, nc - 1, rows, 2 * local), LOW),
            pltpu.VMEM((blocks, nf, 2, half, local), LOW),
            pltpu.VMEM((2, blocks, nf, half, local), LOW),
            pltpu.VMEM((others, blocks, half, local), LOW),
            pltpu.VMEM((2, others, blocks, half, local), LOW),
            pltpu.VMEM((blocks, half, local), LOW),
            pltpu.VMEM((2, overs, blocks, half, local), LOW),
            pltpu.VMEM((blocks, half, local), LOW),
            pltpu.VMEM((8, local), f32),
            pltpu.VMEM((nf, 2, *small), f32),
            pltpu.VMEM((nf, *small), f32),
            pltpu.VMEM((others, *small), f32),
            pltpu.VMEM((others, *small), f32),
            pltpu.VMEM(small, f32),
            pltpu.VMEM((overs, *small), f32),
            pltpu.VMEM(small, f32),
            pltpu.VMEM((nc, count, columns), f32),
            pltpu.VMEM((nf, count, columns), f32),
            pltpu.VMEM((2, shard, 512), f32),
            pltpu.VMEM((shard, LANES), f32),
            pltpu.VMEM((LANES, LANES), f32),
            pltpu.VMEM((nt, padded, shard), f32),
            pltpu.VMEM((nf, padded, width), f32),
            pltpu.VMEM((3, max(sizes.values()), 16, LANES), f32),
            dma((2, 2, count, nt - 1)),
            dma((2, 2, count, nt - 1)),
            dma((2, 2, count, nc - 1)),
            dma((2, 2, 3)),
            dma((2, 2, 3, others)),
            dma((2, 2, 3, overs)),
            dma((2, 2, 3)),
            dma((3,)),
            dma((2, 2)),
            dma((2, others)),
            dma((2, overs)),
            dma((1,)),
            dma((2, nc - 1)),
            dma((2, others)),
            dma((2,)),
            dma((2, nt - 1)),
            dma((2, others)),
            dma((2, 3, max(sizes.values()))),
        ],
        compiler_params=pltpu.CompilerParams(
            collective_id=2, has_side_effects=True, vmem_limit_bytes=60 * 2**20
        ),
        cost_estimate=pl.CostEstimate(
            flops=4 * tokens * width * blocks * local * layers,
            bytes_accessed=layers * blocks * width * local * 4,
            transcendentals=0,
        ),
        name="backward_layers",
    )(dh0, mods, dmods_end, loss, noisy, dpred, final_in, *slopes, *rights, time, cond, full, *saved)


FIX = math.sqrt(1.0 / (1.0 - BETA**STEP))


def update_block(weight, mean, square, grad, outs, where):
    mean_next = BETA * mean[where] + grad
    square_next = BETA * square[where] + (grad * grad) * (1.0 / (1.0 - BETA))
    moved = mean_next / (jnp.sqrt(square_next) + EPSILON / FIX)
    outs[0][where] = weight[where] * (1.0 - RATE * DECAY) - (RATE * FIX) * moved
    outs[1][where] = mean_next
    outs[2][where] = square_next


def mixed(a):
    layers, rows, blocks, columns = a.shape
    a = a.reshape(layers, rows, blocks, columns // LANES, LANES)
    return jnp.swapaxes(a, 2, 3).reshape(layers, -1, LANES)


def update_kernel(
    plan, clip_ref, grads_ref, small_ref, cond_left, cond_right, time_left, time_right, freq_left, freq_right,
    label_left, label_right, *refs,
):
    clip = clip_ref[0, 0] * (1.0 - BETA)
    step = pl.program_id(0) * pl.num_programs(1) + pl.program_id(1)
    names = ("attend", "hidden", "output", "cond", "time", "freq", "label", "patch", "head")
    trios = {name: refs[3 * k : 3 * k + 3] for k, name in enumerate(names)}
    outs = {name: refs[27 + 3 * k : 30 + 3 * k] for k, name in enumerate(names)}

    def change(name, grad, where):
        update_block(*trios[name], grad * clip, outs[name], where)

    for name, first in (("attend", QUERY), ("output", OUT)):
        _, blocks, rows, _ = trios[name][0].shape
        piece = min(64, rows)
        for b in range(blocks):
            for r in range(0, rows, piece):
                grad = grads_ref[0, first + b, r : r + piece].astype(jnp.float32)
                change(name, grad, (0, b, pl.ds(r, piece)))

    _, _, rows, columns = grads_ref.shape
    tiles = columns // LANES
    size = 4 * tiles * 16
    order = interleave(4, tiles)
    for r in range(rows // 16):
        parts = [
            grads_ref[0, HIDDEN + k, 16 * r : 16 * r + 16, n * LANES : (n + 1) * LANES]
            for k in range(4)
            for n in range(tiles)
        ]
        change("hidden", dot(order, jnp.concatenate(parts, 0)), (0, pl.ds(r * size, size)))

    def outer(name, left, right):
        first, count = plan[name]

        @pl.when((step >= first) & (step < first + count))
        def _():
            rows = trios[name][0].shape[0]
            for r in range(0, rows, 64):
                high = min(r + 64, rows)
                change(name, dot_tn(left[:, r:high], right[...]), (pl.ds(r, high - r),))

    outer("cond", cond_left, cond_right)
    outer("time", time_left, time_right)
    outer("freq", freq_left, freq_right)
    outer("label", label_left, label_right)

    @pl.when(step == 0)
    def _():
        small = jnp.transpose(small_ref[...])
        at = 0
        for name in ("patch", "head"):
            rows = trios[name][0].shape[0]
            change(name, small[at : at + rows], (pl.ds(0, rows),))
            at += rows


def update(clip, grads, small, factors, trios):
    attend, hidden, output, patch, freq, time, label, cond, head = trios
    layers, _, rows, local = grads.shape
    parts = 4
    steps = layers * parts
    inner = rows // parts

    def turned(trio):
        return [jnp.swapaxes(a, -1, -2) for a in trio]

    def outward(trio):
        return [jnp.swapaxes(a, 1, 2) for a in trio]

    arrays = {
        "attend": outward(attend),
        "hidden": [mixed(a) for a in hidden],
        "output": outward(output),
        "cond": list(cond),
        "time": list(time),
        "freq": list(freq),
        "label": turned(label),
        "patch": turned(patch),
        "head": turned(head),
    }
    chunks = {"cond": 512, "time": LANES, "freq": LANES, "label": min(LANES, rows)}
    plan, specs = {}, {}
    for name, width in chunks.items():
        count = arrays[name][0].shape[1] // width
        plan[name] = (0 if name == "cond" else steps - count, count)

    def at(name):
        first, count = plan[name]
        return lambda i, j: (0, jnp.clip(i * parts + j - first, 0, count - 1))

    for name, (array, *_) in arrays.items():
        if name in chunks:
            specs[name] = pl.BlockSpec((array.shape[0], chunks[name]), at(name))
        elif name == "hidden":
            specs[name] = pl.BlockSpec((1, array.shape[1] // parts, LANES), lambda i, j: (i, j, 0))
        elif array.ndim == 4:
            specs[name] = pl.BlockSpec((1, array.shape[1], inner, local), lambda i, j: (i, 0, j, 0))
        else:
            specs[name] = pl.BlockSpec(array.shape, lambda i, j: (0, 0))
    factor_specs = []
    for name in ("cond", "time", "freq", "label"):
        left, right = factors[name]
        factor_specs.append(pl.BlockSpec(left.shape, lambda i, j: (0, 0)))
        factor_specs.append(pl.BlockSpec((right.shape[0], chunks[name]), at(name)))
    whole = [specs[name] for name in arrays for _ in range(3)]
    flat = [a for name in arrays for a in arrays[name]]
    size = sum(a.size for a in flat) // 3
    outs = pl.pallas_call(
        functools.partial(update_kernel, plan),
        grid=(layers, parts),
        out_shape=[jax.ShapeDtypeStruct(a.shape, jnp.float32) for a in flat],
        in_specs=[
            pl.BlockSpec(memory_space=pltpu.SMEM),
            pl.BlockSpec((1, grads.shape[1], inner, local), lambda i, j: (i, 0, j, 0)),
            pl.BlockSpec(small.shape, lambda i, j: (0, 0)),
            *factor_specs,
            *whole,
        ],
        out_specs=whole,
        compiler_params=pltpu.CompilerParams(vmem_limit_bytes=60 * 2**20),
        cost_estimate=pl.CostEstimate(flops=20 * size, bytes_accessed=26 * size, transcendentals=2 * size),
        name="update",
    )(clip, grads, small, *(f for name in ("cond", "time", "freq", "label") for f in factors[name]), *flat)
    made = {name: outs[3 * k : 3 * k + 3] for k, name in enumerate(arrays)}
    blocks = hidden[0].shape[2]

    def back(a):
        a = a.reshape(layers, rows, local // LANES, blocks, LANES)
        return jnp.swapaxes(a, 2, 3).reshape(layers, rows, blocks, local)

    return [
        *outward(made["attend"]),
        *(back(a) for a in made["hidden"]),
        *outward(made["output"]),
        *turned(made["patch"]),
        *made["freq"],
        *made["time"],
        *turned(made["label"]),
        *made["cond"],
        *turned(made["head"]),
    ]


def per_device(
    mesh,
    latents,
    noise,
    var_target,
    timesteps,
    labels,
    attend_weight,
    attend_mean,
    attend_square,
    hidden_weight,
    hidden_mean,
    hidden_square,
    output_weight,
    output_mean,
    output_square,
    patch_weight,
    patch_mean,
    patch_square,
    freq_weight,
    freq_mean,
    freq_square,
    time_weight,
    time_mean,
    time_square,
    label_table,
    label_mean,
    label_square,
    cond_weight,
    cond_mean,
    cond_square,
    head_weight,
    head_mean,
    head_square,
):
    count, rows, patch_in = latents.shape
    layers, shard = attend_weight.shape[:2]
    columns = cond_weight.shape[1]

    own = jnp.pad(jnp.stack([timesteps, labels]).astype(jnp.float32), ((0, 6), (0, LANES - count)))
    drawn = lax.all_gather(own, "fsdp", axis=0)[:, :2, :count]
    steps_all, labels_all = (drawn[:, k].reshape(-1).astype(jnp.int32) for k in range(2))
    freqs = time_freqs(steps_all).astype(LOW)
    act = jnp.dot(freqs, freq_weight.astype(LOW).T, preferred_element_type=jnp.float32)
    act = lax.all_gather(act, "fsdp", axis=1, tiled=True)
    swish = jax.nn.silu(act).astype(LOW)
    time_low = time_weight.astype(LOW)
    temb = jnp.dot(swish, time_low.T, preferred_element_type=jnp.float32)
    onehot = (labels_all[:, None] == jnp.arange(label_table.shape[1], dtype=jnp.int32)[None]).astype(
        LOW
    )
    cvec = temb + jnp.dot(onehot, label_table.astype(LOW).T, preferred_element_type=jnp.float32)
    cond_in = jax.nn.silu(cvec).astype(LOW)
    level = noise_level(timesteps)[:, None, None]
    noisy = (jnp.sqrt(level) * latents + jnp.sqrt(1.0 - level) * noise).astype(LOW)
    images = freqs.shape[0]
    width = time_weight.shape[1]
    patch_out = head_weight.shape[1]
    after = LANES - patch_in - patch_out

    def twice(value, each):
        value = jnp.pad(value.astype(LOW), ((0, each - images), (0, 0)))
        return jnp.pad(jnp.concatenate([value, value]), ((0, -2 * each % 16), (0, 0)))

    cond_parts = twice(cond_in, images)
    noisy_wide = jnp.pad(noisy, ((0, 0), (0, 0), (0, LANES - patch_in)))
    d_h, flat_mods, d_mods_end, loss_part, d_pred, final_in, full, *saved = forward(
        mesh,
        images,
        (patch_in, patch_out),
        cond_parts,
        cond_weight,
        patch_weight.T,
        head_weight.T,
        noisy_wide,
        positions(lax.axis_index("ctx") * rows, rows, width),
        jnp.pad(jnp.concatenate([noise, var_target], 2), ((0, 0), (0, 0), (patch_in, after))),
        mixed(hidden_weight),
        jnp.swapaxes(attend_weight, 1, 2),
        jnp.swapaxes(output_weight, 1, 2),
    )
    blocks = full.shape[1]
    full = full.reshape(layers, blocks, width, -1)
    padded = max(8, images) - images
    tokens = count * rows

    def slope(value):
        _, back = jax.vjp(jax.nn.silu, value)
        return jnp.pad(back(jnp.ones_like(value))[0], ((0, padded), (0, 0)))

    each = max(8, images)
    swish_parts, onehot_parts, freq_parts = (twice(v, each) for v in (swish, onehot, freqs))
    grads, d_small, d_cols, d_cvec, d_act, stat = backward(
        mesh,
        images,
        d_h,
        flat_mods,
        d_mods_end,
        loss_part,
        noisy_wide.reshape(tokens, -1),
        d_pred.reshape(tokens, -1),
        final_in.reshape(tokens, -1),
        (slope(cvec), slope(act)),
        (cond_parts, swish_parts, onehot_parts, freq_parts),
        time_weight,
        cond_weight,
        full,
        saved,
    )
    grads = grads.reshape(layers, blocks, shard, -1)
    d_small = d_small.reshape(shard, -1)
    d_act = lax.dynamic_slice_in_dim(d_act, lax.axis_index("fsdp") * shard, shard, 1)
    total_sq, loss = stat[0, 0], stat[8, 0]
    grad_norm = jnp.sqrt(total_sq)
    clip = jnp.minimum(1.0, CLIP / (grad_norm + 1e-06))
    factor = clip.reshape(1, 1)
    updated = update(
        factor,
        grads,
        d_small,
        {
            "cond": (cond_parts, d_cols),
            "time": (d_cvec, swish_parts),
            "freq": (d_act, freq_parts),
            "label": (onehot_parts, d_cvec),
        },
        (
            (attend_weight, attend_mean, attend_square),
            (hidden_weight, hidden_mean, hidden_square),
            (output_weight, output_mean, output_square),
            (patch_weight, patch_mean, patch_square),
            (freq_weight, freq_mean, freq_square),
            (time_weight, time_mean, time_square),
            (label_table, label_mean, label_square),
            (cond_weight, cond_mean, cond_square),
            (head_weight, head_mean, head_square),
        ),
    )
    return (loss, grad_norm, *updated)


def solution(mesh):
    image = P("fsdp", "ctx", None)
    layer = P(None, "fsdp", None, "tp")
    rows = P("fsdp", None)
    cond = P("fsdp", "tp")
    weights = (layer,) * 9 + (rows,) * 12 + (cond,) * 3 + (rows,) * 3
    return jax.shard_map(
        functools.partial(per_device, mesh),
        mesh=mesh,
        in_specs=(image, image, image, P("fsdp"), P("fsdp")) + weights,
        out_specs=(P(), P()) + weights,
        check_vma=False,
    )
```

```python
import functools
import math

import jax
import jax.numpy as jnp
from jax import lax
from jax.experimental import pallas as pl
from jax.experimental.pallas import tpu as pltpu
from jax.sharding import PartitionSpec as P

HEAD_DIM = 64
FREQ = 256
GRID = 16
STEP = 5


HIGH = lax.Precision.HIGHEST
RATE = 0.05
DECAY = 0.1
BETA = 0.5
EPSILON = 1e-08
CLIP = 1.0
LOW = jnp.bfloat16


def noise_level(steps):
    phase = (steps.astype(jnp.float32) / 1000.0 + 0.008) / 1.008 * (0.5 * math.pi)
    return jnp.cos(phase) ** 2


def time_freqs(steps):
    half = FREQ // 2
    rates = jnp.exp(-math.log(10000.0) * jnp.arange(half, dtype=jnp.float32) / half)
    angles = steps.astype(jnp.float32)[:, None] * rates[None, :]
    return jnp.concatenate([jnp.cos(angles), jnp.sin(angles)], -1)


def positions(first, count, width):
    index = first + jnp.arange(count, dtype=jnp.int32)
    row = (index // GRID).astype(jnp.float32)
    column = (index % GRID).astype(jnp.float32)
    quarter = width // 4
    rates = jnp.power(10000.0, -jnp.arange(quarter, dtype=jnp.float32) / quarter)
    across = column[:, None] * rates[None, :]
    down = row[:, None] * rates[None, :]
    return jnp.concatenate([jnp.sin(across), jnp.cos(across), jnp.sin(down), jnp.cos(down)], -1)


MESH = pl.DeviceIdType.MESH
GROUPS = ((4, 4), (0, 4), (8, 4))
QUERY, KEY, VALUE, OUT, HIDDEN, MLP = 4, 5, 6, 7, 0, 8
LANES = 128


def dot(left, right):
    return jnp.dot(left, right, preferred_element_type=jnp.float32)


def dot_nt(left, right):
    return lax.dot_general(left, right, (((1,), (1,)), ((), ())), preferred_element_type=jnp.float32)


def dot_tn(left, right):
    return lax.dot_general(left, right, (((0,), (0,)), ((), ())), preferred_element_type=jnp.float32)


def remote(src, dst, sems, where, **device):
    send, recv = (sems.at[(0, *where)], sems.at[(1, *where)])
    return pltpu.make_async_remote_copy(
        src_ref=src, dst_ref=dst, send_sem=send, recv_sem=recv, device_id=device, device_id_type=MESH
    )


def meet(sizes):
    barrier = pltpu.get_barrier_semaphore()
    count = 0
    for axis, size in sizes.items():
        for step in range(1, size):
            peer = lax.rem(lax.axis_index(axis) + step, size)
            pl.semaphore_signal(barrier, inc=1, device_id={axis: peer}, device_id_type=MESH)
            count += 1
    pl.semaphore_wait(barrier, count)


def norm_parts(h):
    mean = jnp.mean(h, -1, keepdims=True)
    cent = h - mean
    var = jnp.mean(cent * cent, -1, keepdims=True)
    inv = lax.rsqrt(var + 1e-06)
    return cent * inv, inv


def norm_back(grad, normed, inv, scale):
    grad_shift = jnp.sum(grad, 0, keepdims=True)
    grad_scale = jnp.sum(grad * normed, 0, keepdims=True)
    inner = grad * (1.0 + scale)
    mean = jnp.mean(inner, -1, keepdims=True)
    along = jnp.mean(inner * normed, -1, keepdims=True)
    return inv * (inner - mean - normed * along), grad_shift, grad_scale


class Total:
    def __init__(self, size, g, send, first, full, sems):
        self.size, self.g, self.sems = size, g, sems
        self.send, self.first, self.full = send.at[g], first.at[g], full.at[g]
        self.me = lax.axis_index("tp")

    def peer(self, ahead):
        return lax.rem(self.me + ahead, self.size)

    def one(self, ahead):
        peer = self.peer(ahead)
        return remote(
            self.send.at[peer], self.first.at[ahead - 1], self.sems, (0, self.g, ahead - 1), tp=peer
        )

    def two(self, block, ahead):
        block = self.full.at[block]
        return remote(block, block, self.sems, (1, self.g, ahead - 1), tp=self.peer(ahead))

    def scatter(self, part):
        self.send[...] = part.astype(LOW).reshape(self.send.shape)
        for ahead in range(1, self.size):
            self.one(ahead).start()

    def share(self):
        total = self.send[self.me].astype(jnp.float32)
        for ahead in range(1, self.size):
            self.one(ahead).wait()
            total = total + self.first[ahead - 1].astype(jnp.float32)
        self.full[self.me] = total.astype(LOW)
        for ahead in range(1, self.size):
            self.two(self.me, ahead).start()

    def get(self):
        for ahead in range(1, self.size):
            self.two(self.me, ahead).wait_send()
            self.two(lax.rem(self.me + self.size - ahead, self.size), ahead).wait_recv()
        size, rows, width = self.full.shape
        return self.full[...].reshape(size * rows, width)


def spread(block, heads):
    lane = lax.broadcasted_iota(jnp.int32, block.shape, 1) // HEAD_DIM
    zero = jnp.zeros_like(block)
    return jnp.concatenate([jnp.where(lane == k, block, zero) for k in range(heads)], 0)


def pick(stacked, heads):
    rows = stacked.shape[0] // heads
    lane = lax.broadcasted_iota(jnp.int32, (rows, stacked.shape[1]), 1) // HEAD_DIM
    total = jnp.zeros((rows, stacked.shape[1]), stacked.dtype)
    for k in range(heads):
        total = jnp.where(lane == k, stacked[k * rows : (k + 1) * rows], total)
    return total


ROOT_2_PI = math.sqrt(2.0 / math.pi)


def gelu_parts(v):
    inside = jnp.tanh(ROOT_2_PI * (v + 0.044715 * (v * v * v)))
    value = v * (0.5 * (1.0 + inside))
    slope = 0.5 * (1.0 + inside) + 0.5 * v * (1.0 - inside * inside) * ROOT_2_PI * (
        1.0 + 3 * 0.044715 * v * v
    )
    return value, slope


def row(ref, g, index, width):
    return ref[g : g + 1, pl.ds(pl.multiple_of(index * width, LANES), width)]


def put_row(ref, g, index, width, value):
    ref[g : g + 1, pl.ds(pl.multiple_of(index * width, LANES), width)] = value


def interleave(blocks, tiles, back=False):
    size = blocks * tiles * 16
    to = lax.broadcasted_iota(jnp.int32, (size, size), 1 if back else 0)
    source = lax.broadcasted_iota(jnp.int32, (size, size), 0 if back else 1)
    block, tile, at = to % blocks, (to // blocks) % tiles, to // (blocks * tiles)
    return jnp.where(source == (block * tiles + tile) * 16 + at, 1.0, 0.0).astype(LOW)


def forward_kernel(
    sizes, images, target_first, target_count, cond_in_ref, cond_ref, patch_ref, head_ref, noisy_ref, pos_ref, target_ref, hidden_ref, attend_ref, output_ref,
    dh_out, mods_out, dmods_out, loss_out, dpred_out, final_out, full_ref,
    keep_h, keep_mid, keep_a, keep_m, keep_q, keep_kv, keep_p, keep_att, keep_pre,
    weights, stage_h, stage_a, stage_o, part_ref, cond_buf, ends, kv, h_ref, q_ref, mods_ref, mods_got, send_a, first_a, full_a, send_m, first_m, full_m,
    x_sems, y_sems, pair_sems, own_sems, kv_sems, a_sems, m_sems, mods_x_sems, mods_t_sems, cond_sems, ends_sems,
):
    nf, nc, nt = sizes["fsdp"], sizes["ctx"], sizes["tp"]
    chips = nc // 2
    step = pl.program_id(0)
    layers = attend_ref.shape[0]
    f, c, t = lax.axis_index("fsdp"), lax.axis_index("ctx"), lax.axis_index("tp")
    core, chip = lax.rem(c, 2), c // 2
    sibling = c + 1 - 2 * core
    count, rows, width = h_ref.shape
    local = weights.shape[-1]
    heads = local // HEAD_DIM
    scale = 1.0 / math.sqrt(HEAD_DIM)
    columns = part_ref.shape[-1]

    def blocks(k):
        return pl.ds(*GROUPS[k])

    def x_copy(layer, k, ahead):
        return remote(
            weights.at[layer, blocks(k), f, chip, core],
            weights.at[layer, blocks(k), f, chip, core],
            x_sems,
            (layer, k, ahead - 1),
            fsdp=lax.rem(f + ahead, nf),
        )

    def x_arrived(layer, k, ahead):
        source = lax.rem(f + nf - ahead, nf)
        block = weights.at[layer, blocks(k), source, chip, core]
        remote(block, block, x_sems, (layer, k, ahead - 1), fsdp=source).wait_recv()

    def y_copy(layer, k, ahead, over, at):
        source = lax.rem(f + nf - ahead, nf)
        block = weights.at[layer, blocks(k), source, at, core]
        peer = lax.rem(chip + over, chips) * 2 + core
        return remote(block, block, y_sems, (layer, k, ahead - 1, over - 1), ctx=peer)

    def pair_copy(layer, k, ahead, half):
        source = lax.rem(f + nf - ahead, nf)
        block = weights.at[layer, blocks(k), source, :, half]
        return remote(block, block, pair_sems, (layer, k, ahead - 1), ctx=sibling)

    def pass_y(layer, k):
        for ahead in range(1, nf):
            x_arrived(layer, k, ahead)
            for over in range(1, chips):
                y_copy(layer, k, ahead, over, chip).start()

    def pass_pair(layer, k):
        for ahead in range(1, nf):
            for over in range(1, chips):
                y_copy(layer, k, ahead, over, lax.rem(chip + chips - over, chips)).wait_recv()
            pair_copy(layer, k, ahead, core).start()

    def arrived(layer, k):
        for ahead in range(1, nf):
            pair_copy(layer, k, ahead, 1 - core).wait_recv()

    def stage_copies(layer):
        return [
            pltpu.make_async_copy(source.at[layer], stage, own_sems.at[1 + k])
            for k, (source, stage) in enumerate(
                ((attend_ref, stage_a), (hidden_ref, stage_h), (output_ref, stage_o))
            )
        ]

    def quarters(value):
        return value.astype(LOW).reshape(chips, 2, -1, local)

    def send_x(layer, k):
        for ahead in range(1, nf):
            x_copy(layer, k, ahead).start()

    def lower_attend(layer):
        copies = stage_copies(layer)
        copies[0].wait()
        copies[2].wait()
        for k in range(3):
            weights[layer, QUERY + k, f] = quarters(stage_a[k])
        weights[layer, OUT, f] = quarters(stage_o[0])
        send_x(layer, 0)

    def lower_rest(layer):
        stage_copies(layer)[1].wait()
        tiles = local // LANES
        size = 4 * tiles * 16
        order = interleave(4, tiles, back=True)
        quarter = weights.shape[-2]

        def split(r, carry):
            rows_in = pl.ds(pl.multiple_of(r * size, size), size)
            value = dot(order, stage_h[rows_in].astype(LOW)).astype(LOW)
            part = (r * 16) // quarter
            at = pl.ds(pl.multiple_of(lax.rem(r * 16, quarter), 16), 16)
            for k in range(4):
                for n in range(tiles):
                    first = (k * tiles + n) * 16
                    weights[
                        layer, HIDDEN + k, f, part // 2, lax.rem(part, 2), at, n * LANES : (n + 1) * LANES
                    ] = value[first : first + 16]
            return carry

        lax.fori_loop(0, stage_h.shape[0] // size, split, 0, unroll=2)
        send_x(layer, 1)
        for k in range(4):
            weights[layer, MLP + k, f] = quarters(stage_o[1 + k])
        send_x(layer, 2)

    chunk = cond_buf.shape[-1]

    def cond_copy(j):
        return pltpu.make_async_copy(
            cond_ref.at[:, pl.ds(pl.multiple_of(j * chunk, LANES), chunk)],
            cond_buf.at[lax.rem(j, 2)],
            cond_sems.at[lax.rem(j, 2)],
        )

    def multiply(j, carry):
        @pl.when(j + 1 < columns // chunk)
        def _():
            cond_copy(j + 1).start()

        cond_copy(j).wait()
        product = dot(cond_in_ref[...], cond_buf[lax.rem(j, 2)].astype(LOW))
        for n in range(images):
            part_ref[
                n // count, n % count : n % count + 1, pl.ds(pl.multiple_of(j * chunk, LANES), chunk)
            ] = product[n : n + 1]
        return carry

    def ends_copy(ahead, at):
        return remote(ends.at[at], ends.at[at], ends_sems, (ahead - 1,), fsdp=lax.rem(f + ahead, nf))

    def both_ends():
        return ends[...].reshape(width, LANES)

    def store_copy(layer):
        return pltpu.make_async_copy(weights.at[layer], full_ref.at[layer], own_sems.at[4 + layer])

    def share_mods():
        for ahead in range(1, nf):
            peer = lax.rem(f + ahead, nf)
            remote(part_ref.at[peer], mods_got.at[ahead - 1], mods_x_sems, (ahead - 1,), fsdp=peer).start()

    def finish_mods():
        total = part_ref[f]
        for ahead in range(1, nf):
            peer = lax.rem(f + ahead, nf)
            remote(part_ref.at[peer], mods_got.at[ahead - 1], mods_x_sems, (ahead - 1,), fsdp=peer).wait()
            total = total + mods_got[ahead - 1]

        def at(k):
            return mods_ref.at[:, pl.ds(pl.multiple_of(k * columns, LANES), columns)]

        mods_ref[:, pl.ds(pl.multiple_of(t * columns, LANES), columns)] = total
        for ahead in range(1, nt):
            remote(at(t), at(t), mods_t_sems, (ahead - 1,), tp=lax.rem(t + ahead, nt)).start()
        for ahead in range(1, nt):
            source = lax.rem(t + nt - ahead, nt)
            remote(at(t), at(t), mods_t_sems, (ahead - 1,), tp=source).wait_send()
            remote(at(source), at(source), mods_t_sems, (ahead - 1,), tp=source).wait_recv()

    def mod(k, g, layer):
        return row(mods_ref, g, 6 * layer + k, width)

    def total_a(g):
        return Total(nt, g, send_a, first_a, full_a, a_sems)

    def total_m(g):
        return Total(nt, g, send_m, first_m, full_m, m_sems)

    def kv_copy(layer, g, ahead, at):
        block = kv.at[layer, g, at]
        return remote(block, block, kv_sems, (layer, g, ahead - 1), ctx=lax.rem(c + ahead, nc))

    @pl.when(step == 0)
    def _():
        for copy in stage_copies(0):
            copy.start()
        cond_copy(0).start()
        used = jnp.concatenate([patch_ref[...], head_ref[...]], 0)
        unused = jnp.zeros((LANES - used.shape[0], used.shape[1]), jnp.float32)
        ends[f] = jnp.transpose(jnp.concatenate([used, unused], 0)).astype(LOW)
        meet(sizes)
        for ahead in range(1, nf):
            ends_copy(ahead, f).start()
        lower_attend(0)
        lax.fori_loop(0, columns // chunk, multiply, 0)
        share_mods()
        pass_y(0, 0)
        lower_rest(0)
        for copy in stage_copies(1):
            copy.start()
        pass_pair(0, 0)
        for ahead in range(1, nf):
            ends_copy(ahead, f).wait_send()
            ends_copy(ahead, lax.rem(f + nf - ahead, nf)).wait_recv()
        for g in range(count):
            h_ref[g] = dot_nt(noisy_ref[g], both_ends()) + pos_ref[...]
        finish_mods()
        pass_y(0, 1)

    def matrix(k):
        return weights[step, k].reshape(width, local)

    def begin(g):
        h = h_ref[g]
        keep_h[0, g] = h
        normed, _ = norm_parts(h)
        u_in = (normed * (1.0 + mod(1, g, step)) + mod(0, g, step)).astype(LOW)
        kv[step, g, c, :, :local] = dot(u_in, matrix(KEY)).astype(LOW)
        kv[step, g, c, :, local:] = dot(u_in, matrix(VALUE)).astype(LOW)
        for ahead in range(1, nc):
            kv_copy(step, g, ahead, c).start()
        q_ref[g] = dot(u_in, matrix(QUERY)).astype(LOW)

    def last_branch(g):
        branch = total_m(g).get()
        keep_m[0, g] = branch
        h_ref[g] = h_ref[g] + mod(5, g, step - 1) * branch.astype(jnp.float32)

    @pl.when(step < layers)
    def _():
        arrived(step, 0)

    def finish(g):
        normed, inv = norm_parts(h_ref[g])
        shift, scale_row = (row(mods_ref, g, 6 * layers + k, width) for k in range(2))
        final_in = (normed * (1.0 + scale_row) + shift).astype(LOW)
        final_out[g] = final_in
        lane = lax.broadcasted_iota(jnp.int32, (rows, LANES), 1)
        inside = (lane >= target_first) & (lane < target_first + target_count)
        diff = jnp.where(inside, dot(final_in, both_ends()) - target_ref[g], 0.0)
        squares = jnp.sum((diff * diff).reshape(rows // 8, 8, LANES), 0)
        loss_out[...] = squares if g == 0 else loss_out[...] + squares
        d_pred = (2.0 * diff).astype(LOW)
        dpred_out[g] = d_pred
        d_h, d_shift, d_scale = norm_back(dot_nt(d_pred, both_ends()), normed, inv, scale_row)
        dh_out[g] = d_h
        put_row(dmods_out, g, 0, width, d_shift)
        put_row(dmods_out, g, 1, width, d_scale)

    for g in range(count):

        @pl.when(step >= 1)
        def _():
            last_branch(g)

        @pl.when(step == layers)
        def _():
            finish(g)

        @pl.when(step < layers)
        def _():
            begin(g)

    @pl.when(step + 1 < layers)
    def _():
        lower_attend(step + 1)
        lower_rest(step + 1)

    @pl.when(step + 2 < layers)
    def _():
        for copy in stage_copies(step + 2):
            copy.start()

    @pl.when(step < layers)
    def _():
        pass_y(step, 2)
        pass_pair(step, 1)
        for g in range(count):
            for ahead in range(1, nc):
                kv_copy(step, g, ahead, c).wait_send()
                kv_copy(step, g, ahead, lax.rem(c + nc - ahead, nc)).wait_recv()
            keep_q[0, g] = q_ref[g]
            keep_kv[0, g] = kv[step, g]
            keys = kv[step, g, :, :, :local].reshape(nc * rows, local)
            values = kv[step, g, :, :, local:].reshape(nc * rows, local)
            scores = dot_nt(spread(q_ref[g], heads), keys) * scale
            expo = jnp.exp(scores - jnp.max(scores, -1, keepdims=True))
            probs = expo / jnp.sum(expo, -1, keepdims=True)
            keep_p[0, g] = probs
            attended = pick(dot(probs.astype(LOW), values), heads).astype(LOW)
            keep_att[0, g] = attended
            total_a(g).scatter(dot_nt(attended, matrix(OUT)))
        pass_pair(step, 2)
        for g in range(count):
            total_a(g).share()
        arrived(step, 1)

    @pl.when(step + 1 < layers)
    def _():
        pass_y(step + 1, 0)

    @pl.when(step < layers)
    def _():
        for g in range(count):
            branch = total_a(g).get()
            keep_a[0, g] = branch
            h_mid = h_ref[g] + mod(2, g, step) * branch.astype(jnp.float32)
            keep_mid[0, g] = h_mid
            h_ref[g] = h_mid
            normed, _ = norm_parts(h_mid)
            w_in = (normed * (1.0 + mod(4, g, step)) + mod(3, g, step)).astype(LOW)
            if g == 0:
                arrived(step, 2)
                store_copy(step).start()
            part = jnp.zeros((rows, width), jnp.float32)
            for k in range(4):
                pre = dot(w_in, matrix(HIDDEN + k))
                keep_pre[0, g, k] = pre
                part = part + dot_nt(gelu_parts(pre)[0].astype(LOW), matrix(MLP + k))
            total_m(g).scatter(part)

    @pl.when(step + 1 < layers)
    def _():
        pass_pair(step + 1, 0)
        pass_y(step + 1, 1)

    @pl.when(step < layers)
    def _():
        for g in range(count):
            total_m(g).share()

    @pl.when(step == layers)
    def _():
        mods_out[...] = mods_ref[...]

        def drain(layer, carry):
            store_copy(layer).wait()
            for k in range(len(GROUPS)):
                for ahead in range(1, nf):
                    x_copy(layer, k, ahead).wait_send()
                    for over in range(1, chips):
                        y_copy(layer, k, ahead, over, chip).wait_send()
                    pair_copy(layer, k, ahead, core).wait_send()
            return carry

        lax.fori_loop(0, layers, drain, 0)


def forward(mesh, images, target_at, cond_in, cond, patch, head, noisy, pos, target, hidden, attend, output):
    sizes = dict(mesh.shape)
    nf, nc, nt = sizes["fsdp"], sizes["ctx"], sizes["tp"]
    chips = nc // 2
    count, rows, _ = noisy.shape
    width, columns = pos.shape[1], cond.shape[1]
    layers, _, shard, local = attend.shape
    blocks, quarter = 4 + attend.shape[1] + output.shape[1], shard // nc
    heads = local // HEAD_DIM
    tokens = count * rows
    others, overs = max(nf - 1, 1), max(chips - 1, 1)
    f32 = jnp.float32

    def kept(shape, dtype, late=0):
        spec = pl.BlockSpec(
            (1, *shape), lambda i: (jnp.clip(i - late, 0, layers - 1),) + (0,) * len(shape)
        )
        return jax.ShapeDtypeStruct((layers, *shape), dtype), spec

    saves = [
        kept((count, rows, width), f32),
        kept((count, rows, width), f32),
        kept((count, rows, width), LOW),
        kept((count, rows, width), LOW, 1),
        kept((count, rows, local), LOW),
        kept((count, nc, rows, 2 * local), LOW),
        kept((count, heads * rows, nc * rows), f32),
        kept((count, rows, local), LOW),
        kept((count, 4, rows, local), f32),
    ]
    anywhere = pl.BlockSpec(memory_space=pl.ANY)
    vmem = pl.BlockSpec(memory_space=pltpu.VMEM)
    whole = pltpu.VMEM((count, nt, rows // nt, width), LOW)
    first = pltpu.VMEM((count, nt - 1, rows // nt, width), LOW)
    dma = pltpu.SemaphoreType.DMA
    return pl.pallas_call(
        functools.partial(forward_kernel, sizes, images, *target_at),
        grid=(layers + 1,),
        out_shape=[
            jax.ShapeDtypeStruct((count, rows, width), f32),
            jax.ShapeDtypeStruct((count, nt * columns), f32),
            jax.ShapeDtypeStruct((count, 2 * width), f32),
            jax.ShapeDtypeStruct((8, LANES), f32),
            jax.ShapeDtypeStruct((count, rows, LANES), LOW),
            jax.ShapeDtypeStruct((count, rows, width), LOW),
            jax.ShapeDtypeStruct((layers, blocks, nf, chips, 2, quarter, local), LOW),
            *(shape for shape, _ in saves),
        ],
        in_specs=[vmem, anywhere, *[vmem] * 5, anywhere, anywhere, anywhere],
        out_specs=[*[vmem] * 6, anywhere, *(spec for _, spec in saves)],
        scratch_shapes=[
            pltpu.VMEM((layers, blocks, nf, chips, 2, quarter, local), LOW),
            *(pltpu.VMEM(w.shape[1:], f32) for w in (hidden, attend, output)),
            pltpu.VMEM((nf, count, columns), f32),
            pltpu.VMEM((2, shard, 512), f32),
            pltpu.VMEM((nf, shard, LANES), LOW),
            pltpu.VMEM((layers, count, nc, rows, 2 * local), LOW),
            pltpu.VMEM((count, rows, width), f32),
            pltpu.VMEM((count, rows, local), LOW),
            pltpu.VMEM((count, nt * columns), f32),
            pltpu.VMEM((others, count, columns), f32),
            whole, first, whole, whole, first, whole,
            dma((2, layers, 3, others)),
            dma((2, layers, 3, others, overs)),
            dma((2, layers, 3, others)),
            dma((4 + layers,)),
            dma((2, layers, count, nc - 1)),
            dma((2, 2, count, nt - 1)),
            dma((2, 2, count, nt - 1)),
            dma((2, others)),
            dma((2, nt - 1)),
            dma((2,)),
            dma((2, others)),
        ],
        compiler_params=pltpu.CompilerParams(
            collective_id=1, has_side_effects=True, vmem_limit_bytes=56 * 2**20
        ),
        cost_estimate=pl.CostEstimate(
            flops=2 * tokens * width * blocks * local * layers,
            bytes_accessed=layers * blocks * width * local * 4,
            transcendentals=0,
        ),
        name="forward_layers",
    )(cond_in, cond, patch, head, noisy, pos, target, hidden, attend, output)


def halves(value):
    high = value.astype(LOW).astype(jnp.float32)
    return high, value - high


def backward_kernel(
    sizes, images, dh0_ref, mods_ref, dmods_end_ref, loss_ref, noisy_ref, dpred_ref, final_ref,
    slope_c_ref, slope_a_ref, cond_in_ref, swish_ref, onehot_ref, freqs_ref, time_ref, cond_ref,
    w_ref, keep_h, keep_mid, keep_a, keep_m, keep_q, keep_kv, keep_p, keep_att, keep_pre,
    grads_ref, small_ref, dcols_out, dcvec_ref, dact_ref, stat_ref,
    dh_ref, dmid_ref, h_ref, act_ref, dpre_ref, branch_ref, dba_ref, dqkv_ref, dm_ref,
    send_w, first_w, full_w, send_u, first_u, full_u, kv_send, kv_got,
    grads, pair_got, x_send, x_got, y_send, y_got, done, square,
    s_grads, s_pair, s_send, s_x, s_y_send, s_y, s_done,
    c_got, dcols_ref, cond_buf, product, gram, silu_got, swish_got, stat_got,
    w_sems, u_sems, kv_sems, pair_sems, x_sems, y_sems, end_sems, own_sems,
    s_sems, s_x_sems, s_y_sems, s_own_sems, c_sems, f_sems, cond_sems, t_sems, a_sems, n_sems,
):
    nf, nc, nt = sizes["fsdp"], sizes["ctx"], sizes["tp"]
    chips = nc // 2
    layers, _, _, half, local = grads_ref.shape
    step = pl.program_id(0)
    new = lax.rem(step, 2)
    old = 1 - new
    f, c, t = lax.axis_index("fsdp"), lax.axis_index("ctx"), lax.axis_index("tp")
    core, chip = lax.rem(c, 2), c // 2
    sibling = c + 1 - 2 * core
    count, rows, width = dh_ref.shape
    heads = local // HEAD_DIM
    scale = 1.0 / math.sqrt(HEAD_DIM)
    piece = min(256, half)
    columns = cond_ref.shape[1]
    f32 = jnp.float32
    A, H, M = 0, 1, 2
    layer = layers - 1 - step

    def blocks(k):
        return pl.ds(*GROUPS[k])

    def pieces(k, body):
        parts = half // piece

        def one(j, carry):
            body(j // parts, pl.ds(pl.multiple_of(lax.rem(j, parts) * piece, piece), piece))
            return carry

        low, size = GROUPS[k]
        lax.fori_loop(low * parts, (low + size) * parts, one, 0)

    def pair_copy(k, at):
        return remote(
            grads.at[blocks(k), :, 1 - core], pair_got.at[at, blocks(k)], pair_sems, (at, k), ctx=sibling
        )

    def x_copy(k, at, ahead):
        return remote(
            x_send.at[ahead - 1, blocks(k)], x_got.at[at, ahead - 1, blocks(k)],
            x_sems, (at, k, ahead - 1), fsdp=lax.rem(f + ahead, nf),
        )

    def y_copy(k, at, ahead):
        return remote(
            y_send.at[blocks(k)], y_got.at[at, ahead - 1, blocks(k)],
            y_sems, (at, k, ahead - 1), ctx=lax.rem(chip + ahead, chips) * 2 + core,
        )

    def end_copy(k, at, layer, to):
        return remote(done.at[blocks(k)], grads_ref.at[layer, blocks(k), to], end_sems, (at, k), ctx=sibling)

    def own_copy(k, layer):
        return pltpu.make_async_copy(done.at[blocks(k)], grads_ref.at[layer, blocks(k), core], own_sems.at[k])

    def stage_2(k, at):
        pair_copy(k, at).wait()
        for ahead in range(1, nf):
            peer = lax.rem(f + ahead, nf)

            def add(b, r):
                total = grads[b, peer, core, r].astype(f32) + pair_got[at, b, peer, r].astype(f32)
                x_send[ahead - 1, b, r] = total.astype(LOW)

            pieces(k, add)
            x_copy(k, at, ahead).start()

    def stage_3(k, at):
        for ahead in range(1, nf):
            x_copy(k, at, ahead).wait()

        def add(b, r):
            total = grads[b, f, core, r].astype(f32) + pair_got[at, b, f, r].astype(f32)
            for ahead in range(1, nf):
                total = total + x_got[at, ahead - 1, b, r].astype(f32)
            y_send[b, r] = total.astype(LOW)

        pieces(k, add)
        for ahead in range(1, chips):
            y_copy(k, at, ahead).start()

    def end_wait(k, at, layer):
        own_copy(k, layer).wait()
        end_copy(k, at, layer, core).wait_send()
        end_copy(k, at, layer, 1 - core).wait_recv()

    def stage_4(k, at, layer):
        for ahead in range(1, chips):
            y_copy(k, at, ahead).wait()

        def add(b, r):
            total = y_send[b, r].astype(f32)
            for ahead in range(1, chips):
                total = total + y_got[at, ahead - 1, b, r].astype(f32)
            low = total.astype(LOW)
            done[b, r] = low
            total = low.astype(f32)
            square[...] += jnp.sum((total * total).reshape(piece // 8, 8, local), 0)

        pieces(k, add)
        own_copy(k, layer).start()
        end_copy(k, at, layer, core).start()

    def when(low, high, body):
        pl.when((step >= low) & (step <= high))(body)

    def matrix(k):
        return w_ref[0, k].reshape(width, local)

    def mod(k, g, layer):
        return row(mods_ref, g, 6 * layer + k, width)

    def put_dmod(k, g, layer, value):
        put_row(dm_ref, g, 6 * layer + k, width, value)

    def keep_grad(k, value):
        grads[k] = value.astype(LOW).reshape(nf, 2, half, local)

    def total_w(g):
        return Total(nt, g, send_w, first_w, full_w, w_sems)

    def total_u(g):
        return Total(nt, g, send_u, first_u, full_u, u_sems)

    def both(ref):
        value = ref[...]
        return value.reshape(count * rows, value.shape[-1])

    @pl.when(step == 0)
    def _():
        meet(sizes)
        dh_ref[...] = dh0_ref[...]
        square[...] = jnp.zeros_like(square)
        for g in range(count):
            put_row(dm_ref, g, 3 * layers, 2 * width, dmods_end_ref[g : g + 1])

    def finish_input(g):
        normed, inv = norm_parts(h_ref[g])
        d_h, d_shift, d_scale = norm_back(
            total_u(g).get().astype(f32), normed, inv, mod(1, g, layer + 1)
        )
        put_dmod(0, g, layer + 1, d_shift)
        put_dmod(1, g, layer + 1, d_scale)
        dh_ref[g] = d_h + dmid_ref[g]

    def mlp_back(g):
        grad = dh_ref[g]
        put_dmod(5, g, layer, jnp.sum(grad * keep_m[0, g].astype(f32), 0, keepdims=True))
        branch = (mod(5, g, layer) * grad).astype(LOW)
        branch_ref[g] = branch
        part = jnp.zeros((rows, width), f32)
        for k in range(4):
            value, slope = gelu_parts(keep_pre[0, g, k])
            act_ref[k, g] = value.astype(LOW)
            d_pre = (dot(branch, matrix(MLP + k)) * slope).astype(LOW)
            dpre_ref[k, g] = d_pre
            part = part + dot_nt(d_pre, matrix(HIDDEN + k))
        total_w(g).scatter(part)

    for g in range(count):
        when(1, layers, lambda: finish_input(g))
        when(0, layers - 1, lambda: mlp_back(g))

    def share(own, slots, sems, axis, size, where=()):
        me = lax.axis_index(axis)
        for ahead in range(1, size):
            remote(own, slots.at[me], sems, (*where, ahead - 1), **{axis: lax.rem(me + ahead, size)}).start()

    def shared(own, slots, sems, axis, size, where=()):
        me = lax.axis_index(axis)
        for ahead in range(1, size):
            remote(own, slots.at[me], sems, (*where, ahead - 1), **{axis: lax.rem(me + ahead, size)}).wait_send()
            source = lax.rem(me + size - ahead, size)
            remote(slots.at[source], slots.at[source], sems, (*where, ahead - 1), **{axis: source}).wait_recv()

    def slot_sum(slots, size):
        total = slots[0]
        for k in range(1, size):
            total = total + slots[k]
        return total

    chunk = cond_buf.shape[-1]

    def cond_copy(j):
        return pltpu.make_async_copy(
            cond_ref.at[:, pl.ds(pl.multiple_of(j * chunk, LANES), chunk)],
            cond_buf.at[lax.rem(j, 2)],
            cond_sems.at[lax.rem(j, 2)],
        )

    def small_pair():
        return remote(s_grads.at[:, 1 - core], s_pair, s_sems, (0,), ctx=sibling)

    def small_x(ahead):
        return remote(
            s_send.at[ahead - 1], s_x.at[ahead - 1], s_x_sems, (ahead - 1,), fsdp=lax.rem(f + ahead, nf)
        )

    def small_y(ahead):
        return remote(
            s_y_send, s_y.at[ahead - 1], s_y_sems, (ahead - 1,), ctx=lax.rem(chip + ahead, chips) * 2 + core
        )

    def small_end(to):
        return remote(s_done, small_ref.at[to], s_sems, (1,), ctx=sibling)

    @pl.when(step == layers)
    def _():
        cond_copy(0).start()
        c_got[c] = dm_ref[:, pl.ds(pl.multiple_of(t * columns, LANES), columns)]
        share(c_got.at[c], c_got, c_sems, "ctx", nc)
        high, low = halves(both(dh_ref))
        noisy = noisy_ref[...]
        small = dot_tn(high.astype(LOW), noisy) + dot_tn(low.astype(LOW), noisy)
        small = small + dot_tn(final_ref[...], dpred_ref[...])
        s_grads[...] = small.reshape(s_grads.shape)
        small_pair().start()

    when(1, layers, lambda: stage_2(A, old))
    when(2, layers, lambda: (pl.when(step >= 3)(lambda: end_wait(A, old, layer + 3)), stage_4(A, new, layer + 2))[1])
    when(2, layers, lambda: stage_3(M, old))

    @pl.when(step == layers)
    def _():
        small_pair().wait()
        for ahead in range(1, nf):
            peer = lax.rem(f + ahead, nf)
            s_send[ahead - 1] = s_grads[peer, core] + s_pair[peer]
            small_x(ahead).start()
        shared(c_got.at[c], c_got, c_sems, "ctx", nc)
        dcols_ref[f] = slot_sum(c_got, nc)
        share(dcols_ref.at[f], dcols_ref, f_sems, "fsdp", nf)

    def stacked_input(ref, first):
        normed, _ = norm_parts(ref[0])
        parts = [
            normed[g] * (1.0 + mod(first + 1, g, layer)) + mod(first, g, layer) for g in range(count)
        ]
        return jnp.concatenate(parts, 0).astype(LOW)

    def mlp_grads():
        w_in = stacked_input(keep_mid, 3)
        for k in range(4):
            keep_grad(HIDDEN + k, dot_tn(w_in, dpre_ref[k].reshape(count * rows, local)))
        pair_copy(H, new).start()
        branch = both(branch_ref)
        for k in range(4):
            keep_grad(MLP + k, dot_tn(branch, act_ref[k].reshape(count * rows, local)))
        pair_copy(M, new).start()
        for g in range(count):
            total_w(g).share()
        stage_2(H, new)
        stage_2(M, new)

    when(0, layers - 1, mlp_grads)
    when(1, layers, lambda: (pl.when(step >= 2)(lambda: end_wait(H, new, layer + 2)), stage_4(H, old, layer + 1))[1])

    def attention_back(g):
        normed, inv = norm_parts(keep_mid[0, g])
        d_mid, d_shift, d_scale = norm_back(total_w(g).get().astype(f32), normed, inv, mod(4, g, layer))
        d_mid = d_mid + dh_ref[g]
        dmid_ref[g] = d_mid
        put_dmod(3, g, layer, d_shift)
        put_dmod(4, g, layer, d_scale)
        put_dmod(2, g, layer, jnp.sum(d_mid * keep_a[0, g].astype(f32), 0, keepdims=True))
        branch = (mod(2, g, layer) * d_mid).astype(LOW)
        dba_ref[g] = branch
        grad = spread(dot(branch, matrix(OUT)).astype(LOW), heads)
        query = spread(keep_q[0, g], heads)
        keys = keep_kv[0, g, :, :, :local].reshape(nc * rows, local)
        values = keep_kv[0, g, :, :, local:].reshape(nc * rows, local)
        probs = keep_p[0, g]
        d_probs = dot_nt(grad, values)
        d_scores = (probs * (d_probs - jnp.sum(d_probs * probs, -1, keepdims=True))).astype(LOW)
        d_values = dot_tn(probs.astype(LOW), grad)
        d_keys = dot_tn(d_scores, query) * scale
        kv_send[g, :, :, :local] = d_keys.astype(LOW).reshape(nc, rows, local)
        kv_send[g, :, :, local:] = d_values.astype(LOW).reshape(nc, rows, local)
        for ahead in range(1, nc):
            kv_copy(g, ahead).start()
        d_query = pick(dot(d_scores, keys), heads) * scale
        dqkv_ref[0, g] = d_query.astype(LOW)

    def kv_copy(g, ahead):
        peer = lax.rem(c + ahead, nc)
        return remote(kv_send.at[g, peer], kv_got.at[new, g, ahead - 1], kv_sems, (new, g, ahead - 1), ctx=peer)

    @pl.when(step < layers)
    def _():
        for g in range(count):
            attention_back(g)

    when(1, layers, lambda: stage_3(A, old))
    when(0, 0, lambda: stage_3(H, new))

    @pl.when(step < layers)
    def _():
        for g in range(count):
            total = kv_send[g, c].astype(f32)
            for ahead in range(1, nc):
                kv_copy(g, ahead).wait()
                total = total + kv_got[new, g, ahead - 1].astype(f32)
            dqkv_ref[1, g] = total[:, :local].astype(LOW)
            dqkv_ref[2, g] = total[:, local:].astype(LOW)
            part = dot_nt(dqkv_ref[0, g], matrix(QUERY))
            part = part + dot_nt(dqkv_ref[1, g], matrix(KEY))
            part = part + dot_nt(dqkv_ref[2, g], matrix(VALUE))
            total_u(g).scatter(part)
        h_ref[...] = keep_h[0]
        u_in = stacked_input(keep_h, 0)
        for k in range(3):
            keep_grad(QUERY + k, dot_tn(u_in, dqkv_ref[k].reshape(count * rows, local)))
        keep_grad(OUT, dot_tn(both(dba_ref), keep_att[0].reshape(count * rows, local)))
        pair_copy(A, new).start()
        for g in range(count):
            total_u(g).share()

    when(1, layers - 1, lambda: stage_3(H, new))
    when(0, 0, lambda: stage_3(M, new))

    images_row = max(8, images)

    def own_gram(ref):
        return dot_nt(ref[...], ref[...])

    @pl.when(step == layers)
    def _():
        shared(dcols_ref.at[f], dcols_ref, f_sems, "fsdp", nf)
        product[...] = jnp.zeros_like(product)
        gram[...] = jnp.zeros_like(gram)
        index = lax.broadcasted_iota(jnp.int32, (LANES, chunk), 0)

        def multiply(j, carry):
            @pl.when(j + 1 < columns // chunk)
            def _():
                cond_copy(j + 1).start()

            pair = jnp.zeros((LANES, chunk), f32)
            for n in range(images):
                source = dcols_ref[
                    n // count, n % count : n % count + 1, pl.ds(pl.multiple_of(j * chunk, LANES), chunk)
                ]
                high, low = halves(source)
                pair = jnp.where(index == n, high, pair)
                pair = jnp.where(index == images + n, low, pair)
            pair = pair.astype(LOW)
            dcols_out[:, pl.ds(pl.multiple_of(j * chunk, LANES), chunk)] = pair[: dcols_out.shape[0]]
            gram[...] += dot_nt(pair, pair)
            cond_copy(j).wait()
            product[...] += dot_nt(cond_buf[lax.rem(j, 2)].astype(LOW), pair)
            return carry

        lax.fori_loop(0, columns // chunk, multiply, 0)
        total = product[...]
        total = jnp.transpose(total + pltpu.roll(total, LANES - images, 1))[:images_row]
        silu_got[t] = total
        share(silu_got.at[t], silu_got, t_sems, "tp", nt)
        for ahead in range(1, nf):
            small_x(ahead).wait()
        total = s_grads[f, core] + s_pair[f]
        for ahead in range(1, nf):
            total = total + s_x[ahead - 1]
        s_y_send[...] = total
        for ahead in range(1, chips):
            small_y(ahead).start()
        shared(silu_got.at[t], silu_got, t_sems, "tp", nt)
        d_cvec = slot_sum(silu_got, nt) * slope_c_ref[...]
        high, low = halves(d_cvec)
        pair = jnp.concatenate([high, low], 0).astype(LOW)
        dcvec_ref[...] = pair
        fixed = own_gram(swish_ref) + own_gram(onehot_ref)
        time_label = jnp.sum(dot_nt(pair, pair) * fixed)
        total = dot(pair, time_ref[...].astype(LOW))
        swish_got[f] = total[:images_row] + total[images_row:]
        share(swish_got.at[f], swish_got, a_sems, "fsdp", nf)
        shared(swish_got.at[f], swish_got, a_sems, "fsdp", nf)
        d_act = slot_sum(swish_got, nf) * slope_a_ref[...]
        high, low = halves(d_act)
        pair = jnp.concatenate([high, low], 0).astype(LOW)
        dact_ref[...] = pair
        freq = jnp.sum(dot_nt(pair, pair) * own_gram(freqs_ref))
        size = cond_in_ref.shape[0]
        cond = jnp.sum(gram[:size, :size] * own_gram(cond_in_ref))
        stat_ref[...] = jnp.full(
            stat_ref.shape, cond / nc + time_label / (nt * nc) + freq / (nf * nt * nc), f32
        )

    when(1, layers, lambda: (pl.when(step >= 2)(lambda: end_wait(M, new, layer + 2)), stage_4(M, old, layer + 1))[1])

    @pl.when(step == layers)
    def _():
        end_wait(A, new, 1)
        stage_4(A, old, 0)
        total = s_y_send[...]
        for ahead in range(1, chips):
            small_y(ahead).wait()
            total = total + s_y[ahead - 1]
        s_done[...] = total
        own = pltpu.make_async_copy(s_done, small_ref.at[core], s_own_sems.at[0])
        own.start()
        small_end(core).start()
        part = jnp.sum(square[...]) / chips + jnp.sum(total * total) / (nt * chips)
        index = lax.broadcasted_iota(jnp.int32, stat_ref.shape, 0)
        stat_ref[...] = jnp.where(index < 8, stat_ref[...] + part, jnp.sum(loss_ref[...]) / nt)
        for k, (axis, size) in enumerate((("ctx", nc), ("fsdp", nf), ("tp", nt))):
            me = lax.axis_index(axis)
            slots = stat_got.at[k]
            slots[me] = stat_ref[...]
            share(slots.at[me], slots, n_sems, axis, size, (k,))
            shared(slots.at[me], slots, n_sems, axis, size, (k,))
            stat_ref[...] = slot_sum(slots, size)
        for k in range(3):
            end_wait(k, old, 0)
        own.wait()
        small_end(core).wait_send()
        small_end(1 - core).wait_recv()


def backward(mesh, images, dh0, mods, dmods_end, loss, noisy, dpred, final_in, slopes, rights, time, cond, full, saved):
    sizes = dict(mesh.shape)
    nf, nc, nt = sizes["fsdp"], sizes["ctx"], sizes["tp"]
    chips = nc // 2
    others, overs = max(nf - 1, 1), max(chips - 1, 1)
    count, rows, width = dh0.shape
    layers, blocks, _, local = full.shape
    shard, columns = cond.shape
    half = shard // 2
    tokens = count * rows
    padded = max(8, images)
    f32 = jnp.float32

    def per_layer(array):
        shape = array.shape[1:]
        return pl.BlockSpec(
            (1, *shape), lambda i: (jnp.maximum(layers - 1 - i, 0),) + (0,) * len(shape)
        )

    anywhere = pl.BlockSpec(memory_space=pl.ANY)
    vmem = pl.BlockSpec(memory_space=pltpu.VMEM)
    whole = pltpu.VMEM((count, nt, rows // nt, width), LOW)
    first = pltpu.VMEM((count, nt - 1, rows // nt, width), LOW)
    image = pltpu.VMEM((count, rows, width), f32)
    image_low = pltpu.VMEM((count, rows, width), LOW)
    mlp = pltpu.VMEM((4, count, rows, local), LOW)
    small = (half, LANES)
    dma = pltpu.SemaphoreType.DMA
    return pl.pallas_call(
        functools.partial(backward_kernel, sizes, images),
        grid=(layers + 1,),
        out_shape=[
            jax.ShapeDtypeStruct((layers, blocks, 2, half, local), LOW),
            jax.ShapeDtypeStruct((2, half, LANES), f32),
            jax.ShapeDtypeStruct((-(-2 * images // 16) * 16, columns), LOW),
            jax.ShapeDtypeStruct((2 * padded, shard), LOW),
            jax.ShapeDtypeStruct((2 * padded, width), LOW),
            jax.ShapeDtypeStruct((16, LANES), f32),
        ],
        in_specs=[vmem] * 14 + [anywhere, per_layer(full), *(per_layer(s) for s in saved)],
        out_specs=[anywhere, anywhere, vmem, vmem, vmem, vmem],
        scratch_shapes=[
            image, image, image, mlp, mlp, image_low, image_low,
            pltpu.VMEM((3, count, rows, local), LOW),
            pltpu.VMEM(mods.shape, f32),
            whole, first, whole, whole, first, whole,
            pltpu.VMEM((count, nc, rows, 2 * local), LOW),
            pltpu.VMEM((2, count, nc - 1, rows, 2 * local), LOW),
            pltpu.VMEM((blocks, nf, 2, half, local), LOW),
            pltpu.VMEM((2, blocks, nf, half, local), LOW),
            pltpu.VMEM((others, blocks, half, local), LOW),
            pltpu.VMEM((2, others, blocks, half, local), LOW),
            pltpu.VMEM((blocks, half, local), LOW),
            pltpu.VMEM((2, overs, blocks, half, local), LOW),
            pltpu.VMEM((blocks, half, local), LOW),
            pltpu.VMEM((8, local), f32),
            pltpu.VMEM((nf, 2, *small), f32),
            pltpu.VMEM((nf, *small), f32),
            pltpu.VMEM((others, *small), f32),
            pltpu.VMEM((others, *small), f32),
            pltpu.VMEM(small, f32),
            pltpu.VMEM((overs, *small), f32),
            pltpu.VMEM(small, f32),
            pltpu.VMEM((nc, count, columns), f32),
            pltpu.VMEM((nf, count, columns), f32),
            pltpu.VMEM((2, shard, 512), f32),
            pltpu.VMEM((shard, LANES), f32),
            pltpu.VMEM((LANES, LANES), f32),
            pltpu.VMEM((nt, padded, shard), f32),
            pltpu.VMEM((nf, padded, width), f32),
            pltpu.VMEM((3, max(sizes.values()), 16, LANES), f32),
            dma((2, 2, count, nt - 1)),
            dma((2, 2, count, nt - 1)),
            dma((2, 2, count, nc - 1)),
            dma((2, 2, 3)),
            dma((2, 2, 3, others)),
            dma((2, 2, 3, overs)),
            dma((2, 2, 3)),
            dma((3,)),
            dma((2, 2)),
            dma((2, others)),
            dma((2, overs)),
            dma((1,)),
            dma((2, nc - 1)),
            dma((2, others)),
            dma((2,)),
            dma((2, nt - 1)),
            dma((2, others)),
            dma((2, 3, max(sizes.values()))),
        ],
        compiler_params=pltpu.CompilerParams(
            collective_id=2, has_side_effects=True, vmem_limit_bytes=60 * 2**20
        ),
        cost_estimate=pl.CostEstimate(
            flops=4 * tokens * width * blocks * local * layers,
            bytes_accessed=layers * blocks * width * local * 4,
            transcendentals=0,
        ),
        name="backward_layers",
    )(dh0, mods, dmods_end, loss, noisy, dpred, final_in, *slopes, *rights, time, cond, full, *saved)


FIX = math.sqrt(1.0 / (1.0 - BETA**STEP))


def update_block(weight, mean, square, grad, outs, where):
    mean_next = BETA * mean[where] + grad
    square_next = BETA * square[where] + (grad * grad) * (1.0 / (1.0 - BETA))
    moved = mean_next / (jnp.sqrt(square_next) + EPSILON / FIX)
    outs[0][where] = weight[where] * (1.0 - RATE * DECAY) - (RATE * FIX) * moved
    outs[1][where] = mean_next
    outs[2][where] = square_next


def mixed(a):
    layers, rows, blocks, columns = a.shape
    a = a.reshape(layers, rows, blocks, columns // LANES, LANES)
    return jnp.swapaxes(a, 2, 3).reshape(layers, -1, LANES)


def update_kernel(
    plan, clip_ref, grads_ref, small_ref, cond_left, cond_right, time_left, time_right, freq_left, freq_right,
    label_left, label_right, *refs,
):
    clip = clip_ref[0, 0] * (1.0 - BETA)
    step = pl.program_id(0) * pl.num_programs(1) + pl.program_id(1)
    names = ("attend", "hidden", "output", "cond", "time", "freq", "label", "patch", "head")
    trios = {name: refs[3 * k : 3 * k + 3] for k, name in enumerate(names)}
    outs = {name: refs[27 + 3 * k : 30 + 3 * k] for k, name in enumerate(names)}

    def change(name, grad, where):
        update_block(*trios[name], grad * clip, outs[name], where)

    for name, first in (("attend", QUERY), ("output", OUT)):
        _, blocks, rows, _ = trios[name][0].shape
        piece = min(64, rows)
        for b in range(blocks):
            for r in range(0, rows, piece):
                grad = grads_ref[0, first + b, r : r + piece].astype(jnp.float32)
                change(name, grad, (0, b, pl.ds(r, piece)))

    _, _, rows, columns = grads_ref.shape
    tiles = columns // LANES
    size = 4 * tiles * 16
    order = interleave(4, tiles)
    for r in range(rows // 16):
        parts = [
            grads_ref[0, HIDDEN + k, 16 * r : 16 * r + 16, n * LANES : (n + 1) * LANES]
            for k in range(4)
            for n in range(tiles)
        ]
        change("hidden", dot(order, jnp.concatenate(parts, 0)), (0, pl.ds(r * size, size)))

    def outer(name, left, right):
        first, count = plan[name]

        @pl.when((step >= first) & (step < first + count))
        def _():
            rows = trios[name][0].shape[0]
            for r in range(0, rows, 64):
                high = min(r + 64, rows)
                change(name, dot_tn(left[:, r:high], right[...]), (pl.ds(r, high - r),))

    outer("cond", cond_left, cond_right)
    outer("time", time_left, time_right)
    outer("freq", freq_left, freq_right)
    outer("label", label_left, label_right)

    @pl.when(step == 0)
    def _():
        small = jnp.transpose(small_ref[...])
        at = 0
        for name in ("patch", "head"):
            rows = trios[name][0].shape[0]
            change(name, small[at : at + rows], (pl.ds(0, rows),))
            at += rows


def update(clip, grads, small, factors, trios):
    attend, hidden, output, patch, freq, time, label, cond, head = trios
    layers, _, rows, local = grads.shape
    parts = 4
    steps = layers * parts
    inner = rows // parts

    def turned(trio):
        return [jnp.swapaxes(a, -1, -2) for a in trio]

    def outward(trio):
        return [jnp.swapaxes(a, 1, 2) for a in trio]

    arrays = {
        "attend": outward(attend),
        "hidden": [mixed(a) for a in hidden],
        "output": outward(output),
        "cond": list(cond),
        "time": list(time),
        "freq": list(freq),
        "label": turned(label),
        "patch": turned(patch),
        "head": turned(head),
    }
    chunks = {"cond": 512, "time": LANES, "freq": LANES, "label": min(LANES, rows)}
    plan, specs = {}, {}
    for name, width in chunks.items():
        count = arrays[name][0].shape[1] // width
        plan[name] = (0 if name == "cond" else steps - count, count)

    def at(name):
        first, count = plan[name]
        return lambda i, j: (0, jnp.clip(i * parts + j - first, 0, count - 1))

    for name, (array, *_) in arrays.items():
        if name in chunks:
            specs[name] = pl.BlockSpec((array.shape[0], chunks[name]), at(name))
        elif name == "hidden":
            specs[name] = pl.BlockSpec((1, array.shape[1] // parts, LANES), lambda i, j: (i, j, 0))
        elif array.ndim == 4:
            specs[name] = pl.BlockSpec((1, array.shape[1], inner, local), lambda i, j: (i, 0, j, 0))
        else:
            specs[name] = pl.BlockSpec(array.shape, lambda i, j: (0, 0))
    factor_specs = []
    for name in ("cond", "time", "freq", "label"):
        left, right = factors[name]
        factor_specs.append(pl.BlockSpec(left.shape, lambda i, j: (0, 0)))
        factor_specs.append(pl.BlockSpec((right.shape[0], chunks[name]), at(name)))
    whole = [specs[name] for name in arrays for _ in range(3)]
    flat = [a for name in arrays for a in arrays[name]]
    size = sum(a.size for a in flat) // 3
    outs = pl.pallas_call(
        functools.partial(update_kernel, plan),
        grid=(layers, parts),
        out_shape=[jax.ShapeDtypeStruct(a.shape, jnp.float32) for a in flat],
        in_specs=[
            pl.BlockSpec(memory_space=pltpu.SMEM),
            pl.BlockSpec((1, grads.shape[1], inner, local), lambda i, j: (i, 0, j, 0)),
            pl.BlockSpec(small.shape, lambda i, j: (0, 0)),
            *factor_specs,
            *whole,
        ],
        out_specs=whole,
        compiler_params=pltpu.CompilerParams(vmem_limit_bytes=60 * 2**20),
        cost_estimate=pl.CostEstimate(flops=20 * size, bytes_accessed=26 * size, transcendentals=2 * size),
        name="update",
    )(clip, grads, small, *(f for name in ("cond", "time", "freq", "label") for f in factors[name]), *flat)
    made = {name: outs[3 * k : 3 * k + 3] for k, name in enumerate(arrays)}
    blocks = hidden[0].shape[2]

    def back(a):
        a = a.reshape(layers, rows, local // LANES, blocks, LANES)
        return jnp.swapaxes(a, 2, 3).reshape(layers, rows, blocks, local)

    return [
        *outward(made["attend"]),
        *(back(a) for a in made["hidden"]),
        *outward(made["output"]),
        *turned(made["patch"]),
        *made["freq"],
        *made["time"],
        *turned(made["label"]),
        *made["cond"],
        *turned(made["head"]),
    ]


def per_device(
    mesh,
    latents,
    noise,
    var_target,
    timesteps,
    labels,
    attend_weight,
    attend_mean,
    attend_square,
    hidden_weight,
    hidden_mean,
    hidden_square,
    output_weight,
    output_mean,
    output_square,
    patch_weight,
    patch_mean,
    patch_square,
    freq_weight,
    freq_mean,
    freq_square,
    time_weight,
    time_mean,
    time_square,
    label_table,
    label_mean,
    label_square,
    cond_weight,
    cond_mean,
    cond_square,
    head_weight,
    head_mean,
    head_square,
):
    count, rows, patch_in = latents.shape
    layers, shard = attend_weight.shape[:2]
    columns = cond_weight.shape[1]

    own = jnp.pad(jnp.stack([timesteps, labels]).astype(jnp.float32), ((0, 6), (0, LANES - count)))
    drawn = lax.all_gather(own, "fsdp", axis=0)[:, :2, :count]
    steps_all, labels_all = (drawn[:, k].reshape(-1).astype(jnp.int32) for k in range(2))
    freqs = time_freqs(steps_all).astype(LOW)
    act = jnp.dot(freqs, freq_weight.astype(LOW).T, preferred_element_type=jnp.float32)
    act = lax.all_gather(act, "fsdp", axis=1, tiled=True)
    swish = jax.nn.silu(act).astype(LOW)
    time_low = time_weight.astype(LOW)
    temb = jnp.dot(swish, time_low.T, preferred_element_type=jnp.float32)
    onehot = (labels_all[:, None] == jnp.arange(label_table.shape[1], dtype=jnp.int32)[None]).astype(
        LOW
    )
    cvec = temb + jnp.dot(onehot, label_table.astype(LOW).T, preferred_element_type=jnp.float32)
    cond_in = jax.nn.silu(cvec).astype(LOW)
    level = noise_level(timesteps)[:, None, None]
    noisy = (jnp.sqrt(level) * latents + jnp.sqrt(1.0 - level) * noise).astype(LOW)
    images = freqs.shape[0]
    width = time_weight.shape[1]
    patch_out = head_weight.shape[1]
    after = LANES - patch_in - patch_out

    def twice(value, each):
        value = jnp.pad(value.astype(LOW), ((0, each - images), (0, 0)))
        return jnp.pad(jnp.concatenate([value, value]), ((0, -2 * each % 16), (0, 0)))

    cond_parts = twice(cond_in, images)
    noisy_wide = jnp.pad(noisy, ((0, 0), (0, 0), (0, LANES - patch_in)))
    d_h, flat_mods, d_mods_end, loss_part, d_pred, final_in, full, *saved = forward(
        mesh,
        images,
        (patch_in, patch_out),
        cond_parts,
        cond_weight,
        patch_weight.T,
        head_weight.T,
        noisy_wide,
        positions(lax.axis_index("ctx") * rows, rows, width),
        jnp.pad(jnp.concatenate([noise, var_target], 2), ((0, 0), (0, 0), (patch_in, after))),
        mixed(hidden_weight),
        jnp.swapaxes(attend_weight, 1, 2),
        jnp.swapaxes(output_weight, 1, 2),
    )
    blocks = full.shape[1]
    full = full.reshape(layers, blocks, width, -1)
    padded = max(8, images) - images
    tokens = count * rows

    def slope(value):
        _, back = jax.vjp(jax.nn.silu, value)
        return jnp.pad(back(jnp.ones_like(value))[0], ((0, padded), (0, 0)))

    each = max(8, images)
    swish_parts, onehot_parts, freq_parts = (twice(v, each) for v in (swish, onehot, freqs))
    grads, d_small, d_cols, d_cvec, d_act, stat = backward(
        mesh,
        images,
        d_h,
        flat_mods,
        d_mods_end,
        loss_part,
        noisy_wide.reshape(tokens, -1),
        d_pred.reshape(tokens, -1),
        final_in.reshape(tokens, -1),
        (slope(cvec), slope(act)),
        (cond_parts, swish_parts, onehot_parts, freq_parts),
        time_weight,
        cond_weight,
        full,
        saved,
    )
    grads = grads.reshape(layers, blocks, shard, -1)
    d_small = d_small.reshape(shard, -1)
    d_act = lax.dynamic_slice_in_dim(d_act, lax.axis_index("fsdp") * shard, shard, 1)
    total_sq, loss = stat[0, 0], stat[8, 0]
    grad_norm = jnp.sqrt(total_sq)
    clip = jnp.minimum(1.0, CLIP / (grad_norm + 1e-06))
    factor = clip.reshape(1, 1)
    updated = update(
        factor,
        grads,
        d_small,
        {
            "cond": (cond_parts, d_cols),
            "time": (d_cvec, swish_parts),
            "freq": (d_act, freq_parts),
            "label": (onehot_parts, d_cvec),
        },
        (
            (attend_weight, attend_mean, attend_square),
            (hidden_weight, hidden_mean, hidden_square),
            (output_weight, output_mean, output_square),
            (patch_weight, patch_mean, patch_square),
            (freq_weight, freq_mean, freq_square),
            (time_weight, time_mean, time_square),
            (label_table, label_mean, label_square),
            (cond_weight, cond_mean, cond_square),
            (head_weight, head_mean, head_square),
        ),
    )
    return (loss, grad_norm, *updated)


def solution(mesh):
    image = P("fsdp", "ctx", None)
    layer = P(None, "fsdp", None, "tp")
    rows = P("fsdp", None)
    cond = P("fsdp", "tp")
    weights = (layer,) * 9 + (rows,) * 12 + (cond,) * 3 + (rows,) * 3
    return jax.shard_map(
        functools.partial(per_device, mesh),
        mesh=mesh,
        in_specs=(image, image, image, P("fsdp"), P("fsdp")) + weights,
        out_specs=(P(), P()) + weights,
        check_vma=False,
    )
```
